32 devices in a mesh: section: 2 (over core), dp: 4 (over y, x), ctx: 4 (over z).
Axes of the slice: x: 2, y: 2, z: 4, core: 2. Of those that a mesh axis runs over, the one named last changes fastest.
Arguments:
- tokens: bfloat16 [16, 512, 768], P('dp', 'ctx'), may hold values from -6 to 6
- segment_ids: int32 [16, 512], P('dp', 'ctx'), may hold values from 0 to 4, as said below
- padding: int32 [16, 512], P('dp', 'ctx'), may hold values from 0 to 1, as said below
- dropped: int32 [2, 16], P('section', 'dp'), may hold values 0 or 1
- qkv_weight: bfloat16 [2, 768, 2304], P('section'), may hold values from -0.21875 to 0.21875
- query_bias: float32 [2, 768], P('section'), may hold values from -1.75 to 1.75
- value_bias: float32 [2, 768], P('section'), may hold values from -0.0625 to 0.0625
- attn_weight: bfloat16 [2, 768, 768], P('section'), may hold values from -3.5 to 3.5
- attn_bias: float32 [2, 768], P('section'), may hold values from -1.25 to 1.25
- attn_gain: float32 [2, 768], P('section'), may hold values from 0.5 to 1.5
- attn_shift: float32 [2, 768], P('section'), may hold values from -1.25 to 1.25
- inner_weight: bfloat16 [2, 768, 3072], P('section'), may hold values from -0.21875 to 0.21875
- inner_bias: float32 [2, 3072], P('section'), may hold values from -1.75 to 1.75
- outer_weight: bfloat16 [2, 3072, 768], P('section'), may hold values from -0.109375 to 0.109375
- outer_bias: float32 [2, 768], P('section'), may hold values from -1.25 to 1.25
- ffn_gain: float32 [2, 768], P('section'), may hold values from 0.5 to 1.5
- ffn_shift: float32 [2, 768], P('section'), may hold values from -1.25 to 1.25
- cotangent: bfloat16 [16, 512, 768], P('dp', 'ctx'), may hold values from -6 to 6
Outputs:
- encoded: bfloat16 [16, 512, 768], P('dp', 'ctx', 'section')
- tokens_grad: bfloat16 [16, 512, 768], P('dp', 'ctx', 'section')
- grad_qkv_weight: float32 [2, 768, 2304], P('section', 'dp', 'ctx')
- grad_query_bias: float32 [2, 768], P('section')
- grad_value_bias: float32 [2, 768], P('section')
- grad_attn_weight: float32 [2, 768, 768], P('section', 'dp', 'ctx')
- grad_attn_bias: float32 [2, 768], P('section')
- grad_attn_gain: float32 [2, 768], P('section')
- grad_attn_shift: float32 [2, 768], P('section')
- grad_inner_weight: float32 [2, 768, 3072], P('section', 'dp', 'ctx')
- grad_inner_bias: float32 [2, 3072], P('section')
- grad_outer_weight: float32 [2, 3072, 768], P('section', 'dp', 'ctx')
- grad_outer_bias: float32 [2, 768], P('section')
- grad_ffn_gain: float32 [2, 768], P('section')
- grad_ffn_shift: float32 [2, 768], P('section')
The draws below stay inside these ranges and needn't reach their ends.
Inputs may be any that keep to these rules, and one draw needn't show every extreme that they name: `segment_ids`: ids never fall along a row; every row holds exactly the documents 0 to 4. `padding`: 1 on a prefix of each row, 0 on the rest; every row has padded positions, all inside document 4, which keeps at least one real token.
All inputs are finite; a program needn't handle non-finite values. No bound on the sum of `dropped` on one device may be relied on, other than what follows from the above.
Results may differ from the reference program's by a relative error of at most 0.034.
Values may be sent and summed in bfloat16 or wider, within the bound.
No kernel may reach another device: no remote copies, remote signals or barrier semaphores. Data moves between devices by JAX's collectives and lax.ppermute only.
A program may use at most 256 MiB of HBM per device.

```python
import jax
import jax.numpy as jnp
from jax import lax

D = 768
HEADS = 12
HEAD_DIM = 64
FF = 3072
TOK_CTX = 128
ROWS = 16
SEQ = 512
N_SECTION = 2


def row_bounds(key):
    subkeys = jax.random.split(key, 5)
    begin_long = jax.random.randint(subkeys[0], (ROWS,), 2, TOK_CTX // 2)
    first_cut = jax.random.randint(subkeys[1], (ROWS,), 1, begin_long)
    end_long = SEQ - TOK_CTX + jax.random.randint(subkeys[2], (ROWS,), 0, TOK_CTX // 4)
    last_cut = end_long + 1 + jax.random.randint(subkeys[3], (ROWS,), 0, TOK_CTX // 4)
    pad_from = last_cut + 1 + jax.random.randint(subkeys[4], (ROWS,), 0, SEQ - last_cut - 1)
    return (first_cut, begin_long, end_long, last_cut, pad_from)


def draw_segment_ids(key, part):
    bounds = row_bounds(key)
    positions = jnp.arange(SEQ, dtype=jnp.int32)[None, :]
    doc_ids = jnp.zeros((ROWS, SEQ), jnp.int32)
    for bound in bounds[:4]:
        doc_ids = doc_ids + (positions >= bound[:, None]).astype(jnp.int32)
    return doc_ids


def draw_padding(key, part):
    bounds = row_bounds(key)
    positions = jnp.arange(SEQ, dtype=jnp.int32)[None, :]
    return (positions < bounds[4][:, None]).astype(jnp.int32)


def set_ends(drawn, key, smallest, top_value):
    place = [jax.random.randint(jax.random.fold_in(key, axis), (), 0, length) for axis, length in enumerate(drawn.shape)]
    longest = drawn.shape.index(max(drawn.shape))
    next_to = place[:longest] + [(place[longest] + 1) % drawn.shape[longest]] + place[longest + 1:]
    return drawn.at[tuple(place)].set(smallest).at[tuple(next_to)].set(top_value)


def levels(key, extent, shards, low, top_value):
    loudness = 1.0
    for axis_at, blocks in shards:
        draws = jax.random.uniform(jax.random.fold_in(jax.random.fold_in(key, 6), axis_at), (blocks,), jnp.float32, low / len(shards), top_value / len(shards))
        loudness = loudness * jnp.repeat(jnp.exp(draws), extent[axis_at] // blocks).reshape((-1,) + (1,) * (len(extent) - 1 - axis_at))
    return loudness


def scatter_about(key, dims, scale, most, shards=(), kind=jnp.bfloat16):
    values = jax.random.normal(key, dims, jnp.float32) * scale
    if len(shards) > 0:
        values = levels(key, dims, shards, -0.22, 0.18) * values
    return jnp.clip(values, min=-most, max=most).astype(kind)


def setup_inputs(seed: int = 0) -> dict:
    keys = jax.random.split(jax.random.key(seed), 19)
    return {
        "tokens": scatter_about(keys[0], (ROWS, SEQ, D), 1.0, 6.0, ((0, 4), (1, 4))),
        "segment_ids": draw_segment_ids(jax.random.fold_in(keys[18], 71), 0),
        "padding": draw_padding(jax.random.fold_in(keys[18], 71), 0),
        "dropped": set_ends((jax.random.randint(keys[3], (N_SECTION, ROWS), 0, 3) < 1).astype(jnp.int32), jax.random.fold_in(keys[3], 1), 0, 1),
        "qkv_weight": scatter_about(keys[4], (N_SECTION, D, 3 * D), D ** -0.5, 0.21875, ((0, 2),)),
        "query_bias": scatter_about(keys[5], (N_SECTION, D), 0.3, 1.75, ((0, 2),), jnp.float32),
        "value_bias": scatter_about(keys[6], (N_SECTION, D), 0.01, 0.0625, ((0, 2),), jnp.float32),
        "attn_weight": scatter_about(keys[7], (N_SECTION, D, D), (max(1, 2 * D // SEQ)) ** -0.5, 3.5, ((0, 2),)),
        "attn_bias": scatter_about(keys[8], (N_SECTION, D), 0.2, 1.25, ((0, 2),), jnp.float32),
        "attn_gain": jnp.clip(1.0 + 0.1 * jax.random.normal(keys[9], (N_SECTION, D), jnp.float32), 0.5, 1.5),
        "attn_shift": scatter_about(keys[10], (N_SECTION, D), 0.2, 1.25, ((0, 2),), jnp.float32),
        "inner_weight": scatter_about(keys[11], (N_SECTION, D, FF), D ** -0.5, 0.21875, ((0, 2),)),
        "inner_bias": scatter_about(keys[12], (N_SECTION, FF), 0.3, 1.75, ((0, 2),), jnp.float32),
        "outer_weight": scatter_about(keys[13], (N_SECTION, FF, D), FF ** -0.5, 0.109375, ((0, 2),)),
        "outer_bias": scatter_about(keys[14], (N_SECTION, D), 0.2, 1.25, ((0, 2),), jnp.float32),
        "ffn_gain": jnp.clip(1.0 + 0.1 * jax.random.normal(keys[15], (N_SECTION, D), jnp.float32), 0.5, 1.5),
        "ffn_shift": scatter_about(keys[16], (N_SECTION, D), 0.2, 1.25, ((0, 2),), jnp.float32),
        "cotangent": scatter_about(keys[17], (ROWS, SEQ, D), 1.0, 6.0, ((0, 4), (1, 4))),
    }


@jax.custom_vjp
def low(v):
    return lax.optimization_barrier(v.astype(jnp.bfloat16)).astype(jnp.float32)

@jax.custom_vjp
def low_back(v):
    return v

def low_keep(v):
    return (low(v), None)

def low_pass(kept, grad):
    return (grad,)

def back_keep(v):
    return (v, None)

def back_low(kept, grad):
    return (low(grad),)
low.defvjp(low_keep, low_pass)
low_back.defvjp(back_keep, back_low)
highest = lax.Precision.HIGHEST
norm_eps = 1e-05

def matmul(left, right):
    return jnp.dot(left, right, precision=highest, preferred_element_type=jnp.float32)

def layer_norm(values, gain, shift):
    mean_value = lax.optimization_barrier(jnp.mean(values, axis=-1, keepdims=True))
    centered = values - mean_value
    variance = lax.optimization_barrier(jnp.mean(centered * centered, axis=-1, keepdims=True))
    return centered * lax.rsqrt(variance + norm_eps) * gain + shift

def encoder_layer(layer_input, params, allowed, drop_flag):
    qkv_weight, query_bias, value_bias, attn_weight, attn_bias, attn_gain, attn_shift, inner_weight, inner_bias, outer_weight, outer_bias, ffn_gain, ffn_shift = params
    projected = matmul(layer_input, qkv_weight)
    query_low = low_back(low(projected[:, :D] + query_bias))
    key_low = low_back(low(projected[:, D:2 * D]))
    value_low = low_back(low(projected[:, 2 * D:] + value_bias))
    query_heads = query_low.reshape(SEQ, HEADS, HEAD_DIM)
    key_heads = key_low.reshape(SEQ, HEADS, HEAD_DIM)
    value_heads = value_low.reshape(SEQ, HEADS, HEAD_DIM)
    scores = jnp.einsum('qhd,khd->hqk', query_heads, key_heads, precision=highest) * HEAD_DIM ** (-0.5)
    scores = low_back(scores)
    scores = jnp.where(allowed[None], scores, -1e+30)
    prob_rows = jax.nn.softmax(scores, axis=-1)
    attended = jnp.einsum('hqk,khd->qhd', low(prob_rows), value_heads, precision=highest).reshape(SEQ, D)
    attended = low_back(low(attended))
    branch = low_back(matmul(attended, attn_weight) + attn_bias)
    first_norm = layer_norm(layer_input + branch, attn_gain, attn_shift)
    inner_pre = low_back(matmul(low(first_norm), inner_weight) + inner_bias)
    active = low(jax.nn.gelu(inner_pre, approximate=False))
    ffn_out = low_back(matmul(active, outer_weight) + outer_bias)
    result = layer_norm(first_norm + ffn_out, ffn_gain, ffn_shift)
    return jnp.where(drop_flag > 0, layer_input, result)

def two_layers(row_input, params_zero, params_one, allowed, drop_pair):
    middle = encoder_layer(row_input, params_zero, allowed, drop_pair[0])
    middle = low_back(low(middle))
    return encoder_layer(middle, params_one, allowed, drop_pair[1])

def reference(tokens, segment_ids, padding, dropped, qkv_weight, query_bias, value_bias, attn_weight, attn_bias, attn_gain, attn_shift, inner_weight, inner_bias, outer_weight, outer_bias, ffn_gain, ffn_shift, cotangent):
    weights = tuple((member.astype(jnp.float32) for member in (qkv_weight, query_bias, value_bias, attn_weight, attn_bias, attn_gain, attn_shift, inner_weight, inner_bias, outer_weight, outer_bias, ffn_gain, ffn_shift)))
    params_zero = tuple((member[0] for member in weights))
    params_one = tuple((member[1] for member in weights))

    def per_row(totals, members):
        row_tokens, seg_row, pad_row, drop_pair, row_cot = members
        allowed = (seg_row[:, None] == seg_row[None, :]) & (pad_row[None, :] == 1)

        def forward(row_input, weights_zero, weights_one):
            return two_layers(row_input, weights_zero, weights_one, allowed, drop_pair)
        row_out, pull_back = jax.vjp(forward, row_tokens.astype(jnp.float32), params_zero, params_one)
        grad_row, grad_zero, grad_one = pull_back(row_cot.astype(jnp.float32))
        totals = jax.tree.map(lambda total, first_grad, second_grad: total + jnp.stack([first_grad, second_grad]), totals, grad_zero, grad_one)
        return (totals, (row_out.astype(jnp.bfloat16), grad_row.astype(jnp.bfloat16)))
    start_totals = tuple((jnp.zeros_like(member) for member in weights))
    totals, (encoded, tokens_grad) = lax.scan(per_row, start_totals, (tokens, segment_ids, padding, dropped.T, cotangent))
    return (encoded, tokens_grad, totals[0], totals[1], totals[2], totals[3], totals[4], totals[5], totals[6], totals[7], totals[8], totals[9], totals[10], totals[11], totals[12])
```

```python
from functools import partial

import jax
import jax.numpy as jnp
from jax import lax
from jax.experimental import pallas as pl
from jax.experimental.pallas import tpu as pltpu
from jax.sharding import PartitionSpec as P

HEADS = 12
HEAD_DIM = 64


norm_eps = 1e-05
masked_score = -1e30


def shifted(x, axis, by):
    length = lax.axis_size(axis)
    return lax.ppermute(x, axis, [(i, (i + by) % length) for i in range(length)])


def matmul_low(left, right):
    return jnp.dot(left, right, preferred_element_type=jnp.float32)


def left_product(left, right):
    return jnp.einsum("ti,to->io", left, right, preferred_element_type=jnp.float32)


def right_product(left, right):
    return jnp.einsum("to,io->ti", left, right, preferred_element_type=jnp.float32)


def normalize(values):
    mean_value = jnp.mean(values, axis=-1, keepdims=True)
    centered = values - mean_value
    variance = jnp.mean(centered * centered, axis=-1, keepdims=True)
    inverse = lax.rsqrt(variance + norm_eps)
    return (centered * inverse, inverse)


def norm_back(grad_out, normed, inverse, gain):
    scaled = grad_out * gain
    return inverse * (
        scaled
        - jnp.mean(scaled, axis=-1, keepdims=True)
        - normed * jnp.mean(scaled * normed, axis=-1, keepdims=True)
    )


def attend_piece(query_heads, seg_query, running, pieces):
    run_max, run_total, run_acc = running
    key_piece, value_piece, seg_piece, pad_piece = pieces
    count = key_piece.shape[0]
    key_heads = key_piece.reshape(count, HEADS, HEAD_DIM)
    value_heads = value_piece.reshape(count, HEADS, HEAD_DIM)
    scores = jnp.einsum(
        "qhd,khd->hqk", query_heads, key_heads, preferred_element_type=jnp.float32
    ) * HEAD_DIM ** (-0.5)
    allowed = (seg_query[:, None] == seg_piece[None, :]) & (pad_piece[None, :] == 1)
    scores = jnp.where(allowed[None], scores, masked_score)
    new_max = jnp.maximum(run_max, jnp.max(scores, axis=-1))
    weights = jnp.where(allowed[None], jnp.exp(scores - new_max[..., None]), 0.0)
    run_total = jnp.sum(weights, axis=-1)
    run_acc = jnp.einsum(
        "hqk,khd->hqd",
        weights.astype(jnp.bfloat16),
        value_heads,
        preferred_element_type=jnp.float32,
    )
    return (new_max, run_total, run_acc)


def attention_back(
    query_low, key_all, value_all, seg_query, seg_all, pad_all, log_total, row_delta, grad_att
):
    row_count = query_low.shape[0]
    seq_count = key_all.shape[0]
    score_scale = HEAD_DIM ** (-0.5)
    query_heads = query_low.reshape(row_count, HEADS, HEAD_DIM)
    key_heads = key_all.reshape(seq_count, HEADS, HEAD_DIM)
    value_heads = value_all.reshape(seq_count, HEADS, HEAD_DIM)
    grad_heads = grad_att.reshape(row_count, HEADS, HEAD_DIM)
    scores = (
        jnp.einsum("qhd,khd->hqk", query_heads, key_heads, preferred_element_type=jnp.float32)
        * score_scale
    )
    allowed = (seg_query[:, None] == seg_all[None, :]) & (pad_all[None, :] == 1)
    prob_rows = jnp.where(allowed[None], jnp.exp(scores - log_total[..., None]), 0.0)
    grad_probs = jnp.einsum(
        "qhd,khd->hqk", grad_heads, value_heads, preferred_element_type=jnp.float32
    )
    grad_scores = (prob_rows * (grad_probs - row_delta[..., None])).astype(jnp.bfloat16)
    grad_query = (
        jnp.einsum("hqk,khd->qhd", grad_scores, key_heads, preferred_element_type=jnp.float32)
        * score_scale
    )
    grad_key = (
        jnp.einsum("hqk,qhd->khd", grad_scores, query_heads, preferred_element_type=jnp.float32)
        * score_scale
    )
    grad_value = jnp.einsum(
        "hqk,qhd->khd",
        prob_rows.astype(jnp.bfloat16),
        grad_heads,
        preferred_element_type=jnp.float32,
    )
    model_width = HEADS * HEAD_DIM
    return (
        grad_query.reshape(row_count, model_width),
        grad_key.reshape(seq_count, model_width),
        grad_value.reshape(seq_count, model_width),
    )


def layer_forward(layer_input, params, seg_query, pad_query, drop_flag):
    (
        qkv_weight,
        query_bias,
        value_bias,
        attn_weight,
        attn_bias,
        attn_gain,
        attn_shift,
        inner_weight,
        inner_bias,
        outer_weight,
        outer_bias,
        ffn_gain,
        ffn_shift,
    ) = params
    model_width = layer_input.shape[1]
    row_count = layer_input.shape[0]
    projected = matmul_low(layer_input, qkv_weight)
    query_low = (projected[:, :model_width] + query_bias).astype(jnp.bfloat16)
    key_local = projected[:, model_width : 2 * model_width].astype(jnp.bfloat16)
    value_local = (projected[:, 2 * model_width :] + value_bias).astype(jnp.bfloat16)
    query_heads = query_low.reshape(row_count, HEADS, HEAD_DIM)
    start_state = (
        jnp.full((HEADS, row_count), masked_score, jnp.float32),
        jnp.zeros((HEADS, row_count), jnp.float32),
        jnp.zeros((HEADS, row_count, HEAD_DIM), jnp.float32),
    )
    key_all, value_all, seg_all, pad_all = (
        lax.all_gather(key_local, "ctx", axis=0, tiled=True),
        lax.all_gather(value_local, "ctx", axis=0, tiled=True),
        lax.all_gather(seg_query, "ctx", axis=0, tiled=True),
        lax.all_gather(pad_query, "ctx", axis=0, tiled=True),
    )
    run_max, run_total, run_acc = attend_piece(
        query_heads, seg_query, start_state, (key_all, value_all, seg_all, pad_all)
    )
    gathered = (key_all, value_all, seg_all, pad_all)
    attended = (run_acc / run_total[..., None]).transpose(1, 0, 2).reshape(row_count, model_width)
    log_total = run_max + jnp.log(run_total)
    branch = matmul_low(attended.astype(jnp.bfloat16), attn_weight) + attn_bias
    sum_attn = layer_input.astype(jnp.float32) + branch
    normed, inverse = normalize(sum_attn)
    first_norm = normed * attn_gain + attn_shift
    inner_pre = matmul_low(first_norm.astype(jnp.bfloat16), inner_weight) + inner_bias
    active_low = jax.nn.gelu(inner_pre, approximate=False).astype(jnp.bfloat16)
    sum_ffn = first_norm + matmul_low(active_low, outer_weight) + outer_bias
    normed_two, inverse_two = normalize(sum_ffn)
    result = normed_two * ffn_gain + ffn_shift
    result = jnp.where(drop_flag > 0, layer_input.astype(jnp.float32), result)
    kept_items = (
        layer_input,
        query_low,
        key_local,
        value_local,
        attended,
        log_total,
        sum_attn,
        inner_pre,
        sum_ffn,
    ) + gathered
    return (result, kept_items)


def layer_backward(grad_out, kept_items, params, seg_query):
    (
        qkv_weight,
        query_bias,
        value_bias,
        attn_weight,
        attn_bias,
        attn_gain,
        attn_shift,
        inner_weight,
        inner_bias,
        outer_weight,
        outer_bias,
        ffn_gain,
        ffn_shift,
    ) = params
    (
        layer_input,
        query_low,
        key_local,
        value_local,
        attended,
        log_total,
        sum_attn,
        inner_pre,
        sum_ffn,
    ) = kept_items[:9]
    model_width = layer_input.shape[1]
    row_count = layer_input.shape[0]
    normed, inverse = normalize(sum_attn)
    first_norm = normed * attn_gain + attn_shift
    normed_two, inverse_two = normalize(sum_ffn)
    grad_ffn_gain = jnp.sum(grad_out * normed_two, axis=0)
    grad_ffn_shift = jnp.sum(grad_out, axis=0)
    grad_sum_ffn = norm_back(grad_out, normed_two, inverse_two, ffn_gain)
    grad_ffn_low = grad_sum_ffn.astype(jnp.bfloat16)
    active, gelu_pull = jax.vjp(partial(jax.nn.gelu, approximate=False), inner_pre)
    grad_outer_weight = left_product(active.astype(jnp.bfloat16), grad_ffn_low)
    grad_outer_bias = jnp.sum(grad_ffn_low.astype(jnp.float32), axis=0)
    grad_active = right_product(grad_ffn_low, outer_weight)
    grad_inner = gelu_pull(grad_active)[0].astype(jnp.bfloat16)
    grad_inner_weight = left_product(first_norm.astype(jnp.bfloat16), grad_inner)
    grad_inner_bias = jnp.sum(grad_inner.astype(jnp.float32), axis=0)
    grad_first = grad_sum_ffn + right_product(grad_inner, inner_weight)
    grad_attn_gain = jnp.sum(grad_first * normed, axis=0)
    grad_attn_shift = jnp.sum(grad_first, axis=0)
    grad_sum_attn = norm_back(grad_first, normed, inverse, attn_gain)
    grad_branch = grad_sum_attn.astype(jnp.bfloat16)
    grad_attn_weight = left_product(attended.astype(jnp.bfloat16), grad_branch)
    grad_attn_bias = jnp.sum(grad_branch.astype(jnp.float32), axis=0)
    grad_attended = right_product(grad_branch, attn_weight).astype(jnp.bfloat16)
    key_all, value_all, seg_all, pad_all = kept_items[9:]
    row_delta = jnp.sum(
        (grad_attended.astype(jnp.float32) * attended).reshape(row_count, HEADS, HEAD_DIM), axis=-1
    ).T
    grad_query, grad_key_all, grad_value_all = attention_back(
        query_low,
        key_all,
        value_all,
        seg_query,
        seg_all,
        pad_all,
        log_total,
        row_delta,
        grad_attended,
    )
    grad_key, grad_value = (
        lax.psum_scatter(
            grad_key_all.astype(jnp.bfloat16), "ctx", scatter_dimension=0, tiled=True
        ).astype(jnp.float32),
        lax.psum_scatter(
            grad_value_all.astype(jnp.bfloat16), "ctx", scatter_dimension=0, tiled=True
        ).astype(jnp.float32),
    )
    grad_qkv = jnp.concatenate([grad_query, grad_key, grad_value], axis=1).astype(jnp.bfloat16)
    grad_qkv_weight = left_product(layer_input, grad_qkv)
    grad_query_bias = jnp.sum(grad_qkv[:, :model_width].astype(jnp.float32), axis=0)
    grad_value_bias = jnp.sum(grad_qkv[:, 2 * model_width :].astype(jnp.float32), axis=0)
    grad_input = grad_sum_attn + right_product(grad_qkv, qkv_weight)
    layer_grads = (
        grad_qkv_weight,
        grad_query_bias,
        grad_value_bias,
        grad_attn_weight,
        grad_attn_bias,
        grad_attn_gain,
        grad_attn_shift,
        grad_inner_weight,
        grad_inner_bias,
        grad_outer_weight,
        grad_outer_bias,
        grad_ffn_gain,
        grad_ffn_shift,
    )
    return (layer_grads, grad_input)


def body(
    tokens,
    segment_ids,
    padding,
    dropped,
    qkv_weight,
    query_bias,
    value_bias,
    attn_weight,
    attn_bias,
    attn_gain,
    attn_shift,
    inner_weight,
    inner_bias,
    outer_weight,
    outer_bias,
    ffn_gain,
    ffn_shift,
    cotangent,
):
    micro_count = tokens.shape[0]
    section_index = lax.axis_index("section")
    half_width = tokens.shape[2] // lax.axis_size("section")
    params = tuple(
        (
            member[0]
            for member in (
                qkv_weight,
                query_bias,
                value_bias,
                attn_weight,
                attn_bias,
                attn_gain,
                attn_shift,
                inner_weight,
                inner_bias,
                outer_weight,
                outer_bias,
                ffn_gain,
                ffn_shift,
            )
        )
    )
    drop_row = dropped[0]
    incoming = jnp.zeros(tokens.shape[1:], jnp.bfloat16)
    saved_ticks = []
    encoded_rows = []
    for tick_index in range(micro_count + 1):
        micro_index = jnp.clip(tick_index - section_index, 0, micro_count - 1)
        own_input = lax.dynamic_index_in_dim(tokens, micro_index, 0, False)
        layer_input = jnp.where(section_index == 0, own_input, incoming)
        seg_query = lax.dynamic_index_in_dim(segment_ids, micro_index, 0, False)
        pad_query = lax.dynamic_index_in_dim(padding, micro_index, 0, False)
        drop_flag = lax.dynamic_index_in_dim(drop_row, micro_index, 0, False)
        layer_out, kept_items = layer_forward(layer_input, params, seg_query, pad_query, drop_flag)
        layer_low = layer_out.astype(jnp.bfloat16)
        received = shifted(layer_low, "section", 1)
        incoming = received
        if tick_index >= 1:
            encoded_rows.append(jnp.where(section_index == 0, received, layer_low))
        saved_ticks.append(kept_items)
    stacked = jax.tree.map(lambda *members: jnp.stack(members), *saved_ticks)
    grad_totals = tuple((jnp.zeros(member.shape, jnp.float32) for member in params))
    grad_incoming = jnp.zeros(tokens.shape[1:], jnp.bfloat16)
    input_rows = []
    for tick_index in range(micro_count + 1):
        raw_index = tick_index - 1 + section_index
        micro_index = jnp.clip(raw_index, 0, micro_count - 1)
        live_tick = ((raw_index >= 0) & (raw_index < micro_count)).astype(jnp.float32)
        forward_tick = jnp.clip(tick_index - 1 + 2 * section_index, 0, micro_count)
        kept_items = jax.tree.map(
            lambda member: lax.dynamic_index_in_dim(member, forward_tick, 0, False), stacked
        )
        own_cot = lax.dynamic_index_in_dim(cotangent, micro_index, 0, False)
        upstream = jnp.where(section_index == 1, own_cot, grad_incoming).astype(jnp.float32)
        seg_query = lax.dynamic_index_in_dim(segment_ids, micro_index, 0, False)
        pad_query = lax.dynamic_index_in_dim(padding, micro_index, 0, False)
        drop_flag = lax.dynamic_index_in_dim(drop_row, micro_index, 0, False)
        keep_scale = (drop_flag == 0).astype(jnp.float32) * live_tick
        layer_grads, grad_input = layer_backward(
            upstream * keep_scale, kept_items, params, seg_query
        )
        grad_totals = tuple((total + term for total, term in zip(grad_totals, layer_grads)))
        grad_input = grad_input + (drop_flag > 0).astype(jnp.float32) * upstream
        grad_low = grad_input.astype(jnp.bfloat16)
        received = shifted(grad_low, "section", 1)
        grad_incoming = received
        if tick_index >= 1:
            input_rows.append(jnp.where(section_index == 0, grad_low, received))
    reduced_once = (
        lax.psum_scatter(
            grad_totals[0][None].astype(jnp.bfloat16), "dp", scatter_dimension=1, tiled=True
        ).astype(jnp.float32),
        lax.psum_scatter(
            grad_totals[3][None].astype(jnp.bfloat16), "dp", scatter_dimension=1, tiled=True
        ).astype(jnp.float32),
        lax.psum_scatter(
            grad_totals[7][None].astype(jnp.bfloat16), "dp", scatter_dimension=1, tiled=True
        ).astype(jnp.float32),
        lax.psum_scatter(
            grad_totals[9][None].astype(jnp.bfloat16), "dp", scatter_dimension=1, tiled=True
        ).astype(jnp.float32),
    )
    matrix_grads = (
        lax.psum_scatter(
            reduced_once[0].astype(jnp.bfloat16), "ctx", scatter_dimension=2, tiled=True
        ).astype(jnp.float32),
        lax.psum_scatter(
            reduced_once[1].astype(jnp.bfloat16), "ctx", scatter_dimension=2, tiled=True
        ).astype(jnp.float32),
        lax.psum_scatter(
            reduced_once[2].astype(jnp.bfloat16), "ctx", scatter_dimension=2, tiled=True
        ).astype(jnp.float32),
        lax.psum_scatter(
            reduced_once[3].astype(jnp.bfloat16), "ctx", scatter_dimension=2, tiled=True
        ).astype(jnp.float32),
    )
    vector_grads = lax.psum(
        (
            grad_totals[1][None],
            grad_totals[2][None],
            grad_totals[4][None],
            grad_totals[5][None],
            grad_totals[6][None],
            grad_totals[8][None],
            grad_totals[10][None],
            grad_totals[11][None],
            grad_totals[12][None],
        ),
        ("dp", "ctx"),
    )
    encoded = lax.dynamic_slice_in_dim(
        jnp.stack(encoded_rows), section_index * half_width, half_width, 2
    )
    tokens_grad = lax.dynamic_slice_in_dim(
        jnp.stack(input_rows), section_index * half_width, half_width, 2
    )
    return (
        encoded,
        tokens_grad,
        matrix_grads[0],
        vector_grads[0],
        vector_grads[1],
        matrix_grads[1],
        vector_grads[2],
        vector_grads[3],
        vector_grads[4],
        matrix_grads[2],
        vector_grads[5],
        matrix_grads[3],
        vector_grads[6],
        vector_grads[7],
        vector_grads[8],
    )


def dot_plain(left, right):
    return lax.dot_general(left, right, (((1,), (0,)), ((), ())), preferred_element_type=jnp.float32)


def dot_flipped(left, right):
    return lax.dot_general(left, right, (((1,), (1,)), ((), ())), preferred_element_type=jnp.float32)


def gelu_parts(x):
    below = 0.5 * (1.0 + lax.erf(x * 0.7071067811865476))
    density = jnp.exp(-0.5 * x * x) * 0.3989422804014327
    return (x * below, below + x * density)


def rows_of(index, size):
    return pl.ds(pl.multiple_of(index * size, size), size)


def piece_rows(ctx, at, count, n_pieces):
    return pl.ds(0, count) if n_pieces == 1 else rows_of(ctx ^ at, count)


def head_lanes(shape, which):
    lane = lax.broadcasted_iota(jnp.int32, shape, 1)
    return (lane < HEAD_DIM) if which == 0 else (lane >= HEAD_DIM)


def mask_into(mask_ref, code_ref, seg_ref):
    mask_ref[...] = jnp.where(code_ref[...] == seg_ref[...], 0.0, masked_score)


def copy_list(pairs, sems, first=0):
    copies = [pltpu.make_async_copy(src, dst, sems.at[first + at]) for at, (src, dst) in enumerate(pairs)]
    for copy in copies:
        copy.start()
    return copies


def forward_kernel(active, n_pieces, n_alias, scal, seg_ref, code_ref, qkv_bias_ref, qkv_scale_ref, vec_ref, inner_bias_ref, *refs):
    pieces = refs[:n_pieces]
    wqkv_h, wattn_h, win_h, wout_h = refs[n_pieces : n_pieces + 4]
    outs = refs[n_pieces + 4 + n_alias :]
    u_h, qkv_h, att_h, lse_h, n1_h, r1_h, first_h, dg_h, n2_h, r2_h, res_h = outs[:11]
    (wqkv, wattn, win, wout, u, qkv, att, lse, n1, r1, flow, dg, n2, r2, res, first, acc, mask, sems) = outs[11:]
    size, width = u.shape
    hidden = win.shape[1]

    @pl.when(scal[0] == active)
    def _():
        count = size // n_pieces
        ctx = scal[1]
        start = copy_list(
            [
                (piece, u.at[piece_rows(ctx, at, count, n_pieces)]) for at, piece in enumerate(pieces)
            ]
            + [(wqkv_h, wqkv), (wattn_h, wattn), (win_h, win), (wout_h, wout)],
            sems,
        )
        mask_into(mask, code_ref, seg_ref)
        for copy in start[: n_pieces + 1]:
            copy.wait()

        def project(at, carry):
            cols = rows_of(at, 256)
            value = dot_plain(u[...], wqkv[:, cols]) + qkv_bias_ref[:, cols]
            qkv[:, cols] = (value * qkv_scale_ref[:, cols]).astype(jnp.bfloat16)
            return carry

        lax.fori_loop(0, 3 * width // 256, project, 0)

        def heads(at, carry):
            cols = [rows_of(at + part * (width // 128), 128) for part in range(3)]
            query, key, value = (qkv[:, col] for col in cols)
            value_t = value.T
            both = []
            for which in range(2):
                key_own = jnp.where(head_lanes(key.shape, which), key, jnp.zeros_like(key))
                scores = dot_flipped(key_own, query) + mask[...]
                top = jnp.max(scores, axis=0, keepdims=True)
                weights = jnp.exp(scores - top)
                total = jnp.sum(weights, axis=0, keepdims=True)
                lse[pl.ds(2 * at + which, 1), :] = top + jnp.log(total)
                part = value_t[which * HEAD_DIM : (which + 1) * HEAD_DIM]
                both.append(dot_plain(part, weights.astype(jnp.bfloat16)) / total)
            att[:, cols[0]] = jnp.concatenate(both, axis=0).T.astype(jnp.bfloat16)
            return carry

        lax.fori_loop(0, width // 128, heads, 0)
        out_copies = copy_list([(u, u_h), (qkv, qkv_h), (att, att_h), (lse, lse_h)], sems, n_pieces + 4)
        start[n_pieces + 1].wait()

        def branch(at, carry):
            cols = rows_of(at, 256)
            first[:, cols] = dot_plain(att[...], wattn[:, cols])
            return carry

        lax.fori_loop(0, width // 256, branch, 0)

        def norm_one(at, carry):
            rows = rows_of(at, 64)
            value = u[rows].astype(jnp.float32) + first[rows] + vec_ref[0:1, :]
            normed, inverse = normalize(value)
            n1[rows] = normed
            r1[rows] = jnp.broadcast_to(inverse, (64, 128))
            value = normed * vec_ref[1:2, :] + vec_ref[2:3, :]
            first[rows] = value
            flow[rows] = value.astype(jnp.bfloat16)
            return carry

        lax.fori_loop(0, size // 64, norm_one, 0)
        out_copies += copy_list([(n1, n1_h), (r1, r1_h), (flow, first_h)], sems, n_pieces + 8)
        start[n_pieces + 2].wait()
        start[n_pieces + 3].wait()
        acc[...] = first[...] + vec_ref[3:4, :]

        def feed(at, carry):
            cols = rows_of(at, 512)
            inner = dot_plain(flow[...], win[:, cols]) + inner_bias_ref[:, cols]
            active_value, slope = gelu_parts(inner)
            dg[:, cols] = slope.astype(jnp.bfloat16)
            acc[...] += dot_plain(active_value.astype(jnp.bfloat16), wout[cols, :])
            return carry

        lax.fori_loop(0, hidden // 512, feed, 0)
        dropped = scal[2]

        def norm_two(at, carry):
            rows = rows_of(at, 64)
            normed, inverse = normalize(acc[rows])
            n2[rows] = normed
            r2[rows] = jnp.broadcast_to(inverse, (64, 128))
            value = normed * vec_ref[4:5, :] + vec_ref[5:6, :]
            value = jnp.where(dropped > 0, u[rows].astype(jnp.float32), value)
            res[rows] = value.astype(jnp.bfloat16)
            return carry

        lax.fori_loop(0, size // 64, norm_two, 0)
        out_copies += copy_list([(dg, dg_h), (n2, n2_h), (r2, r2_h), (res, res_h)], sems, n_pieces + 11)
        for copy in out_copies:
            copy.wait()


def kernel_call(body, out_shapes, scratch, operands, n_smem, n_vmem, aliases=None, flops=0, nbytes=0):
    specs = (
        [pl.BlockSpec(memory_space=pltpu.SMEM)] * n_smem
        + [pl.BlockSpec(memory_space=pltpu.VMEM)] * n_vmem
        + [pl.BlockSpec(memory_space=pl.ANY)] * (len(operands) - n_smem - n_vmem)
    )
    return pl.pallas_call(
        body,
        out_shape=out_shapes,
        in_specs=specs,
        out_specs=jax.tree.map(lambda s: pl.BlockSpec(memory_space=pl.ANY), out_shapes),
        scratch_shapes=scratch,
        input_output_aliases=aliases or {},
        cost_estimate=pl.CostEstimate(flops=flops, bytes_accessed=nbytes, transcendentals=0),
        compiler_params=pltpu.CompilerParams(vmem_limit_bytes=60 * 2**20),
    )(*operands)


def run_forward(active, scal, seg_row, code_col, small, pieces, weights, earlier):
    qkv_bias, qkv_scale, vecs, inner_bias = small
    wqkv, wattn, win, wout = weights
    width, hidden = win.shape
    size = seg_row.shape[1]
    low, full = jnp.bfloat16, jnp.float32
    outs = [
        jax.ShapeDtypeStruct(shape, kind)
        for shape, kind in (
            ((size, width), low),
            ((size, 3 * width), low),
            ((size, width), low),
            ((16, size), full),
            ((size, width), full),
            ((size, 128), full),
            ((size, width), low),
            ((size, hidden), low),
            ((size, width), full),
            ((size, 128), full),
            ((size, width), low),
        )
    ]
    scratch = (
        [pltpu.VMEM(w.shape, low) for w in weights]
        + [pltpu.VMEM(out.shape, out.dtype) for out in outs]
        + [
            pltpu.VMEM((size, width), full),
            pltpu.VMEM((size, width), full),
            pltpu.VMEM((size, size), full),
            pltpu.SemaphoreType.DMA((len(pieces) + 15,)),
        ]
    )
    operands = [scal, seg_row, code_col, qkv_bias, qkv_scale, vecs, inner_bias, *pieces, *weights, *earlier]
    at_alias = len(operands) - len(earlier)
    body = partial(forward_kernel, active, len(pieces), len(earlier))
    return kernel_call(
        body, outs, scratch, operands, 1, 6, {at_alias + i: i for i in range(len(earlier))}, 8 * 10**9, 10**7
    )


def top_kernel(active, n_pieces, n_alias, scal, vec_ref, *refs):
    pieces = refs[:n_pieces]
    n2_h, r2_h = refs[n_pieces : n_pieces + 2]
    outs = refs[n_pieces + 2 + n_alias :]
    inc_h, dffn_h, dsum_h, vec_h = outs[:4]
    inc, dffn, dsum, vec, n2, r2, sems = outs[4:]
    size, width = inc.shape

    @pl.when(scal[0] == active)
    def _():
        count = size // n_pieces
        ctx = scal[1]
        start = copy_list(
            [
                (piece, inc.at[piece_rows(ctx, at, count, n_pieces)]) for at, piece in enumerate(pieces)
            ]
            + [(n2_h, n2), (r2_h, r2)],
            sems,
        )
        for copy in start:
            copy.wait()
        keep = jnp.where(scal[2] > 0, 0.0, 1.0)
        vec[...] = jnp.zeros_like(vec)

        def step(at, carry):
            rows = rows_of(at, 64)
            grad = inc[rows].astype(jnp.float32) * keep
            normed = n2[rows]
            value = norm_back(grad, normed, r2[rows][:, :1], vec_ref[4:5, :])
            dsum[rows] = value
            low = value.astype(jnp.bfloat16)
            dffn[rows] = low
            vec[0:1, :] += jnp.sum(low.astype(jnp.float32), axis=0, keepdims=True)
            vec[1:2, :] += jnp.sum(grad * normed, axis=0, keepdims=True)
            vec[2:3, :] += jnp.sum(grad, axis=0, keepdims=True)
            return carry

        lax.fori_loop(0, size // 64, step, 0)
        for copy in copy_list([(inc, inc_h), (dffn, dffn_h), (dsum, dsum_h), (vec, vec_h)], sems, n_pieces + 2):
            copy.wait()


def run_top(active, scal, vecs, pieces, n2, r2, earlier):
    size, width = n2.shape
    low, full = jnp.bfloat16, jnp.float32
    outs = [
        jax.ShapeDtypeStruct((size, width), low),
        jax.ShapeDtypeStruct((size, width), low),
        jax.ShapeDtypeStruct((size, width), full),
        jax.ShapeDtypeStruct((8, width), full),
    ]
    scratch = [pltpu.VMEM(out.shape, out.dtype) for out in outs] + [
        pltpu.VMEM((size, width), full),
        pltpu.VMEM((size, 128), full),
        pltpu.SemaphoreType.DMA((len(pieces) + 6,)),
    ]
    operands = [scal, vecs, *pieces, n2, r2, *earlier]
    at_alias = len(operands) - len(earlier)
    body = partial(top_kernel, active, len(pieces), len(earlier))
    return kernel_call(
        body, outs, scratch, operands, 1, 1, {at_alias + i: i for i in range(len(earlier))}, 10**7, 10**7
    )


def chain_kernel(active, n_alias, scal, seg_ref, code_ref, vec_ref, *refs):
    ins, rest = refs[:15], refs[15 + n_alias :]
    inc_h, dffn_h, dsum_h, dg_h, n1_h, r1_h, att_h, qkv_h, lse_h = ins[:9]
    wqkv_h, wattn_h, win_h, wout_h = ins[9:13]
    dqkv_h, dbranch_h, din_h, vec_h = rest[:4]
    (dqkv, dbranch, din, vec, inc, dffn, dsum, dg, n1, r1, qkv, lse, wqkv, wattn, win, wout, first, datt, mask, sems) = rest[4:]
    size, width = inc.shape
    hidden = win.shape[1]

    @pl.when(scal[0] == active)
    def _():
        start = copy_list(
            [
                (dffn_h, dffn),
                (wout_h, wout),
                (dg_h, dg),
                (win_h, win),
                (dsum_h, dsum),
                (n1_h, n1),
                (r1_h, r1),
                (wattn_h, wattn),
                (qkv_h, qkv),
                (lse_h, lse),
                (wqkv_h, wqkv),
                (inc_h, inc),
            ],
            sems,
        )
        mask_into(mask, code_ref, seg_ref)
        vec[...] = jnp.zeros_like(vec)
        for copy in start[:3]:
            copy.wait()

        def inner(at, carry):
            cols = rows_of(at, width)
            grad = dot_flipped(dffn[...], wout[cols, :]) * dg[:, cols].astype(jnp.float32)
            low = grad.astype(jnp.bfloat16)
            dg[:, cols] = low
            vec[pl.ds(8 + at, 1), :] = jnp.sum(low.astype(jnp.float32), axis=0, keepdims=True)
            return carry

        lax.fori_loop(0, hidden // width, inner, 0)
        start[3].wait()

        def outer(at, carry):
            cols = rows_of(at, 256)
            first[:, cols] = dot_flipped(dg[...], win[cols, :])
            return carry

        lax.fori_loop(0, width // 256, outer, 0)
        for copy in start[4:8]:
            copy.wait()

        def norm_step(at, carry):
            rows = rows_of(at, 64)
            grad = first[rows] + dsum[rows]
            normed = n1[rows]
            value = norm_back(grad, normed, r1[rows][:, :1], vec_ref[1:2, :])
            dsum[rows] = value
            low = value.astype(jnp.bfloat16)
            dbranch[rows] = low
            vec[2:3, :] += jnp.sum(low.astype(jnp.float32), axis=0, keepdims=True)
            vec[3:4, :] += jnp.sum(grad * normed, axis=0, keepdims=True)
            vec[4:5, :] += jnp.sum(grad, axis=0, keepdims=True)
            return carry

        lax.fori_loop(0, size // 64, norm_step, 0)

        def attended(at, carry):
            cols = rows_of(at, 256)
            datt[:, cols] = dot_flipped(dbranch[...], wattn[cols, :]).astype(jnp.bfloat16)
            return carry

        lax.fori_loop(0, width // 256, attended, 0)
        for copy in start[8:10]:
            copy.wait()

        def heads(at, carry):
            cols = [rows_of(at + part * (width // 128), 128) for part in range(3)]
            query, key, value = (qkv[:, col] for col in cols)
            grad = datt[:, cols[0]]
            key_t = key.T
            parts = []
            for which in range(2):
                own = head_lanes(key.shape, which)
                key_own = jnp.where(own, key, jnp.zeros_like(key))
                value_own = jnp.where(own, value, jnp.zeros_like(value))
                scores = dot_flipped(key_own, query) + mask[...]
                probs = jnp.exp(scores - lse[pl.ds(2 * at + which, 1), :])
                dprobs = dot_flipped(value_own, grad)
                delta = jnp.sum(probs * dprobs, axis=0, keepdims=True)
                dscores = (probs * (dprobs - delta)).astype(jnp.bfloat16)
                parts.append(
                    (
                        dot_plain(key_t[which * HEAD_DIM : (which + 1) * HEAD_DIM], dscores),
                        dot_plain(dscores, query),
                        dot_plain(probs.astype(jnp.bfloat16), grad),
                    )
                )
            low_lanes = head_lanes((size, 128), 0)
            dquery = jnp.concatenate([parts[0][0], parts[1][0]], axis=0).T * HEAD_DIM ** (-0.5)
            dkey = jnp.where(low_lanes, parts[0][1], parts[1][1])
            dvalue = jnp.where(low_lanes, parts[0][2], parts[1][2])
            dquery = dquery.astype(jnp.bfloat16)
            dvalue = dvalue.astype(jnp.bfloat16)
            dqkv[:, cols[0]] = dquery
            dqkv[:, cols[1]] = dkey.astype(jnp.bfloat16)
            dqkv[:, cols[2]] = dvalue
            vec[0:1, cols[0]] = jnp.sum(dquery.astype(jnp.float32), axis=0, keepdims=True)
            vec[1:2, cols[0]] = jnp.sum(dvalue.astype(jnp.float32), axis=0, keepdims=True)
            return carry

        lax.fori_loop(0, width // 128, heads, 0)
        out_copies = copy_list([(dqkv, dqkv_h), (dbranch, dbranch_h), (vec, vec_h)], sems, 12)
        for copy in start[10:]:
            copy.wait()
        dropped = scal[2]

        def back(at, carry):
            cols = rows_of(at, 256)
            value = dsum[:, cols] + dot_flipped(dqkv[...], wqkv[cols, :])
            value = jnp.where(dropped > 0, inc[:, cols].astype(jnp.float32), value)
            din[:, cols] = value.astype(jnp.bfloat16)
            return carry

        lax.fori_loop(0, width // 256, back, 0)
        out_copies += copy_list([(din, din_h)], sems, 15)
        for copy in out_copies:
            copy.wait()


def run_chain(active, scal, seg_row, code_col, vecs, top, kept, weights, earlier):
    u, qkv, att, lse, n1, r1, first, dg, n2, r2, res = kept
    inc, dffn, dsum, vec = top
    wqkv, wattn, win, wout = weights
    size, width = u.shape
    low, full = jnp.bfloat16, jnp.float32
    outs = [
        jax.ShapeDtypeStruct((size, 3 * width), low),
        jax.ShapeDtypeStruct((size, width), low),
        jax.ShapeDtypeStruct((size, width), low),
        jax.ShapeDtypeStruct((16, width), full),
    ]
    held = [inc, dffn, dsum, dg, n1, r1, qkv, lse, *weights]
    scratch = (
        [pltpu.VMEM(out.shape, out.dtype) for out in outs]
        + [pltpu.VMEM(member.shape, member.dtype) for member in held]
        + [
            pltpu.VMEM((size, width), full),
            pltpu.VMEM((size, width), low),
            pltpu.VMEM((size, size), full),
            pltpu.SemaphoreType.DMA((16,)),
        ]
    )
    operands = [scal, seg_row, code_col, vecs, inc, dffn, dsum, dg, n1, r1, att, qkv, lse, *weights, u, res, *earlier]
    at_alias = len(operands) - len(earlier)
    body = partial(chain_kernel, active, len(earlier))
    return kernel_call(
        body, outs, scratch, operands, 1, 3, {at_alias + i: i for i in range(len(earlier))}, 10**10, 10**7
    )


def attn_grad_kernel(u_ref, att_ref, dqkv_ref, dbranch_ref, out_ref, flipped):
    width = u_ref.shape[1]
    flipped[...] = u_ref[...].T

    def project(at, carry):
        cols = rows_of(at, 256)
        out_ref[:, cols] = dot_plain(flipped[...], dqkv_ref[:, cols]).astype(jnp.bfloat16)
        return carry

    lax.fori_loop(0, 3 * width // 256, project, 0)
    flipped[...] = att_ref[...].T

    def branch(at, carry):
        cols = rows_of(at, 256)
        out_ref[:, rows_of(at + 3 * width // 256, 256)] = dot_plain(flipped[...], dbranch_ref[:, cols]).astype(
            jnp.bfloat16
        )
        return carry

    lax.fori_loop(0, width // 256, branch, 0)


def run_attn_grad(u, att, dqkv, dbranch):
    size, width = u.shape
    return pl.pallas_call(
        attn_grad_kernel,
        out_shape=jax.ShapeDtypeStruct((width, 4 * width), jnp.bfloat16),
        scratch_shapes=[pltpu.VMEM((width, size), jnp.bfloat16)],
        cost_estimate=pl.CostEstimate(flops=2 * size * width * 4 * width, bytes_accessed=10**7, transcendentals=0),
        compiler_params=pltpu.CompilerParams(vmem_limit_bytes=60 * 2**20),
    )(u, att, dqkv, dbranch)


def ffn_grad_kernel(n_pieces, n_blocks, scal, inner_bias_ref, *refs):
    firsts, dffns = refs[:n_pieces], refs[n_pieces : 2 * n_pieces]
    win_h, wout_h, out_h = refs[2 * n_pieces : 2 * n_pieces + 3]
    win, wout, bias, first, dffn, first_t, dffn_t, active, dinner, out, sems = refs[2 * n_pieces + 3 :]
    width = win.shape[0]
    each = width // n_blocks
    size = first.shape[0] // n_pieces
    own = rows_of(scal[3], width)
    start = copy_list(
        [(win_h.at[:, own], win), (wout_h.at[own, :], wout)]
        + [(piece, first.at[pl.ds(at * size, size)]) for at, piece in enumerate(firsts)]
        + [(piece, dffn.at[pl.ds(at * size, size)]) for at, piece in enumerate(dffns)],
        sems,
    )
    bias[...] = inner_bias_ref[:, own]
    for copy in start:
        copy.wait()

    def tokens(at, carry):
        rows = rows_of(at, 256)
        value, grad = first[rows], dffn[rows]
        first_t[:, rows] = value.T
        dffn_t[:, rows] = grad.T
        inner = dot_plain(value, win[...]) + bias[...]
        active_value, slope = gelu_parts(inner)
        active[rows] = active_value.astype(jnp.bfloat16)
        dinner[rows] = (dot_flipped(grad, wout[...]) * slope).astype(jnp.bfloat16)
        return carry

    lax.fori_loop(0, n_pieces * size // 256, tokens, 0)

    def blocks(at, carry):
        cols = rows_of(at, 256)
        inner_part = dot_plain(first_t[...], dinner[:, cols]).astype(jnp.bfloat16)
        outer_part = dot_plain(dffn_t[...], active[:, cols]).astype(jnp.bfloat16)
        for block in range(n_blocks):
            out[2 * each * block : 2 * each * block + each, cols] = inner_part[each * block : each * (block + 1)]
            out[2 * each * block + each : 2 * each * (block + 1), cols] = outer_part[
                each * block : each * (block + 1)
            ]
        return carry

    lax.fori_loop(0, width // 256, blocks, 0)
    for copy in copy_list([(out, out_h)], sems, 2 * n_pieces + 2):
        copy.wait()


def run_ffn_grad(scal, inner_bias, firsts, dffns, win, wout, n_blocks):
    size, width = firsts[0].shape
    count = len(firsts)
    low = jnp.bfloat16
    out = jax.ShapeDtypeStruct((2 * width, width), low)
    scratch = [
        pltpu.VMEM((width, width), low),
        pltpu.VMEM((width, width), low),
        pltpu.VMEM((1, width), jnp.float32),
        pltpu.VMEM((count * size, width), low),
        pltpu.VMEM((count * size, width), low),
        pltpu.VMEM((width, count * size), low),
        pltpu.VMEM((width, count * size), low),
        pltpu.VMEM((count * size, width), low),
        pltpu.VMEM((count * size, width), low),
        pltpu.VMEM((2 * width, width), low),
        pltpu.SemaphoreType.DMA((2 * count + 3,)),
    ]
    operands = [scal, inner_bias, *firsts, *dffns, win, wout]
    return kernel_call(
        partial(ffn_grad_kernel, count, n_blocks), out, scratch, operands, 1, 1, None, 8 * size * count * width**2, 10**7
    )


def swapped(x, axis, by):
    return lax.ppermute(x, axis, [(i, i ^ by) for i in range(lax.axis_size(axis))])


def swapped_in(section, x, by):
    length = lax.axis_size("ctx")
    pairs = [(section * length + i, section * length + (i ^ by)) for i in range(length)]
    return lax.ppermute(x, ("section", "ctx"), pairs)


def pick(x, at, dim=0):
    return lax.dynamic_index_in_dim(x, at, dim, False)


def halved(x, dim, axis, by):
    own = (lax.axis_index(axis) & by) // by
    received = swapped(pick(x, 1 - own, dim), axis, by)
    return (pick(x, own, dim).astype(jnp.float32) + received.astype(jnp.float32)).astype(jnp.bfloat16)


def whole_row(pieces, ctx):
    out = jnp.zeros((len(pieces),) + pieces[0].shape, pieces[0].dtype)
    for at, piece in enumerate(pieces):
        out = lax.dynamic_update_index_in_dim(out, piece, ctx ^ at, 0)
    return out


def spread(row_half, ctx):
    length = lax.axis_size("ctx")
    size, width = row_half.shape
    parts = row_half.reshape(length, size // length, width)
    pieces = [pick(parts, ctx)] + [swapped(pick(parts, ctx ^ k), "ctx", k) for k in range(1, length)]
    return whole_row(pieces, ctx)


def row_body(
    tokens,
    segment_ids,
    padding,
    dropped,
    qkv_weight,
    query_bias,
    value_bias,
    attn_weight,
    attn_bias,
    attn_gain,
    attn_shift,
    inner_weight,
    inner_bias,
    outer_weight,
    outer_bias,
    ffn_gain,
    ffn_shift,
    cotangent,
):
    width = tokens.shape[2]
    half = width // 2
    length = lax.axis_size("ctx")
    dp_size = lax.axis_size("dp")
    section, dp, ctx = (lax.axis_index(name) for name in ("section", "dp", "ctx"))
    weights = (qkv_weight[0], attn_weight[0], inner_weight[0], outer_weight[0])
    vecs = jnp.concatenate(
        [attn_bias, attn_gain, attn_shift, outer_bias, ffn_gain, ffn_shift, query_bias, value_bias]
    )
    qkv_bias = jnp.concatenate([query_bias, jnp.zeros_like(query_bias), value_bias], axis=1)
    qkv_scale = jnp.concatenate(
        [jnp.full((1, width), HEAD_DIM ** (-0.5), jnp.float32), jnp.ones((1, 2 * width), jnp.float32)], axis=1
    )
    small = (qkv_bias, qkv_scale, vecs, inner_bias)
    scal = jnp.stack([section, ctx, pick(dropped[0], ctx), dp]).astype(jnp.int32)

    ids = jnp.stack([segment_ids, jnp.where(padding == 1, segment_ids, -1)], axis=1)
    id_pieces = [pick(ids, ctx)] + [swapped(pick(ids, ctx ^ k), "ctx", k) for k in range(1, length)]
    row_ids = whole_row(id_pieces, ctx)
    seg_row = row_ids[:, 0].reshape(1, -1)
    code_col = row_ids[:, 1].reshape(-1, 1)
    own_tokens = [pick(tokens, ctx)] + [swapped_in(0, pick(tokens, ctx ^ k), k) for k in range(1, length)]
    own_cot = [pick(cotangent, ctx)] + [swapped_in(1, pick(cotangent, ctx ^ k), k) for k in range(1, length)]

    kept = run_forward(0, scal, seg_row, code_col, small, own_tokens, weights, [])
    middle = lax.ppermute(kept[10], "section", [(0, 1)])
    kept = run_forward(1, scal, seg_row, code_col, small, [middle], weights, kept)
    first = kept[6]
    firsts = [first] + [swapped(first, "dp", k) for k in range(1, dp_size)]
    result = kept[10]
    encoded_half = jnp.where(
        section == 1, result[:, half:], lax.ppermute(result[:, :half], "section", [(1, 0)])
    )
    encoded = spread(encoded_half, ctx)

    top = run_top(1, scal, vecs, own_cot, kept[8], kept[9], [])
    chain = run_chain(1, scal, seg_row, code_col, vecs, top, kept, weights, [])
    incoming = lax.ppermute(chain[2], "section", [(1, 0)])
    top = run_top(0, scal, vecs, [incoming], kept[8], kept[9], top)
    dffn = top[1]
    dffns = [dffn] + [swapped(dffn, "dp", k) for k in range(1, dp_size)]
    chain = run_chain(0, scal, seg_row, code_col, vecs, top, kept, weights, chain)
    dqkv, dbranch, d_input, chain_vec = chain

    grad_half = jnp.where(section == 0, d_input[:, :half], lax.ppermute(d_input[:, half:], "section", [(0, 1)]))
    tokens_grad = spread(grad_half, ctx)

    attn_grads = run_attn_grad(kept[0], kept[2], dqkv, dbranch)
    bits = dp_size.bit_length() - 1
    blocks = (2,) * bits
    cut = 2 * width
    parts = []
    for number, columns in enumerate((attn_grads[:, :cut], attn_grads[:, cut:])):
        value = columns.reshape(blocks + (width // dp_size, cut))
        order = list(range(bits)) if number == 0 else list(reversed(range(bits)))
        left = list(reversed(range(bits)))
        for bit in order:
            value = halved(value, left.index(bit), "dp", 1 << bit)
            left.remove(bit)
        parts.append(value)
    own_rows = jnp.concatenate(parts, axis=1)
    rows = width // dp_size
    own_rows = jnp.concatenate(
        [
            own_rows[:, : 3 * width].reshape(rows, length, 3 * width // length).transpose(1, 0, 2),
            own_rows[:, 3 * width :].reshape(rows, length, width // length).transpose(1, 0, 2),
        ],
        axis=2,
    )
    ffn_grads = run_ffn_grad(scal, inner_bias, firsts, dffns, weights[2], weights[3], length)
    ffn_rows = ffn_grads.reshape(length, 2 * width // length, width)
    ctx_bits = length.bit_length() - 1

    def over_ctx(value):
        value = value.reshape((2,) * ctx_bits + value.shape[1:])
        left = list(reversed(range(ctx_bits)))
        for bit in range(ctx_bits):
            value = halved(value, left.index(bit), "ctx", 1 << bit)
            left.remove(bit)
        return value

    own_rows = over_ctx(own_rows).astype(jnp.float32)
    ffn_rows = over_ctx(ffn_rows)
    qkv_grad = own_rows[:, : 3 * width // length]
    attn_grad = own_rows[:, 3 * width // length :]
    each = width // length
    inner_grad = lax.ppermute(
        ffn_rows[:each],
        ("dp", "ctx"),
        [(i * length + j, j * length + i) for i in range(dp_size) for j in range(length)],
    ).astype(jnp.float32)
    outer_grad = ffn_rows[each:].astype(jnp.float32).T

    vec = jnp.concatenate([top[3], chain_vec])
    for axis, bound in (("ctx", length), ("dp", dp_size)):
        by = 1
        while by < bound:
            vec = vec + swapped(vec, axis, by)
            by *= 2
    return (
        encoded,
        tokens_grad,
        qkv_grad[None],
        vec[8:9],
        vec[9:10],
        attn_grad[None],
        vec[10:11],
        vec[11:12],
        vec[12:13],
        inner_grad[None],
        vec[16 : 16 + inner_bias.shape[1] // width].reshape(1, -1),
        outer_grad[None],
        vec[0:1],
        vec[1:2],
        vec[2:3],
    )


def solution(mesh):
    placed = (
        P("dp", "ctx", None),
        P("dp", "ctx"),
        P("dp", "ctx"),
        P("section", "dp"),
        P("section", None, None),
        P("section", None),
        P("section", None),
        P("section", None, None),
        P("section", None),
        P("section", None),
        P("section", None),
        P("section", None, None),
        P("section", None),
        P("section", None, None),
        P("section", None),
        P("section", None),
        P("section", None),
        P("dp", "ctx", None),
    )

    def dispatch(*members):
        rows = members[0].shape[0]
        same = rows == lax.axis_size("ctx") == lax.axis_size("dp")
        return (row_body if same and rows & (rows - 1) == 0 else body)(*members)

    return jax.shard_map(
        dispatch,
        mesh=mesh,
        in_specs=placed,
        out_specs=(
            P("dp", "ctx", "section"),
            P("dp", "ctx", "section"),
            P("section", "dp", "ctx"),
            P("section", None),
            P("section", None),
            P("section", "dp", "ctx"),
            P("section", None),
            P("section", None),
            P("section", None),
            P("section", "dp", "ctx"),
            P("section", None),
            P("section", "dp", "ctx"),
            P("section", None),
            P("section", None),
            P("section", None),
        ),
        check_vma=False,
    )
```

```python
from functools import partial

import jax
import jax.numpy as jnp
from jax import lax
from jax.experimental import pallas as pl
from jax.experimental.pallas import tpu as pltpu
from jax.sharding import PartitionSpec as P

HEADS = 12
HEAD_DIM = 64


norm_eps = 1e-05
masked_score = -1e30


def shifted(x, axis, by):
    length = lax.axis_size(axis)
    return lax.ppermute(x, axis, [(i, (i + by) % length) for i in range(length)])


def matmul_low(left, right):
    return jnp.dot(left, right, preferred_element_type=jnp.float32)


def left_product(left, right):
    return jnp.einsum("ti,to->io", left, right, preferred_element_type=jnp.float32)


def right_product(left, right):
    return jnp.einsum("to,io->ti", left, right, preferred_element_type=jnp.float32)


def normalize(values):
    mean_value = jnp.mean(values, axis=-1, keepdims=True)
    centered = values - mean_value
    variance = jnp.mean(centered * centered, axis=-1, keepdims=True)
    inverse = lax.rsqrt(variance + norm_eps)
    return (centered * inverse, inverse)


def norm_back(grad_out, normed, inverse, gain):
    scaled = grad_out * gain
    return inverse * (
        scaled
        - jnp.mean(scaled, axis=-1, keepdims=True)
        - normed * jnp.mean(scaled * normed, axis=-1, keepdims=True)
    )


def attend_piece(query_heads, seg_query, running, pieces):
    run_max, run_total, run_acc = running
    key_piece, value_piece, seg_piece, pad_piece = pieces
    count = key_piece.shape[0]
    key_heads = key_piece.reshape(count, HEADS, HEAD_DIM)
    value_heads = value_piece.reshape(count, HEADS, HEAD_DIM)
    scores = jnp.einsum(
        "qhd,khd->hqk", query_heads, key_heads, preferred_element_type=jnp.float32
    ) * HEAD_DIM ** (-0.5)
    allowed = (seg_query[:, None] == seg_piece[None, :]) & (pad_piece[None, :] == 1)
    scores = jnp.where(allowed[None], scores, masked_score)
    new_max = jnp.maximum(run_max, jnp.max(scores, axis=-1))
    weights = jnp.where(allowed[None], jnp.exp(scores - new_max[..., None]), 0.0)
    run_total = jnp.sum(weights, axis=-1)
    run_acc = jnp.einsum(
        "hqk,khd->hqd",
        weights.astype(jnp.bfloat16),
        value_heads,
        preferred_element_type=jnp.float32,
    )
    return (new_max, run_total, run_acc)


def attention_back(
    query_low, key_all, value_all, seg_query, seg_all, pad_all, log_total, row_delta, grad_att
):
    row_count = query_low.shape[0]
    seq_count = key_all.shape[0]
    score_scale = HEAD_DIM ** (-0.5)
    query_heads = query_low.reshape(row_count, HEADS, HEAD_DIM)
    key_heads = key_all.reshape(seq_count, HEADS, HEAD_DIM)
    value_heads = value_all.reshape(seq_count, HEADS, HEAD_DIM)
    grad_heads = grad_att.reshape(row_count, HEADS, HEAD_DIM)
    scores = (
        jnp.einsum("qhd,khd->hqk", query_heads, key_heads, preferred_element_type=jnp.float32)
        * score_scale
    )
    allowed = (seg_query[:, None] == seg_all[None, :]) & (pad_all[None, :] == 1)
    prob_rows = jnp.where(allowed[None], jnp.exp(scores - log_total[..., None]), 0.0)
    grad_probs = jnp.einsum(
        "qhd,khd->hqk", grad_heads, value_heads, preferred_element_type=jnp.float32
    )
    grad_scores = (prob_rows * (grad_probs - row_delta[..., None])).astype(jnp.bfloat16)
    grad_query = (
        jnp.einsum("hqk,khd->qhd", grad_scores, key_heads, preferred_element_type=jnp.float32)
        * score_scale
    )
    grad_key = (
        jnp.einsum("hqk,qhd->khd", grad_scores, query_heads, preferred_element_type=jnp.float32)
        * score_scale
    )
    grad_value = jnp.einsum(
        "hqk,qhd->khd",
        prob_rows.astype(jnp.bfloat16),
        grad_heads,
        preferred_element_type=jnp.float32,
    )
    model_width = HEADS * HEAD_DIM
    return (
        grad_query.reshape(row_count, model_width),
        grad_key.reshape(seq_count, model_width),
        grad_value.reshape(seq_count, model_width),
    )


def layer_forward(layer_input, params, seg_query, pad_query, drop_flag):
    (
        qkv_weight,
        query_bias,
        value_bias,
        attn_weight,
        attn_bias,
        attn_gain,
        attn_shift,
        inner_weight,
        inner_bias,
        outer_weight,
        outer_bias,
        ffn_gain,
        ffn_shift,
    ) = params
    model_width = layer_input.shape[1]
    row_count = layer_input.shape[0]
    projected = matmul_low(layer_input, qkv_weight)
    query_low = (projected[:, :model_width] + query_bias).astype(jnp.bfloat16)
    key_local = projected[:, model_width : 2 * model_width].astype(jnp.bfloat16)
    value_local = (projected[:, 2 * model_width :] + value_bias).astype(jnp.bfloat16)
    query_heads = query_low.reshape(row_count, HEADS, HEAD_DIM)
    start_state = (
        jnp.full((HEADS, row_count), masked_score, jnp.float32),
        jnp.zeros((HEADS, row_count), jnp.float32),
        jnp.zeros((HEADS, row_count, HEAD_DIM), jnp.float32),
    )
    key_all, value_all, seg_all, pad_all = (
        lax.all_gather(key_local, "ctx", axis=0, tiled=True),
        lax.all_gather(value_local, "ctx", axis=0, tiled=True),
        lax.all_gather(seg_query, "ctx", axis=0, tiled=True),
        lax.all_gather(pad_query, "ctx", axis=0, tiled=True),
    )
    run_max, run_total, run_acc = attend_piece(
        query_heads, seg_query, start_state, (key_all, value_all, seg_all, pad_all)
    )
    gathered = (key_all, value_all, seg_all, pad_all)
    attended = (run_acc / run_total[..., None]).transpose(1, 0, 2).reshape(row_count, model_width)
    log_total = run_max + jnp.log(run_total)
    branch = matmul_low(attended.astype(jnp.bfloat16), attn_weight) + attn_bias
    sum_attn = layer_input.astype(jnp.float32) + branch
    normed, inverse = normalize(sum_attn)
    first_norm = normed * attn_gain + attn_shift
    inner_pre = matmul_low(first_norm.astype(jnp.bfloat16), inner_weight) + inner_bias
    active_low = jax.nn.gelu(inner_pre, approximate=False).astype(jnp.bfloat16)
    sum_ffn = first_norm + matmul_low(active_low, outer_weight) + outer_bias
    normed_two, inverse_two = normalize(sum_ffn)
    result = normed_two * ffn_gain + ffn_shift
    result = jnp.where(drop_flag > 0, layer_input.astype(jnp.float32), result)
    kept_items = (
        layer_input,
        query_low,
        key_local,
        value_local,
        attended,
        log_total,
        sum_attn,
        inner_pre,
        sum_ffn,
    ) + gathered
    return (result, kept_items)


def layer_backward(grad_out, kept_items, params, seg_query):
    (
        qkv_weight,
        query_bias,
        value_bias,
        attn_weight,
        attn_bias,
        attn_gain,
        attn_shift,
        inner_weight,
        inner_bias,
        outer_weight,
        outer_bias,
        ffn_gain,
        ffn_shift,
    ) = params
    (
        layer_input,
        query_low,
        key_local,
        value_local,
        attended,
        log_total,
        sum_attn,
        inner_pre,
        sum_ffn,
    ) = kept_items[:9]
    model_width = layer_input.shape[1]
    row_count = layer_input.shape[0]
    normed, inverse = normalize(sum_attn)
    first_norm = normed * attn_gain + attn_shift
    normed_two, inverse_two = normalize(sum_ffn)
    grad_ffn_gain = jnp.sum(grad_out * normed_two, axis=0)
    grad_ffn_shift = jnp.sum(grad_out, axis=0)
    grad_sum_ffn = norm_back(grad_out, normed_two, inverse_two, ffn_gain)
    grad_ffn_low = grad_sum_ffn.astype(jnp.bfloat16)
    active, gelu_pull = jax.vjp(partial(jax.nn.gelu, approximate=False), inner_pre)
    grad_outer_weight = left_product(active.astype(jnp.bfloat16), grad_ffn_low)
    grad_outer_bias = jnp.sum(grad_ffn_low.astype(jnp.float32), axis=0)
    grad_active = right_product(grad_ffn_low, outer_weight)
    grad_inner = gelu_pull(grad_active)[0].astype(jnp.bfloat16)
    grad_inner_weight = left_product(first_norm.astype(jnp.bfloat16), grad_inner)
    grad_inner_bias = jnp.sum(grad_inner.astype(jnp.float32), axis=0)
    grad_first = grad_sum_ffn + right_product(grad_inner, inner_weight)
    grad_attn_gain = jnp.sum(grad_first * normed, axis=0)
    grad_attn_shift = jnp.sum(grad_first, axis=0)
    grad_sum_attn = norm_back(grad_first, normed, inverse, attn_gain)
    grad_branch = grad_sum_attn.astype(jnp.bfloat16)
    grad_attn_weight = left_product(attended.astype(jnp.bfloat16), grad_branch)
    grad_attn_bias = jnp.sum(grad_branch.astype(jnp.float32), axis=0)
    grad_attended = right_product(grad_branch, attn_weight).astype(jnp.bfloat16)
    key_all, value_all, seg_all, pad_all = kept_items[9:]
    row_delta = jnp.sum(
        (grad_attended.astype(jnp.float32) * attended).reshape(row_count, HEADS, HEAD_DIM), axis=-1
    ).T
    grad_query, grad_key_all, grad_value_all = attention_back(
        query_low,
        key_all,
        value_all,
        seg_query,
        seg_all,
        pad_all,
        log_total,
        row_delta,
        grad_attended,
    )
    grad_key, grad_value = (
        lax.psum_scatter(
            grad_key_all.astype(jnp.bfloat16), "ctx", scatter_dimension=0, tiled=True
        ).astype(jnp.float32),
        lax.psum_scatter(
            grad_value_all.astype(jnp.bfloat16), "ctx", scatter_dimension=0, tiled=True
        ).astype(jnp.float32),
    )
    grad_qkv = jnp.concatenate([grad_query, grad_key, grad_value], axis=1).astype(jnp.bfloat16)
    grad_qkv_weight = left_product(layer_input, grad_qkv)
    grad_query_bias = jnp.sum(grad_qkv[:, :model_width].astype(jnp.float32), axis=0)
    grad_value_bias = jnp.sum(grad_qkv[:, 2 * model_width :].astype(jnp.float32), axis=0)
    grad_input = grad_sum_attn + right_product(grad_qkv, qkv_weight)
    layer_grads = (
        grad_qkv_weight,
        grad_query_bias,
        grad_value_bias,
        grad_attn_weight,
        grad_attn_bias,
        grad_attn_gain,
        grad_attn_shift,
        grad_inner_weight,
        grad_inner_bias,
        grad_outer_weight,
        grad_outer_bias,
        grad_ffn_gain,
        grad_ffn_shift,
    )
    return (layer_grads, grad_input)


def body(
    tokens,
    segment_ids,
    padding,
    dropped,
    qkv_weight,
    query_bias,
    value_bias,
    attn_weight,
    attn_bias,
    attn_gain,
    attn_shift,
    inner_weight,
    inner_bias,
    outer_weight,
    outer_bias,
    ffn_gain,
    ffn_shift,
    cotangent,
):
    micro_count = tokens.shape[0]
    section_index = lax.axis_index("section")
    half_width = tokens.shape[2] // lax.axis_size("section")
    params = tuple(
        (
            member[0]
            for member in (
                qkv_weight,
                query_bias,
                value_bias,
                attn_weight,
                attn_bias,
                attn_gain,
                attn_shift,
                inner_weight,
                inner_bias,
                outer_weight,
                outer_bias,
                ffn_gain,
                ffn_shift,
            )
        )
    )
    drop_row = dropped[0]
    incoming = jnp.zeros(tokens.shape[1:], jnp.bfloat16)
    saved_ticks = []
    encoded_rows = []
    for tick_index in range(micro_count + 1):
        micro_index = jnp.clip(tick_index - section_index, 0, micro_count - 1)
        own_input = lax.dynamic_index_in_dim(tokens, micro_index, 0, False)
        layer_input = jnp.where(section_index == 0, own_input, incoming)
        seg_query = lax.dynamic_index_in_dim(segment_ids, micro_index, 0, False)
        pad_query = lax.dynamic_index_in_dim(padding, micro_index, 0, False)
        drop_flag = lax.dynamic_index_in_dim(drop_row, micro_index, 0, False)
        layer_out, kept_items = layer_forward(layer_input, params, seg_query, pad_query, drop_flag)
        layer_low = layer_out.astype(jnp.bfloat16)
        received = shifted(layer_low, "section", 1)
        incoming = received
        if tick_index >= 1:
            encoded_rows.append(jnp.where(section_index == 0, received, layer_low))
        saved_ticks.append(kept_items)
    stacked = jax.tree.map(lambda *members: jnp.stack(members), *saved_ticks)
    grad_totals = tuple((jnp.zeros(member.shape, jnp.float32) for member in params))
    grad_incoming = jnp.zeros(tokens.shape[1:], jnp.bfloat16)
    input_rows = []
    for tick_index in range(micro_count + 1):
        raw_index = tick_index - 1 + section_index
        micro_index = jnp.clip(raw_index, 0, micro_count - 1)
        live_tick = ((raw_index >= 0) & (raw_index < micro_count)).astype(jnp.float32)
        forward_tick = jnp.clip(tick_index - 1 + 2 * section_index, 0, micro_count)
        kept_items = jax.tree.map(
            lambda member: lax.dynamic_index_in_dim(member, forward_tick, 0, False), stacked
        )
        own_cot = lax.dynamic_index_in_dim(cotangent, micro_index, 0, False)
        upstream = jnp.where(section_index == 1, own_cot, grad_incoming).astype(jnp.float32)
        seg_query = lax.dynamic_index_in_dim(segment_ids, micro_index, 0, False)
        pad_query = lax.dynamic_index_in_dim(padding, micro_index, 0, False)
        drop_flag = lax.dynamic_index_in_dim(drop_row, micro_index, 0, False)
        keep_scale = (drop_flag == 0).astype(jnp.float32) * live_tick
        layer_grads, grad_input = layer_backward(
            upstream * keep_scale, kept_items, params, seg_query
        )
        grad_totals = tuple((total + term for total, term in zip(grad_totals, layer_grads)))
        grad_input = grad_input + (drop_flag > 0).astype(jnp.float32) * upstream
        grad_low = grad_input.astype(jnp.bfloat16)
        received = shifted(grad_low, "section", 1)
        grad_incoming = received
        if tick_index >= 1:
            input_rows.append(jnp.where(section_index == 0, grad_low, received))
    reduced_once = (
        lax.psum_scatter(
            grad_totals[0][None].astype(jnp.bfloat16), "dp", scatter_dimension=1, tiled=True
        ).astype(jnp.float32),
        lax.psum_scatter(
            grad_totals[3][None].astype(jnp.bfloat16), "dp", scatter_dimension=1, tiled=True
        ).astype(jnp.float32),
        lax.psum_scatter(
            grad_totals[7][None].astype(jnp.bfloat16), "dp", scatter_dimension=1, tiled=True
        ).astype(jnp.float32),
        lax.psum_scatter(
            grad_totals[9][None].astype(jnp.bfloat16), "dp", scatter_dimension=1, tiled=True
        ).astype(jnp.float32),
    )
    matrix_grads = (
        lax.psum_scatter(
            reduced_once[0].astype(jnp.bfloat16), "ctx", scatter_dimension=2, tiled=True
        ).astype(jnp.float32),
        lax.psum_scatter(
            reduced_once[1].astype(jnp.bfloat16), "ctx", scatter_dimension=2, tiled=True
        ).astype(jnp.float32),
        lax.psum_scatter(
            reduced_once[2].astype(jnp.bfloat16), "ctx", scatter_dimension=2, tiled=True
        ).astype(jnp.float32),
        lax.psum_scatter(
            reduced_once[3].astype(jnp.bfloat16), "ctx", scatter_dimension=2, tiled=True
        ).astype(jnp.float32),
    )
    vector_grads = lax.psum(
        (
            grad_totals[1][None],
            grad_totals[2][None],
            grad_totals[4][None],
            grad_totals[5][None],
            grad_totals[6][None],
            grad_totals[8][None],
            grad_totals[10][None],
            grad_totals[11][None],
            grad_totals[12][None],
        ),
        ("dp", "ctx"),
    )
    encoded = lax.dynamic_slice_in_dim(
        jnp.stack(encoded_rows), section_index * half_width, half_width, 2
    )
    tokens_grad = lax.dynamic_slice_in_dim(
        jnp.stack(input_rows), section_index * half_width, half_width, 2
    )
    return (
        encoded,
        tokens_grad,
        matrix_grads[0],
        vector_grads[0],
        vector_grads[1],
        matrix_grads[1],
        vector_grads[2],
        vector_grads[3],
        vector_grads[4],
        matrix_grads[2],
        vector_grads[5],
        matrix_grads[3],
        vector_grads[6],
        vector_grads[7],
        vector_grads[8],
    )


def dot_plain(left, right):
    return lax.dot_general(left, right, (((1,), (0,)), ((), ())), preferred_element_type=jnp.float32)


def dot_flipped(left, right):
    return lax.dot_general(left, right, (((1,), (1,)), ((), ())), preferred_element_type=jnp.float32)


def dot_leading(left, right):
    return lax.dot_general(left, right, (((0,), (0,)), ((), ())), preferred_element_type=jnp.float32)


def gelu_parts(x):
    below = 0.5 * (1.0 + lax.erf(x * 0.7071067811865476))
    density = jnp.exp(-0.5 * x * x) * 0.3989422804014327
    return (x * below, below + x * density)


def rows_of(index, size):
    return pl.ds(pl.multiple_of(index * size, size), size)


def piece_rows(ctx, at, count, n_pieces):
    return pl.ds(0, count) if n_pieces == 1 else rows_of(ctx ^ at, count)


def head_lanes(shape, which):
    lane = lax.broadcasted_iota(jnp.int32, shape, 1)
    return (lane < HEAD_DIM) if which == 0 else (lane >= HEAD_DIM)


def copy_list(pairs, sems, first=0):
    copies = [pltpu.make_async_copy(src, dst, sems.at[first + at]) for at, (src, dst) in enumerate(pairs)]
    for copy in copies:
        copy.start()
    return copies


def wait_all(copies):
    for copy in copies:
        copy.wait()


low, full = jnp.bfloat16, jnp.float32


def kernel_call(body, operands, outs, scratch, mib, aliases=None):
    spaces = {"s": pltpu.SMEM, "v": pltpu.VMEM, "h": pltpu.HBM, "c": pltpu.VMEM}
    members = []
    for space, array in operands:
        if space in "vh":
            array = pltpu.with_memory_space_constraint(array, spaces[space])
        members.append(array)
    return pl.pallas_call(
        body,
        out_shape=[spaces[space](shape, kind) for space, shape, kind in outs],
        in_specs=[pl.BlockSpec(memory_space=spaces[space]) for space, _ in operands],
        out_specs=[pl.BlockSpec(memory_space=spaces[space]) for space, _, _ in outs],
        scratch_shapes=scratch,
        input_output_aliases=aliases or {},
        compiler_params=pltpu.CompilerParams(vmem_limit_bytes=mib * 2**20),
    )(*members)


class Outgoing:
    def __init__(self, sems):
        self.sems, self.copies = sems, []

    def send(self, src, dst):
        copy = pltpu.make_async_copy(src, dst, self.sems.at[len(self.copies)])
        copy.start()
        self.copies.append(copy)

    def finish(self):
        wait_all(self.copies)


def scratch_like(shapes):
    return [pltpu.VMEM(shape, kind) for _, shape, kind in shapes]


def in_pairs(count, step):
    def both_steps(at, carry):
        for which in range(UNROLL):
            step(UNROLL * at + which)
        return carry

    lax.fori_loop(0, count // UNROLL, both_steps, 0)


UNROLL = 2


def forward_kernel(active, n_pieces, n_cot, n_alias, scal, qkv_bias_ref, qkv_scale_ref, vec_ref, inner_bias_ref, *refs):
    pieces, refs = refs[:n_pieces], refs[n_pieces:]
    cot_pieces, refs = refs[:n_cot], refs[n_cot:]
    weights_h, refs = refs[:4], refs[4 + n_alias :]
    n_outs = 17 if n_cot else 12
    outs_h, outs, (wqkv, wattn, win, wout, first, code_rows, ids, in_sems, out_sems) = (
        refs[:n_outs],
        refs[n_outs : 2 * n_outs],
        refs[2 * n_outs :],
    )
    u, qkv, att, lse, n1, r1, dg, n2, r2, first_low, res, mask = outs[:12]
    top = outs[12:]
    size, width = u.shape

    @pl.when(scal[0] == active)
    def _():
        loads = [
            pltpu.make_async_copy(src, dst, in_sems.at[at])
            for at, (src, dst) in enumerate(zip(weights_h, (wqkv, wattn, win, wout)))
        ]
        loads[0].start()
        out = Outgoing(out_sems)

        def save(*places):
            for place in places:
                out.send(outs[place], outs_h[place])

        count = size // 4
        if n_pieces == 1:
            u[...] = pieces[0][:size]
            ids[...] = pieces[0][size:, :size].astype(full)[:8]
        else:
            for at, piece in enumerate(pieces):
                place = rows_of(scal[1] ^ at, count)
                u[place, :] = piece[:count]
                ids[:, place] = piece[count:, :count].astype(full)[:8]
        for at in range(4):
            place = slice(at * count, (at + 1) * count)
            code_rows[place, :] = jnp.broadcast_to(ids[1:2, place], (count, count)).T
        mask[...] = jnp.where(code_rows[:, 0:1] == ids[0:1, :], 0.0, masked_score)
        loads[0].wait()
        loads[1].start()
        loads[2].start()
        save(0, 11)
        value = dot_plain(u[...], wqkv[...]) + qkv_bias_ref[...]
        qkv[...] = (value * qkv_scale_ref[...]).astype(low)
        save(1)
        def heads(pair):
            query, key, value = (qkv[:, rows_of(pair + part * (width // 128), 128)] for part in range(3))
            sides = []
            for which in range(2):
                key_own = jnp.where(head_lanes(key.shape, which), key, jnp.zeros_like(key))
                scores = dot_flipped(key_own, query) + mask[...]
                top_score = jnp.max(scores, axis=0, keepdims=True)
                weights = jnp.exp(scores - top_score)
                total = jnp.sum(weights, axis=0, keepdims=True)
                head = 2 * pair + which
                lse[pl.ds(head, 1), :] = top_score + jnp.log(total)
                sides.append(dot_leading((weights * (1.0 / total)).astype(low), value))
            att[:, rows_of(pair, 128)] = jnp.where(head_lanes((size, 128), 0), sides[0], sides[1]).astype(low)

        in_pairs(width // 128, heads)
        save(2, 3)
        loads[1].wait()
        value = dot_plain(att[...], wattn[...]) + u[...].astype(full) + vec_ref[0:1, :]
        normed, inverse = normalize(value)
        n1[...] = normed
        r1[...] = jnp.broadcast_to(inverse, r1.shape)
        value = normed * vec_ref[1:2, :] + vec_ref[2:3, :]
        first[...] = value + vec_ref[3:4, :]
        first_low[...] = value.astype(low)
        save(9, 4, 5)
        loads[2].wait()
        loads[3].start()
        inner = dot_plain(first_low[...], win[...]) + inner_bias_ref[...]
        active_value, slope = gelu_parts(inner)
        dg[...] = slope.astype(low)
        save(6)
        loads[3].wait()
        normed, inverse = normalize(first[...] + dot_plain(active_value.astype(low), wout[...]))
        n2[...] = normed
        r2[...] = jnp.broadcast_to(inverse, r2.shape)
        value = normed * vec_ref[4:5, :] + vec_ref[5:6, :]
        res[:size] = jnp.where(scal[2] > 0, u[...], value.astype(low))
        res[size:, :size] = jnp.concatenate([ids[...], jnp.zeros_like(ids)], axis=0).astype(low)
        save(10, 7, 8)
        if n_cot:
            for at, piece in enumerate(cot_pieces):
                top[0][rows_of(scal[1] ^ at, count), :] = piece[...]
            top_of_backward(scal, vec_ref, n2, r2, *top[:4])
            top[4][0] = first_low[...]
            top[4][1] = top[1][...]
            save(16, 13, 14, 12, 15)
        out.finish()


def top_of_backward(scal, vec_ref, n2, r2, inc, dffn, dsum, vec):
    grad = inc[...].astype(full) * jnp.where(scal[2] > 0, 0.0, 1.0)
    normed = n2[...]
    value = norm_back(grad, normed, r2[:, :1], vec_ref[4:5, :])
    dsum[...] = value
    rounded = value.astype(low)
    dffn[...] = rounded
    vec[0:1, :] = column_sum(rounded.astype(full))
    vec[1:2, :] = column_sum(grad * normed)
    vec[2:3, :] = column_sum(grad)


def top_shapes(size, width):
    return [
        ("h", (size, width), low),
        ("h", (size, width), low),
        ("h", (size, width), full),
        ("h", (8, width), full),
    ]


def run_forward(active, scal, small, pieces, cot_pieces, held, earlier, after):
    width, hidden = held[2].shape
    size = len(pieces) * (pieces[0].shape[0] - 16)
    outs = [
        ("h", (size, width), low),
        ("h", (size, 3 * width), low),
        ("h", (size, width), low),
        ("h", (16, size), full),
        ("h", (size, width), full),
        ("h", (size, 128), full),
        ("h", (size, hidden), low),
        ("h", (size, width), full),
        ("h", (size, 128), full),
        ("h", (size, width), low),
        ("h", (size + 16, width), low),
        ("h", (size, size), full),
    ]
    if cot_pieces:
        outs += top_shapes(size, width) + [("h", (2, size, width), low)]
    operands = [("s", scal)] + [("c", member) for member in small]
    operands += [("c", member) for member in (*pieces, *cot_pieces)] + [("h", member) for member in held]
    at_alias = len(operands)
    operands += [(out[0], member) for out, member in zip(outs, earlier)] + [("c", member) for member in after]
    return kernel_call(
        partial(forward_kernel, active, len(pieces), len(cot_pieces), len(earlier) + len(after)),
        operands,
        outs,
        scratch_like(outs)
        + [pltpu.VMEM(member.shape, low) for member in held]
        + [
            pltpu.VMEM((size, width), full),
            pltpu.VMEM((size, size // 4), full),
            pltpu.VMEM((8, size), full),
            pltpu.SemaphoreType.DMA((4,)),
            pltpu.SemaphoreType.DMA((len(outs),)),
        ],
        48,
        {at_alias + i: i for i in range(len(earlier))},
    )


def column_sum(value):
    return jnp.sum(value, axis=0, keepdims=True)


def top_kernel(active, n_alias, n_after, scal, vec_ref, incoming, n2_h, r2_h, *refs):
    refs = refs[n_alias + n_after :]
    outs_h, outs, (n2, r2, in_sems, out_sems) = refs[:4], refs[4:8], refs[8:]

    @pl.when(scal[0] == active)
    def _():
        loads = copy_list([(n2_h, n2), (r2_h, r2)], in_sems)
        outs[0][...] = incoming[:, : outs[0].shape[1]]
        wait_all(loads)
        top_of_backward(scal, vec_ref, n2, r2, *outs)
        wait_all(copy_list(list(zip(outs, outs_h)), out_sems))


def run_top(active, scal, vecs, incoming, n2, r2, earlier, after):
    size, width = n2.shape
    outs = top_shapes(size, width)
    operands = [("s", scal), ("c", vecs), ("c", incoming)] + [("h", member) for member in (n2, r2)]
    at_alias = len(operands)
    operands += [(out[0], member) for out, member in zip(outs, earlier)] + list(after)
    return kernel_call(
        partial(top_kernel, active, len(earlier), len(after)),
        operands,
        outs,
        scratch_like(outs)
        + [
            pltpu.VMEM(n2.shape, full),
            pltpu.VMEM(r2.shape, full),
            pltpu.SemaphoreType.DMA((2,)),
            pltpu.SemaphoreType.DMA((4,)),
        ],
        16,
        {at_alias + i: i for i in range(len(earlier))},
    )


def chain_kernel(active, n_alias, n_after, scal, vec_ref, *refs):
    held_h, res_h, refs = refs[:13], refs[13], refs[14 + n_alias + n_after :]
    outs_h, outs, held, (dinner, datt, first, in_sems, out_sems) = refs[:4], refs[4:8], refs[8:21], refs[21:]
    inc, dffn, dsum, dg, n1, r1, qkv, lse, wqkv, wattn, win, wout, mask = held
    dqkv, dbranch, vec, din = outs
    size, width = inc.shape
    hidden = win.shape[1]

    @pl.when(scal[0] == active)
    def _():
        chunks = hidden // width
        cuts = [slice(at * width, (at + 1) * width) for at in range(chunks)]
        order = [(held_h[1], dffn)]
        for cut in cuts:
            order += [(held_h[11].at[cut, :], wout.at[cut, :]), (held_h[3].at[:, cut], dg.at[:, cut])]
        order += [(held_h[at], held[at]) for at in (10, 2, 4, 5, 9, 6, 7, 12, 8, 0)]
        order += [(res_h.at[pl.ds(0, size), pl.ds(0, width // 2)], din.at[:, pl.ds(width, width // 2)])]
        loads = [pltpu.make_async_copy(src, dst, in_sems.at[at]) for at, (src, dst) in enumerate(order)]

        def begin(first_copy, last_copy):
            for copy in loads[first_copy:last_copy]:
                copy.start()

        begin(0, 5)
        out = Outgoing(out_sems)
        for at, cut in enumerate(cuts):
            wait_all(loads[: 3] if at == 0 else loads[2 * at + 1 : 2 * at + 3])
            begin(2 * at + 5, 2 * at + 7)
            value = (dot_flipped(dffn[...], wout[cut, :]) * dg[:, cut].astype(full)).astype(low)
            dinner[:, cut] = value
            vec[8 + at : 9 + at, :] = column_sum(value.astype(full))
        begin(2 * chunks + 5, len(loads))
        loads = loads[2 * chunks + 1 :]
        wait_all(loads[:4])
        grad = dot_flipped(dinner[...], win[...]) + dsum[...]
        normed = n1[...]
        value = norm_back(grad, normed, r1[:, :1], vec_ref[1:2, :])
        first[...] = value
        rounded = value.astype(low)
        dbranch[...] = rounded
        vec[2:3, :] = column_sum(rounded.astype(full))
        vec[3:4, :] = column_sum(grad * normed)
        vec[4:5, :] = column_sum(grad)
        out.send(dbranch, outs_h[1])
        loads[4].wait()
        datt[...] = dot_flipped(dbranch[...], wattn[...]).astype(low)
        wait_all(loads[5:8])
        def heads(pair):
            cols = [rows_of(pair + part * (width // 128), 128) for part in range(3)]
            query, key, value = (qkv[:, col] for col in cols)
            grad = datt[:, cols[0]]
            parts = []
            for which in range(2):
                own = head_lanes(key.shape, which)
                key_own = jnp.where(own, key, jnp.zeros_like(key))
                value_own = jnp.where(own, value, jnp.zeros_like(value))
                head = 2 * pair + which
                probs = jnp.exp(dot_flipped(key_own, query) + mask[...] - lse[pl.ds(head, 1), :])
                dprobs = dot_flipped(value_own, grad)
                delta = column_sum(probs * dprobs)
                dscores = (probs * (dprobs - delta)).astype(low)
                parts.append(
                    (dot_leading(dscores, key), dot_plain(dscores, query), dot_plain(probs.astype(low), grad))
                )
            low_lanes = head_lanes((size, 128), 0)
            dquery, dkey, dvalue = (jnp.where(low_lanes, one, two) for one, two in zip(*parts))
            dquery = (dquery * HEAD_DIM ** (-0.5)).astype(low)
            dvalue = dvalue.astype(low)
            dqkv[:, cols[0]] = dquery
            dqkv[:, cols[1]] = dkey.astype(low)
            dqkv[:, cols[2]] = dvalue
            vec[0:1, cols[0]] = column_sum(dquery.astype(full))
            vec[1:2, cols[0]] = column_sum(dvalue.astype(full))

        in_pairs(width // 128, heads)
        out.send(dqkv, outs_h[0])
        out.send(vec, outs_h[2])
        wait_all(loads[8:])
        value = first[...] + dot_flipped(dqkv[...], wqkv[...])
        din[:, :width] = jnp.where(scal[2] > 0, inc[...], value.astype(low))
        out.send(din, outs_h[3])
        out.finish()


def run_chain(active, scal, vecs, top, kept, held, earlier, after):
    u, qkv, att, lse, n1, r1, dg = kept[:7]
    inc, dffn, dsum = top[:3]
    size, width = u.shape
    hidden = dg.shape[1]
    outs = [
        ("h", (size, 3 * width), low),
        ("h", (size, width), low),
        ("h", (16, width), full),
        ("h", (size, 3 * width // 2), low),
    ]
    members = (inc, dffn, dsum, dg, n1, r1, qkv, lse, *held, kept[11])
    operands = [("s", scal), ("c", vecs)] + [("h", member) for member in (*members, kept[10])]
    at_alias = len(operands)
    operands += [(out[0], member) for out, member in zip(outs, earlier)]
    operands += list(after)
    return kernel_call(
        partial(chain_kernel, active, len(earlier), len(after)),
        operands,
        outs,
        scratch_like(outs)
        + [pltpu.VMEM(member.shape, member.dtype) for member in members]
        + [
            pltpu.VMEM((size, hidden), low),
            pltpu.VMEM((size, width), low),
            pltpu.VMEM((size, width), full),
            pltpu.SemaphoreType.DMA((2 * (hidden // width) + 12,)),
            pltpu.SemaphoreType.DMA((4,)),
        ],
        48,
        {at_alias + i: i for i in range(len(earlier))},
    )


def split_high(value):
    high = value.astype(low)
    return high, (value - high.astype(full)).astype(low)


def wide_pair(value, rows):
    pair = jnp.concatenate(split_high(value), axis=1)
    return jnp.concatenate([pair, jnp.zeros((rows - pair.shape[0], pair.shape[1]), low)], axis=0)


def joined(high, rest):
    return high.astype(full) + rest.astype(full)


def attn_grad_kernel(n_after, scal, top_vec, chain_vec, *refs):
    ins_h, refs = refs[:4], refs[4 + n_after :]
    send_a, keep_a, send_b, keep_b, vec = refs[:5]
    (u, att, dqkv, dbranch), out, pair, in_sems, sems = refs[5:9], *refs[9:]
    width = u.shape[1]
    dp = scal[3]
    bit_y, bit_x = dp // 2, dp % 2
    left, right = pl.ds(0, 2 * width), pl.ds(2 * width, 2 * width)
    each = width // 4
    loads = copy_list([(ins_h[at], (u, att, dqkv, dbranch)[at]) for at in (0, 2, 1, 3)], in_sems)
    sent = Outgoing(sems)
    value = jnp.concatenate([top_vec[...], chain_vec[...]], axis=0)
    vec[...] = value
    pair[...] = wide_pair(value, VEC_ROWS)
    sent.send(pair, send_a.at[pl.ds(2 * each, VEC_ROWS)])
    wait_all(loads[:2])
    flipped = u[...].T
    out[:, : 2 * width] = dot_plain(flipped, dqkv[:, : 2 * width]).astype(low)
    for at in range(2):
        sent.send(out.at[rows_of(2 * at + 1 - bit_x, each), left], send_a.at[pl.ds(at * each, each)])
        sent.send(out.at[rows_of(2 * at + bit_x, each), left], keep_a.at[at])
    out[:, 2 * width : 3 * width] = dot_plain(flipped, dqkv[:, 2 * width :]).astype(low)
    wait_all(loads[2:])
    out[:, 3 * width :] = dot_leading(att[...], dbranch[...]).astype(low)
    for at in range(2):
        sent.send(out.at[rows_of(2 * (1 - bit_y) + at, each), right], send_b.at[at])
        sent.send(out.at[rows_of(2 * bit_y + at, each), right], keep_b.at[at])
    sent.finish()


VEC_ROWS = 32


def run_attn_grad(scal, top_vec, chain_vec, u, att, dqkv, dbranch, after):
    width = u.shape[1]
    each = width // 4
    members = (u, att, dqkv, dbranch)
    half_shape = ("h", (2, each, 2 * width), low)
    return kernel_call(
        partial(attn_grad_kernel, len(after)),
        [("s", scal), ("c", top_vec), ("c", chain_vec)] + [("h", member) for member in members] + list(after),
        [("h", (2 * each + VEC_ROWS, 2 * width), low)] + [half_shape] * 3 + [("c", (24, width), full)],
        [pltpu.VMEM(member.shape, low) for member in members]
        + [
            pltpu.VMEM((width, 4 * width), low),
            pltpu.VMEM((VEC_ROWS, 2 * width), low),
            pltpu.SemaphoreType.DMA((4,)),
            pltpu.SemaphoreType.DMA((9,)),
        ],
        24,
    )


def ffn_grad_kernel(n_after, scal, inner_bias_ref, win_h, wout_h, first_h, dffn_h, *refs):
    from_one, firsts, dffns = refs[:3], refs[3:6], refs[6:9]
    send, keep, first, dffn, active, dinner, win, wout, out, sems = refs[9 + n_after :]
    size, width = dffn_h.shape
    own = rows_of(scal[3], width)
    loads = copy_list(
        [
            (first_h, first.at[:size]),
            (win_h.at[:, own], win),
            (dffn_h, dffn.at[:size]),
            (wout_h.at[own, :], wout),
        ],
        sems,
    )
    is_zero = scal[0] == 0
    for at in range(4):
        rows = slice(at * size, (at + 1) * size)
        if at == 0:
            wait_all(loads)
            value, grad = first[rows], dffn[rows]
        else:
            value = jnp.where(is_zero, firsts[at - 1][...], from_one[at - 1][0])
            grad = jnp.where(is_zero, dffns[at - 1][...], from_one[at - 1][1])
            first[rows] = value
            dffn[rows] = grad
        inner = dot_plain(value, win[...]) + inner_bias_ref[:, own]
        active_value, slope = gelu_parts(inner)
        active[rows] = active_value.astype(low)
        dinner[rows] = (dot_flipped(grad, wout[...]) * slope).astype(low)
    each = width // 4
    for half, (left, right) in enumerate(((first, dinner), (dffn, active))):
        part = dot_leading(left[...], right[...]).astype(low)
        for block in range(4):
            out[block, each * half : each * (half + 1)] = part[each * block : each * (block + 1)]
    bit = scal[1] % 2
    wait_all(
        copy_list(
            [(out.at[2 * at + 1 - bit], send.at[at]) for at in range(2)]
            + [(out.at[2 * at + bit], keep.at[at]) for at in range(2)],
            sems,
        )
    )


def run_ffn_grad(scal, inner_bias, win, wout, first_own, dffn_own, from_one, firsts, dffns, after):
    size, width = dffn_own.shape
    return kernel_call(
        partial(ffn_grad_kernel, len(after)),
        [("s", scal), ("c", inner_bias)]
        + [("h", member) for member in (win, wout, first_own, dffn_own)]
        + [("c", member) for member in (*from_one, *firsts, *dffns)]
        + list(after),
        [("h", (2, width // 2, width), low)] * 2,
        [pltpu.VMEM((4 * size, width), low) for _ in range(4)]
        + [pltpu.VMEM((width, width), low), pltpu.VMEM((width, width), low)]
        + [pltpu.VMEM((4, width // 2, width), low), pltpu.SemaphoreType.DMA((4,))],
        32,
    )


def merge_kernel(scal, got_a, keep_a, got_b, keep_b, vec, send_a, left_a, send_b, left_b, vec_out):
    bit_y, bit_x = scal[3] // 2, scal[3] % 2
    each, width = keep_a.shape[1], vec.shape[1]
    send_a[:each] = added(got_a[rows_of(1 - bit_y, each)], keep_a[1 - bit_y])
    left_a[...] = added(got_a[rows_of(bit_y, each)], keep_a[bit_y])
    send_b[...] = added(got_b[1 - bit_x], keep_b[1 - bit_x])
    left_b[...] = added(got_b[bit_x], keep_b[bit_x])
    pair = got_a[2 * each :]
    value = vec[...] + joined(pair[:24, :width], pair[:24, width:])
    vec_out[...] = value
    send_a[each:] = wide_pair(value, VEC_ROWS)


def turn_kernel(scal, got_a, keep_a, got_b, keep_b, vec, send, keep, vec_out, rows, blocks):
    each, cut = keep_a.shape
    rows[:, :cut] = added(got_a[:each], keep_a[...])
    rows[:, cut:] = added(got_b[...], keep_b[...])
    width = cut // 2
    wide, narrow = 3 * width // 4, width // 4
    for at in range(4):
        blocks[at, :, :wide] = rows[:, wide * at : wide * (at + 1)]
        blocks[at, :, wide:] = rows[:, 3 * width + narrow * at : 3 * width + narrow * (at + 1)]
    bit = scal[1] % 2
    for at in range(2):
        send[at * each : (at + 1) * each] = blocks[2 * at + 1 - bit]
        keep[at] = blocks[2 * at + bit]
    pair = got_a[each:]
    value = vec[...] + joined(pair[:24, :width], pair[:24, width:])
    vec_out[...] = value
    send[2 * each :] = jnp.concatenate(split_high(value), axis=0)


def last_kernel(scal, got, keep, vec, send, left, vec_out):
    bit = scal[1] // 2
    each = keep.shape[1]
    send[:each] = added(got[rows_of(1 - bit, each)], keep[1 - bit])
    left[...] = added(got[rows_of(bit, each)], keep[bit])
    pair = got[2 * each :]
    value = vec[...] + joined(pair[:24], pair[24:])
    vec_out[...] = value
    send[each:] = jnp.concatenate(split_high(value), axis=0)


def end_kernel(scal, got, keep, vec, qkv_out, attn_out, vec_out):
    each = keep.shape[0]
    value = got[:each].astype(full) + keep[...].astype(full)
    qkv_out[...] = value[:, : 3 * each]
    attn_out[...] = value[:, 3 * each :]
    pair = got[each:]
    vec_out[...] = vec[...] + joined(pair[:24], pair[24:])


def half_kernel(scal, got, keep, send, left):
    bit = scal[1] // 2
    send[...] = added(got[1 - bit], keep[1 - bit])
    left[...] = added(got[bit], keep[bit])


def swapped(x, axis, by):
    return lax.ppermute(x, axis, [(i, i ^ by) for i in range(lax.axis_size(axis))])


def swapped_in(section, x, axis, by):
    length = lax.axis_size(axis)
    pairs = [(section * length + i, section * length + (i ^ by)) for i in range(length)]
    return lax.ppermute(x, ("section", axis), pairs)


def pick(x, at, dim=0):
    return lax.dynamic_index_in_dim(x, at, dim, False)


def added(one, two):
    return (one.astype(full) + two.astype(full)).astype(low)


def spread(row_half, ctx):
    length = lax.axis_size("ctx")
    size, width = row_half.shape
    parts = row_half.reshape(length, size // length, width)
    out = jnp.zeros(parts.shape, parts.dtype)
    out = lax.dynamic_update_index_in_dim(out, pick(parts, ctx), ctx, 0)
    for k in range(1, length):
        out = lax.dynamic_update_index_in_dim(out, swapped(pick(parts, ctx ^ k), "ctx", k), ctx ^ k, 0)
    return out


def to_section(x, section):
    return lax.ppermute(x, "section", [(1 - section, section)])


def merged(body, scal, operands, outs, scratch=()):
    return kernel_call(
        body,
        [("s", scal)] + [("c", member) for member in operands],
        [("c", shape, kind) for shape, kind in outs],
        list(scratch),
        16,
    )


def row_body(
    tokens,
    segment_ids,
    padding,
    dropped,
    qkv_weight,
    query_bias,
    value_bias,
    attn_weight,
    attn_bias,
    attn_gain,
    attn_shift,
    inner_weight,
    inner_bias,
    outer_weight,
    outer_bias,
    ffn_gain,
    ffn_shift,
    cotangent,
):
    width = tokens.shape[2]
    half, each = width // 2, width // 4
    count = tokens.shape[1]
    section, dp, ctx = (lax.axis_index(name) for name in ("section", "dp", "ctx"))
    weights = (qkv_weight[0], attn_weight[0], inner_weight[0], outer_weight[0])
    vecs = jnp.concatenate(
        [attn_bias, attn_gain, attn_shift, outer_bias, ffn_gain, ffn_shift, query_bias, value_bias]
    )
    qkv_bias = jnp.concatenate([query_bias, jnp.zeros_like(query_bias), value_bias], axis=1)
    qkv_scale = jnp.concatenate(
        [jnp.full((1, width), HEAD_DIM ** (-0.5), jnp.float32), jnp.ones((1, 2 * width), jnp.float32)], axis=1
    )
    small = (qkv_bias, qkv_scale, vecs, inner_bias)
    scal = jnp.stack([section, ctx, pick(dropped[0], ctx), dp]).astype(jnp.int32)

    ids = jnp.stack([segment_ids, jnp.where(padding == 1, segment_ids, -1)], axis=1).astype(low)
    ids = jnp.pad(ids, ((0, 0), (0, 14), (0, width - count)))
    sent = jnp.concatenate([tokens, ids], axis=1)
    own_tokens = [pick(sent, ctx)] + [swapped_in(0, pick(sent, ctx ^ k), "ctx", k) for k in range(1, 4)]
    held = weights
    own_cot = [pick(cotangent, ctx)] + [swapped_in(1, pick(cotangent, ctx ^ k), "ctx", k) for k in range(1, 4)]

    kept = run_forward(0, scal, small, own_tokens, [], held, [], [])
    middle = lax.ppermute(kept[10], "section", [(0, 1)])
    firsts = [swapped_in(0, kept[9], "dp", k) for k in range(1, 4)]
    made = run_forward(1, scal, small, [middle], own_cot, held, kept, firsts)
    kept, top, both = made[:12], made[12:16], made[16]
    from_one = [swapped_in(1, both, "dp", k) for k in range(1, 4)]
    chain = run_chain(1, scal, vecs, top, kept, held, [], [])
    incoming = to_section(chain[3], 0)
    top = run_top(0, scal, vecs, incoming, kept[7], kept[8], top, [("c", member) for member in from_one])
    dffns = [swapped_in(0, top[1], "dp", k) for k in range(1, 4)]
    chain = run_chain(0, scal, vecs, top, kept, held, chain, [])
    dqkv, dbranch, chain_vec, d_input = chain
    encoded_other = incoming[:, width:]
    result = kept[10][: 4 * count]
    grad_other = to_section(d_input[:, half:width], 1)

    send_a, keep_a, send_b, keep_b, vec = run_attn_grad(
        scal, top[3], chain_vec, kept[0], kept[2], dqkv, dbranch, []
    )
    got_a, got_b = swapped(send_a, "dp", 1), swapped(send_b, "dp", 2)
    send, keep = run_ffn_grad(
        scal, inner_bias, held[2], held[3], kept[9], top[1], from_one, firsts, dffns, [("h", keep_b)]
    )
    got = swapped(send, "ctx", 1)

    wide, block, flat = (each, 2 * width), (each, width), ((24, width), full)
    ffn_send, ffn_keep = merged(half_kernel, scal, (got, keep), [(keep.shape[1:], low)] * 2)
    ffn_got = swapped(ffn_send, "ctx", 2)
    send_a, keep_a, send_b, keep_b, vec = merged(
        merge_kernel,
        scal,
        (got_a, keep_a, got_b, keep_b, vec),
        [((each + VEC_ROWS, 2 * width), low), (wide, low), (wide, low), (wide, low), flat],
    )
    got_a, got_b = swapped(send_a, "dp", 2), swapped(send_b, "dp", 1)
    send, keep, vec = merged(
        turn_kernel,
        scal,
        (got_a, keep_a, got_b, keep_b, vec),
        [((2 * each + 48, width), low), ((2, each, width), low), flat],
        [pltpu.VMEM((each, 4 * width), low), pltpu.VMEM((4, each, width), low)],
    )
    got = swapped(send, "ctx", 1)
    send, keep, vec = merged(last_kernel, scal, (got, keep, vec), [((each + 48, width), low), (block, low), flat])
    encoded_other, grad_other, keep = lax.optimization_barrier((encoded_other, grad_other, keep))
    pair = jnp.where(
        section == 0,
        jnp.concatenate([encoded_other, d_input[:, :half]], axis=1),
        jnp.concatenate([result[:, half:], grad_other], axis=1),
    )
    pair = spread(pair, ctx)
    encoded, tokens_grad = pair[..., :half], pair[..., half:]
    got = swapped(send, "ctx", 2)
    qkv_grad, attn_grad, vec = merged(
        end_kernel, scal, (got, keep, vec), [((each, 3 * each), full), ((each, each), full), flat]
    )
    ffn_rows = ffn_got.astype(full) + ffn_keep.astype(full)
    inner_grad = lax.ppermute(
        ffn_rows[:each].astype(low), ("dp", "ctx"), [(i * 4 + j, j * 4 + i) for i in range(4) for j in range(4)]
    ).astype(full)
    outer_grad = ffn_rows[each:].T
    return (
        encoded,
        tokens_grad,
        qkv_grad[None],
        vec[8:9],
        vec[9:10],
        attn_grad[None],
        vec[10:11],
        vec[11:12],
        vec[12:13],
        inner_grad[None],
        vec[16 : 16 + inner_bias.shape[1] // width].reshape(1, -1),
        outer_grad[None],
        vec[0:1],
        vec[1:2],
        vec[2:3],
    )


def solution(mesh):
    placed = (
        P("dp", "ctx", None),
        P("dp", "ctx"),
        P("dp", "ctx"),
        P("section", "dp"),
        P("section", None, None),
        P("section", None),
        P("section", None),
        P("section", None, None),
        P("section", None),
        P("section", None),
        P("section", None),
        P("section", None, None),
        P("section", None),
        P("section", None, None),
        P("section", None),
        P("section", None),
        P("section", None),
        P("dp", "ctx", None),
    )

    def dispatch(*members):
        rows = members[0].shape[0]
        same = rows == lax.axis_size("ctx") == lax.axis_size("dp") == 4
        return (row_body if same else body)(*members)

    return jax.shard_map(
        dispatch,
        mesh=mesh,
        in_specs=placed,
        out_specs=(
            P("dp", "ctx", "section"),
            P("dp", "ctx", "section"),
            P("section", "dp", "ctx"),
            P("section", None),
            P("section", None),
            P("section", "dp", "ctx"),
            P("section", None),
            P("section", None),
            P("section", None),
            P("section", "dp", "ctx"),
            P("section", None),
            P("section", "dp", "ctx"),
            P("section", None),
            P("section", None),
            P("section", None),
        ),
        check_vma=False,
    )
```

```python
from functools import partial

import jax
import jax.numpy as jnp
from jax import lax
from jax.experimental import pallas as pl
from jax.experimental.pallas import tpu as pltpu
from jax.sharding import PartitionSpec as P

HEADS = 12
HEAD_DIM = 64


norm_eps = 1e-05
masked_score = -1e30


def shifted(x, axis, by):
    length = lax.axis_size(axis)
    return lax.ppermute(x, axis, [(i, (i + by) % length) for i in range(length)])


def matmul_low(left, right):
    return jnp.dot(left, right, preferred_element_type=jnp.float32)


def left_product(left, right):
    return jnp.einsum("ti,to->io", left, right, preferred_element_type=jnp.float32)


def right_product(left, right):
    return jnp.einsum("to,io->ti", left, right, preferred_element_type=jnp.float32)


def normalize(values):
    mean_value = jnp.mean(values, axis=-1, keepdims=True)
    centered = values - mean_value
    variance = jnp.mean(centered * centered, axis=-1, keepdims=True)
    inverse = lax.rsqrt(variance + norm_eps)
    return (centered * inverse, inverse)


def norm_back(grad_out, normed, inverse, gain):
    scaled = grad_out * gain
    return inverse * (
        scaled
        - jnp.mean(scaled, axis=-1, keepdims=True)
        - normed * jnp.mean(scaled * normed, axis=-1, keepdims=True)
    )


def attend_piece(query_heads, seg_query, running, pieces):
    run_max, run_total, run_acc = running
    key_piece, value_piece, seg_piece, pad_piece = pieces
    count = key_piece.shape[0]
    key_heads = key_piece.reshape(count, HEADS, HEAD_DIM)
    value_heads = value_piece.reshape(count, HEADS, HEAD_DIM)
    scores = jnp.einsum(
        "qhd,khd->hqk", query_heads, key_heads, preferred_element_type=jnp.float32
    ) * HEAD_DIM ** (-0.5)
    allowed = (seg_query[:, None] == seg_piece[None, :]) & (pad_piece[None, :] == 1)
    scores = jnp.where(allowed[None], scores, masked_score)
    new_max = jnp.maximum(run_max, jnp.max(scores, axis=-1))
    weights = jnp.where(allowed[None], jnp.exp(scores - new_max[..., None]), 0.0)
    run_total = jnp.sum(weights, axis=-1)
    run_acc = jnp.einsum(
        "hqk,khd->hqd",
        weights.astype(jnp.bfloat16),
        value_heads,
        preferred_element_type=jnp.float32,
    )
    return (new_max, run_total, run_acc)


def attention_back(
    query_low, key_all, value_all, seg_query, seg_all, pad_all, log_total, row_delta, grad_att
):
    row_count = query_low.shape[0]
    seq_count = key_all.shape[0]
    score_scale = HEAD_DIM ** (-0.5)
    query_heads = query_low.reshape(row_count, HEADS, HEAD_DIM)
    key_heads = key_all.reshape(seq_count, HEADS, HEAD_DIM)
    value_heads = value_all.reshape(seq_count, HEADS, HEAD_DIM)
    grad_heads = grad_att.reshape(row_count, HEADS, HEAD_DIM)
    scores = (
        jnp.einsum("qhd,khd->hqk", query_heads, key_heads, preferred_element_type=jnp.float32)
        * score_scale
    )
    allowed = (seg_query[:, None] == seg_all[None, :]) & (pad_all[None, :] == 1)
    prob_rows = jnp.where(allowed[None], jnp.exp(scores - log_total[..., None]), 0.0)
    grad_probs = jnp.einsum(
        "qhd,khd->hqk", grad_heads, value_heads, preferred_element_type=jnp.float32
    )
    grad_scores = (prob_rows * (grad_probs - row_delta[..., None])).astype(jnp.bfloat16)
    grad_query = (
        jnp.einsum("hqk,khd->qhd", grad_scores, key_heads, preferred_element_type=jnp.float32)
        * score_scale
    )
    grad_key = (
        jnp.einsum("hqk,qhd->khd", grad_scores, query_heads, preferred_element_type=jnp.float32)
        * score_scale
    )
    grad_value = jnp.einsum(
        "hqk,qhd->khd",
        prob_rows.astype(jnp.bfloat16),
        grad_heads,
        preferred_element_type=jnp.float32,
    )
    model_width = HEADS * HEAD_DIM
    return (
        grad_query.reshape(row_count, model_width),
        grad_key.reshape(seq_count, model_width),
        grad_value.reshape(seq_count, model_width),
    )


def layer_forward(layer_input, params, seg_query, pad_query, drop_flag):
    (
        qkv_weight,
        query_bias,
        value_bias,
        attn_weight,
        attn_bias,
        attn_gain,
        attn_shift,
        inner_weight,
        inner_bias,
        outer_weight,
        outer_bias,
        ffn_gain,
        ffn_shift,
    ) = params
    model_width = layer_input.shape[1]
    row_count = layer_input.shape[0]
    projected = matmul_low(layer_input, qkv_weight)
    query_low = (projected[:, :model_width] + query_bias).astype(jnp.bfloat16)
    key_local = projected[:, model_width : 2 * model_width].astype(jnp.bfloat16)
    value_local = (projected[:, 2 * model_width :] + value_bias).astype(jnp.bfloat16)
    query_heads = query_low.reshape(row_count, HEADS, HEAD_DIM)
    start_state = (
        jnp.full((HEADS, row_count), masked_score, jnp.float32),
        jnp.zeros((HEADS, row_count), jnp.float32),
        jnp.zeros((HEADS, row_count, HEAD_DIM), jnp.float32),
    )
    key_all, value_all, seg_all, pad_all = (
        lax.all_gather(key_local, "ctx", axis=0, tiled=True),
        lax.all_gather(value_local, "ctx", axis=0, tiled=True),
        lax.all_gather(seg_query, "ctx", axis=0, tiled=True),
        lax.all_gather(pad_query, "ctx", axis=0, tiled=True),
    )
    run_max, run_total, run_acc = attend_piece(
        query_heads, seg_query, start_state, (key_all, value_all, seg_all, pad_all)
    )
    gathered = (key_all, value_all, seg_all, pad_all)
    attended = (run_acc / run_total[..., None]).transpose(1, 0, 2).reshape(row_count, model_width)
    log_total = run_max + jnp.log(run_total)
    branch = matmul_low(attended.astype(jnp.bfloat16), attn_weight) + attn_bias
    sum_attn = layer_input.astype(jnp.float32) + branch
    normed, inverse = normalize(sum_attn)
    first_norm = normed * attn_gain + attn_shift
    inner_pre = matmul_low(first_norm.astype(jnp.bfloat16), inner_weight) + inner_bias
    active_low = jax.nn.gelu(inner_pre, approximate=False).astype(jnp.bfloat16)
    sum_ffn = first_norm + matmul_low(active_low, outer_weight) + outer_bias
    normed_two, inverse_two = normalize(sum_ffn)
    result = normed_two * ffn_gain + ffn_shift
    result = jnp.where(drop_flag > 0, layer_input.astype(jnp.float32), result)
    kept_items = (
        layer_input,
        query_low,
        key_local,
        value_local,
        attended,
        log_total,
        sum_attn,
        inner_pre,
        sum_ffn,
    ) + gathered
    return (result, kept_items)


def layer_backward(grad_out, kept_items, params, seg_query):
    (
        qkv_weight,
        query_bias,
        value_bias,
        attn_weight,
        attn_bias,
        attn_gain,
        attn_shift,
        inner_weight,
        inner_bias,
        outer_weight,
        outer_bias,
        ffn_gain,
        ffn_shift,
    ) = params
    (
        layer_input,
        query_low,
        key_local,
        value_local,
        attended,
        log_total,
        sum_attn,
        inner_pre,
        sum_ffn,
    ) = kept_items[:9]
    model_width = layer_input.shape[1]
    row_count = layer_input.shape[0]
    normed, inverse = normalize(sum_attn)
    first_norm = normed * attn_gain + attn_shift
    normed_two, inverse_two = normalize(sum_ffn)
    grad_ffn_gain = jnp.sum(grad_out * normed_two, axis=0)
    grad_ffn_shift = jnp.sum(grad_out, axis=0)
    grad_sum_ffn = norm_back(grad_out, normed_two, inverse_two, ffn_gain)
    grad_ffn_low = grad_sum_ffn.astype(jnp.bfloat16)
    active, gelu_pull = jax.vjp(partial(jax.nn.gelu, approximate=False), inner_pre)
    grad_outer_weight = left_product(active.astype(jnp.bfloat16), grad_ffn_low)
    grad_outer_bias = jnp.sum(grad_ffn_low.astype(jnp.float32), axis=0)
    grad_active = right_product(grad_ffn_low, outer_weight)
    grad_inner = gelu_pull(grad_active)[0].astype(jnp.bfloat16)
    grad_inner_weight = left_product(first_norm.astype(jnp.bfloat16), grad_inner)
    grad_inner_bias = jnp.sum(grad_inner.astype(jnp.float32), axis=0)
    grad_first = grad_sum_ffn + right_product(grad_inner, inner_weight)
    grad_attn_gain = jnp.sum(grad_first * normed, axis=0)
    grad_attn_shift = jnp.sum(grad_first, axis=0)
    grad_sum_attn = norm_back(grad_first, normed, inverse, attn_gain)
    grad_branch = grad_sum_attn.astype(jnp.bfloat16)
    grad_attn_weight = left_product(attended.astype(jnp.bfloat16), grad_branch)
    grad_attn_bias = jnp.sum(grad_branch.astype(jnp.float32), axis=0)
    grad_attended = right_product(grad_branch, attn_weight).astype(jnp.bfloat16)
    key_all, value_all, seg_all, pad_all = kept_items[9:]
    row_delta = jnp.sum(
        (grad_attended.astype(jnp.float32) * attended).reshape(row_count, HEADS, HEAD_DIM), axis=-1
    ).T
    grad_query, grad_key_all, grad_value_all = attention_back(
        query_low,
        key_all,
        value_all,
        seg_query,
        seg_all,
        pad_all,
        log_total,
        row_delta,
        grad_attended,
    )
    grad_key, grad_value = (
        lax.psum_scatter(
            grad_key_all.astype(jnp.bfloat16), "ctx", scatter_dimension=0, tiled=True
        ).astype(jnp.float32),
        lax.psum_scatter(
            grad_value_all.astype(jnp.bfloat16), "ctx", scatter_dimension=0, tiled=True
        ).astype(jnp.float32),
    )
    grad_qkv = jnp.concatenate([grad_query, grad_key, grad_value], axis=1).astype(jnp.bfloat16)
    grad_qkv_weight = left_product(layer_input, grad_qkv)
    grad_query_bias = jnp.sum(grad_qkv[:, :model_width].astype(jnp.float32), axis=0)
    grad_value_bias = jnp.sum(grad_qkv[:, 2 * model_width :].astype(jnp.float32), axis=0)
    grad_input = grad_sum_attn + right_product(grad_qkv, qkv_weight)
    layer_grads = (
        grad_qkv_weight,
        grad_query_bias,
        grad_value_bias,
        grad_attn_weight,
        grad_attn_bias,
        grad_attn_gain,
        grad_attn_shift,
        grad_inner_weight,
        grad_inner_bias,
        grad_outer_weight,
        grad_outer_bias,
        grad_ffn_gain,
        grad_ffn_shift,
    )
    return (layer_grads, grad_input)


def body(
    tokens,
    segment_ids,
    padding,
    dropped,
    qkv_weight,
    query_bias,
    value_bias,
    attn_weight,
    attn_bias,
    attn_gain,
    attn_shift,
    inner_weight,
    inner_bias,
    outer_weight,
    outer_bias,
    ffn_gain,
    ffn_shift,
    cotangent,
):
    micro_count = tokens.shape[0]
    section_index = lax.axis_index("section")
    half_width = tokens.shape[2] // lax.axis_size("section")
    params = tuple(
        (
            member[0]
            for member in (
                qkv_weight,
                query_bias,
                value_bias,
                attn_weight,
                attn_bias,
                attn_gain,
                attn_shift,
                inner_weight,
                inner_bias,
                outer_weight,
                outer_bias,
                ffn_gain,
                ffn_shift,
            )
        )
    )
    drop_row = dropped[0]
    incoming = jnp.zeros(tokens.shape[1:], jnp.bfloat16)
    saved_ticks = []
    encoded_rows = []
    for tick_index in range(micro_count + 1):
        micro_index = jnp.clip(tick_index - section_index, 0, micro_count - 1)
        own_input = lax.dynamic_index_in_dim(tokens, micro_index, 0, False)
        layer_input = jnp.where(section_index == 0, own_input, incoming)
        seg_query = lax.dynamic_index_in_dim(segment_ids, micro_index, 0, False)
        pad_query = lax.dynamic_index_in_dim(padding, micro_index, 0, False)
        drop_flag = lax.dynamic_index_in_dim(drop_row, micro_index, 0, False)
        layer_out, kept_items = layer_forward(layer_input, params, seg_query, pad_query, drop_flag)
        layer_low = layer_out.astype(jnp.bfloat16)
        received = shifted(layer_low, "section", 1)
        incoming = received
        if tick_index >= 1:
            encoded_rows.append(jnp.where(section_index == 0, received, layer_low))
        saved_ticks.append(kept_items)
    stacked = jax.tree.map(lambda *members: jnp.stack(members), *saved_ticks)
    grad_totals = tuple((jnp.zeros(member.shape, jnp.float32) for member in params))
    grad_incoming = jnp.zeros(tokens.shape[1:], jnp.bfloat16)
    input_rows = []
    for tick_index in range(micro_count + 1):
        raw_index = tick_index - 1 + section_index
        micro_index = jnp.clip(raw_index, 0, micro_count - 1)
        live_tick = ((raw_index >= 0) & (raw_index < micro_count)).astype(jnp.float32)
        forward_tick = jnp.clip(tick_index - 1 + 2 * section_index, 0, micro_count)
        kept_items = jax.tree.map(
            lambda member: lax.dynamic_index_in_dim(member, forward_tick, 0, False), stacked
        )
        own_cot = lax.dynamic_index_in_dim(cotangent, micro_index, 0, False)
        upstream = jnp.where(section_index == 1, own_cot, grad_incoming).astype(jnp.float32)
        seg_query = lax.dynamic_index_in_dim(segment_ids, micro_index, 0, False)
        pad_query = lax.dynamic_index_in_dim(padding, micro_index, 0, False)
        drop_flag = lax.dynamic_index_in_dim(drop_row, micro_index, 0, False)
        keep_scale = (drop_flag == 0).astype(jnp.float32) * live_tick
        layer_grads, grad_input = layer_backward(
            upstream * keep_scale, kept_items, params, seg_query
        )
        grad_totals = tuple((total + term for total, term in zip(grad_totals, layer_grads)))
        grad_input = grad_input + (drop_flag > 0).astype(jnp.float32) * upstream
        grad_low = grad_input.astype(jnp.bfloat16)
        received = shifted(grad_low, "section", 1)
        grad_incoming = received
        if tick_index >= 1:
            input_rows.append(jnp.where(section_index == 0, grad_low, received))
    reduced_once = (
        lax.psum_scatter(
            grad_totals[0][None].astype(jnp.bfloat16), "dp", scatter_dimension=1, tiled=True
        ).astype(jnp.float32),
        lax.psum_scatter(
            grad_totals[3][None].astype(jnp.bfloat16), "dp", scatter_dimension=1, tiled=True
        ).astype(jnp.float32),
        lax.psum_scatter(
            grad_totals[7][None].astype(jnp.bfloat16), "dp", scatter_dimension=1, tiled=True
        ).astype(jnp.float32),
        lax.psum_scatter(
            grad_totals[9][None].astype(jnp.bfloat16), "dp", scatter_dimension=1, tiled=True
        ).astype(jnp.float32),
    )
    matrix_grads = (
        lax.psum_scatter(
            reduced_once[0].astype(jnp.bfloat16), "ctx", scatter_dimension=2, tiled=True
        ).astype(jnp.float32),
        lax.psum_scatter(
            reduced_once[1].astype(jnp.bfloat16), "ctx", scatter_dimension=2, tiled=True
        ).astype(jnp.float32),
        lax.psum_scatter(
            reduced_once[2].astype(jnp.bfloat16), "ctx", scatter_dimension=2, tiled=True
        ).astype(jnp.float32),
        lax.psum_scatter(
            reduced_once[3].astype(jnp.bfloat16), "ctx", scatter_dimension=2, tiled=True
        ).astype(jnp.float32),
    )
    vector_grads = lax.psum(
        (
            grad_totals[1][None],
            grad_totals[2][None],
            grad_totals[4][None],
            grad_totals[5][None],
            grad_totals[6][None],
            grad_totals[8][None],
            grad_totals[10][None],
            grad_totals[11][None],
            grad_totals[12][None],
        ),
        ("dp", "ctx"),
    )
    encoded = lax.dynamic_slice_in_dim(
        jnp.stack(encoded_rows), section_index * half_width, half_width, 2
    )
    tokens_grad = lax.dynamic_slice_in_dim(
        jnp.stack(input_rows), section_index * half_width, half_width, 2
    )
    return (
        encoded,
        tokens_grad,
        matrix_grads[0],
        vector_grads[0],
        vector_grads[1],
        matrix_grads[1],
        vector_grads[2],
        vector_grads[3],
        vector_grads[4],
        matrix_grads[2],
        vector_grads[5],
        matrix_grads[3],
        vector_grads[6],
        vector_grads[7],
        vector_grads[8],
    )


def dot_plain(left, right):
    return lax.dot_general(left, right, (((1,), (0,)), ((), ())), preferred_element_type=jnp.float32)


def dot_flipped(left, right):
    return lax.dot_general(left, right, (((1,), (1,)), ((), ())), preferred_element_type=jnp.float32)


def dot_leading(left, right):
    return lax.dot_general(left, right, (((0,), (0,)), ((), ())), preferred_element_type=jnp.float32)


def gelu_parts(x):
    below = 0.5 * (1.0 + lax.erf(x * 0.7071067811865476))
    density = jnp.exp(-0.5 * x * x) * 0.3989422804014327
    return (x * below, below + x * density)


def rows_of(index, size):
    return pl.ds(pl.multiple_of(index * size, size), size)


def piece_rows(ctx, at, count, n_pieces):
    return pl.ds(0, count) if n_pieces == 1 else rows_of(ctx ^ at, count)


def head_lanes(shape, which):
    lane = lax.broadcasted_iota(jnp.int32, shape, 1)
    return (lane < HEAD_DIM) if which == 0 else (lane >= HEAD_DIM)


def copy_list(pairs, sems, first=0):
    copies = [pltpu.make_async_copy(src, dst, sems.at[first + at]) for at, (src, dst) in enumerate(pairs)]
    for copy in copies:
        copy.start()
    return copies


def wait_all(copies):
    for copy in copies:
        copy.wait()


low, full = jnp.bfloat16, jnp.float32


def kernel_call(body, operands, outs, scratch, mib, aliases=None):
    spaces = {"a": pl.ANY, "s": pltpu.SMEM, "v": pltpu.VMEM, "h": pltpu.HBM, "c": pltpu.VMEM}
    members = []
    for space, array in operands:
        if space in "vh":
            array = pltpu.with_memory_space_constraint(array, spaces[space])
        members.append(array)
    return pl.pallas_call(
        body,
        out_shape=[spaces[space](shape, kind) for space, shape, kind in outs],
        in_specs=[pl.BlockSpec(memory_space=spaces[space]) for space, _ in operands],
        out_specs=[pl.BlockSpec(memory_space=spaces[space]) for space, _, _ in outs],
        scratch_shapes=scratch,
        input_output_aliases=aliases or {},
        compiler_params=pltpu.CompilerParams(vmem_limit_bytes=mib * 2**20),
    )(*members)


class Outgoing:
    def __init__(self, sems):
        self.sems, self.copies = sems, []

    def send(self, src, dst):
        copy = pltpu.make_async_copy(src, dst, self.sems.at[len(self.copies)])
        copy.start()
        self.copies.append(copy)

    def finish(self):
        wait_all(self.copies)


def scratch_like(shapes):
    return [pltpu.VMEM(shape, kind) for _, shape, kind in shapes]


def in_pairs(count, step):
    def both_steps(at, carry):
        for which in range(UNROLL):
            step(UNROLL * at + which)
        return carry

    lax.fori_loop(0, count // UNROLL, both_steps, 0)


UNROLL = 2


documents = 5


def forward_kernel(active, n_pieces, n_cot, n_alias, scal, qkv_bias_ref, qkv_scale_ref, vec_ref, inner_bias_ref, *refs):
    pieces, refs = refs[:n_pieces], refs[n_pieces:]
    cot_pieces, refs = refs[:n_cot], refs[n_cot:]
    weights_h, refs = refs[:4], refs[4 + n_alias :]
    n_outs = 16 if n_cot else 12
    outs_h, outs, (wqkv, wattn, win, wout, first, code_rows, ids, in_sems, out_sems) = (
        refs[:n_outs],
        refs[n_outs : 2 * n_outs],
        refs[2 * n_outs :],
    )
    u, qkv, att, lse, n1, r1, dg, n2, r2, first_low, res, feats = outs[:12]
    top = outs[12:]
    size, width = u.shape

    @pl.when(scal[0] == active)
    def _():
        loads = [
            pltpu.make_async_copy(src, dst, in_sems.at[at])
            for at, (src, dst) in enumerate(zip(weights_h, (wqkv, wattn, win, wout)))
        ]
        loads[0].start()
        out = Outgoing(out_sems)

        def save(*places):
            for place in places:
                out.send(outs[place], outs_h[place])

        count = size // 4
        if n_pieces == 1:
            u[...] = pieces[0][:size]
            ids[...] = pieces[0][size:, :size].astype(full)[:8]
        else:
            for at, piece in enumerate(pieces):
                place = rows_of(scal[1] ^ at, count)
                u[place, :] = piece[:count]
                ids[:, place] = piece[count:, :count].astype(full)[:8]
        lane = lax.broadcasted_iota(jnp.int32, (size, 128), 1)
        lane = jnp.where(lane < HEAD_DIM, lane, lane - HEAD_DIM).astype(full)
        for which in range(2):
            for at in range(4):
                place = slice(at * count, (at + 1) * count)
                code_rows[place, :] = jnp.broadcast_to(ids[which : which + 1, place], (count, count)).T
            if which == 0:
                differs = (lane < documents) & (code_rows[...] != lane)
                feats[0] = jnp.where(differs | (lane == documents), masked_score, 0.0).astype(low)
            else:
                padded = (lane == documents) & (code_rows[...] < 0)
                feats[1] = jnp.where(padded | (code_rows[...] == lane), 1.0, 0.0).astype(low)
        loads[0].wait()
        loads[1].start()
        loads[2].start()
        save(0, 11)
        value = dot_plain(u[...], wqkv[...]) + qkv_bias_ref[...]
        qkv[...] = (value * qkv_scale_ref[...]).astype(low)
        save(1)
        def heads(pair):
            query, key, value = (qkv[:, rows_of(pair + part * (width // 128), 128)] for part in range(3))
            sides = []
            for which in range(2):
                own = head_lanes(key.shape, which)
                scores = dot_flipped(jnp.where(own, key, feats[1]), jnp.where(own, query, feats[0]))
                top_score = jnp.max(scores, axis=0, keepdims=True)
                weights = jnp.exp(scores - top_score)
                total = jnp.sum(weights, axis=0, keepdims=True)
                head = 2 * pair + which
                lse[pl.ds(head, 1), :] = top_score + jnp.log(total)
                sides.append(dot_leading((weights * (1.0 / total)).astype(low), value))
            att[:, rows_of(pair, 128)] = jnp.where(head_lanes((size, 128), 0), sides[0], sides[1]).astype(low)

        in_pairs(width // 128, heads)
        save(2, 3)
        loads[1].wait()
        value = dot_plain(att[...], wattn[...]) + u[...].astype(full) + vec_ref[0:1, :]
        normed, inverse = normalize(value)
        n1[...] = normed.astype(low)
        r1[...] = jnp.broadcast_to(inverse, r1.shape)
        value = normed * vec_ref[1:2, :] + vec_ref[2:3, :]
        first[...] = value + vec_ref[3:4, :]
        first_low[...] = value.astype(low)
        save(9, 4, 5)
        loads[2].wait()
        loads[3].start()
        inner = dot_plain(first_low[...], win[...]) + inner_bias_ref[...]
        active_value, slope = gelu_parts(inner)
        dg[...] = slope.astype(low)
        save(6)
        loads[3].wait()
        normed, inverse = normalize(first[...] + dot_plain(active_value.astype(low), wout[...]))
        n2[...] = normed.astype(low)
        r2[...] = jnp.broadcast_to(inverse, r2.shape)
        value = normed * vec_ref[4:5, :] + vec_ref[5:6, :]
        res[:size] = jnp.where(scal[2] > 0, u[...], value.astype(low))
        res[size:, :size] = jnp.concatenate([ids[...], jnp.zeros_like(ids)], axis=0).astype(low)
        save(10)
        if n_cot:
            for at, piece in enumerate(cot_pieces):
                top[0][rows_of(scal[1] ^ at, count), :] = piece[...]
            top_of_backward(scal, vec_ref, normed, inverse, *top[:3])
            top[3][0] = first_low[...]
            top[3][1] = top[1][...]
            save(15, 13, 12, 14)
        else:
            save(7, 8)
        out.finish()


def top_of_backward(scal, vec_ref, normed, inverse, inc, dffn, vec):
    grad = inc[...].astype(full) * jnp.where(scal[2] > 0, 0.0, 1.0)
    value = norm_back(grad, normed, inverse, vec_ref[4:5, :])
    rounded = value.astype(low)
    dffn[...] = rounded
    vec[0:1, :] = column_sum(rounded.astype(full))
    vec[1:2, :] = column_sum(grad * normed)
    vec[2:3, :] = column_sum(grad)


def top_shapes(size, width):
    return [
        ("h", (size, width), low),
        ("h", (size, width), low),
        ("h", (8, width), full),
    ]


def run_forward(active, scal, small, pieces, cot_pieces, held, earlier, after):
    width, hidden = held[2].shape
    size = len(pieces) * (pieces[0].shape[0] - 16)
    outs = [
        ("h", (size, width), low),
        ("h", (size, 3 * width), low),
        ("h", (size, width), low),
        ("h", (16, size), full),
        ("h", (size, width), low),
        ("h", (size, 128), full),
        ("h", (size, hidden), low),
        ("h", (size, width), low),
        ("h", (size, 128), full),
        ("h", (size, width), low),
        ("h", (size + 16, width), low),
        ("h", (2, size, 128), low),
    ]
    if cot_pieces:
        outs += top_shapes(size, width) + [("h", (2, size, width), low)]
    operands = [("s", scal)] + [("c", member) for member in small]
    operands += [("c", member) for member in (*pieces, *cot_pieces)] + [("h", member) for member in held]
    at_alias = len(operands)
    operands += [(out[0], member) for out, member in zip(outs, earlier)] + [("c", member) for member in after]
    return kernel_call(
        partial(forward_kernel, active, len(pieces), len(cot_pieces), len(earlier) + len(after)),
        operands,
        outs,
        scratch_like(outs)
        + [pltpu.VMEM(member.shape, low) for member in held]
        + [
            pltpu.VMEM((size, width), full),
            pltpu.VMEM((size, size // 4), full),
            pltpu.VMEM((8, size), full),
            pltpu.SemaphoreType.DMA((4,)),
            pltpu.SemaphoreType.DMA((len(outs),)),
        ],
        48,
        {at_alias + i: i for i in range(len(earlier))},
    )


def column_sum(value):
    return jnp.sum(value, axis=0, keepdims=True)


def top_kernel(active, n_alias, n_after, scal, vec_ref, incoming, n2_h, r2_h, *refs):
    refs = refs[n_alias + n_after :]
    outs_h, outs, (n2, r2, in_sems, out_sems) = refs[:3], refs[3:6], refs[6:]

    @pl.when(scal[0] == active)
    def _():
        loads = copy_list([(n2_h, n2), (r2_h, r2)], in_sems)
        outs[0][...] = incoming[...]
        wait_all(loads)
        top_of_backward(scal, vec_ref, n2[...].astype(full), r2[:, :1], *outs)
        wait_all(copy_list(list(zip(outs, outs_h)), out_sems))


def run_top(active, scal, vecs, incoming, n2, r2, earlier, after):
    size, width = n2.shape
    outs = top_shapes(size, width)
    operands = [("s", scal), ("c", vecs), ("c", incoming)] + [("h", member) for member in (n2, r2)]
    at_alias = len(operands)
    operands += [(out[0], member) for out, member in zip(outs, earlier)] + list(after)
    return kernel_call(
        partial(top_kernel, active, len(earlier), len(after)),
        operands,
        outs,
        scratch_like(outs)
        + [
            pltpu.VMEM(n2.shape, low),
            pltpu.VMEM(r2.shape, full),
            pltpu.SemaphoreType.DMA((2,)),
            pltpu.SemaphoreType.DMA((3,)),
        ],
        16,
        {at_alias + i: i for i in range(len(earlier))},
    )


def chain_kernel(active, n_alias, n_after, scal, vec_ref, *refs):
    held_h, refs = refs[:12], refs[12 + n_alias + n_after :]
    outs_h, outs, held, (dinner, datt, first, in_sems, out_sems) = refs[:4], refs[4:8], refs[8:20], refs[20:]
    inc, dffn, dg, n1, r1, qkv, lse, wqkv, wattn, win, wout, feats = held
    dqkv, dbranch, vec, din = outs
    size, width = inc.shape
    hidden = win.shape[1]

    @pl.when(scal[0] == active)
    def _():
        chunks = hidden // width
        cuts = [slice(at * width, (at + 1) * width) for at in range(chunks)]
        order = [(held_h[1], dffn)]
        for cut in cuts:
            order += [(held_h[10].at[cut, :], wout.at[cut, :]), (held_h[2].at[:, cut], dg.at[:, cut])]
        order += [(held_h[at], held[at]) for at in (9, 3, 4, 8, 5, 6, 11, 7, 0)]
        loads = [pltpu.make_async_copy(src, dst, in_sems.at[at]) for at, (src, dst) in enumerate(order)]

        def begin(first_copy, last_copy):
            for copy in loads[first_copy:last_copy]:
                copy.start()

        begin(0, 5)
        out = Outgoing(out_sems)
        for at, cut in enumerate(cuts):
            wait_all(loads[: 3] if at == 0 else loads[2 * at + 1 : 2 * at + 3])
            begin(2 * at + 5, 2 * at + 7)
            value = (dot_flipped(dffn[...], wout[cut, :]) * dg[:, cut].astype(full)).astype(low)
            dinner[:, cut] = value
            vec[8 + at : 9 + at, :] = column_sum(value.astype(full))
        begin(2 * chunks + 5, len(loads))
        loads = loads[2 * chunks + 1 :]
        wait_all(loads[:3])
        grad = dot_flipped(dinner[...], win[...]) + dffn[...].astype(full)
        normed = n1[...].astype(full)
        value = norm_back(grad, normed, r1[:, :1], vec_ref[1:2, :])
        first[...] = value
        rounded = value.astype(low)
        dbranch[...] = rounded
        vec[2:3, :] = column_sum(rounded.astype(full))
        vec[3:4, :] = column_sum(grad * normed)
        vec[4:5, :] = column_sum(grad)
        out.send(dbranch, outs_h[1])
        loads[3].wait()
        datt[...] = dot_flipped(dbranch[...], wattn[...]).astype(low)
        wait_all(loads[4:7])
        def heads(pair):
            cols = [rows_of(pair + part * (width // 128), 128) for part in range(3)]
            query, key, value = (qkv[:, col] for col in cols)
            grad = datt[:, cols[0]]
            parts = []
            for which in range(2):
                own = head_lanes(key.shape, which)
                scores = dot_flipped(jnp.where(own, key, feats[1]), jnp.where(own, query, feats[0]))
                value_own = jnp.where(own, value, jnp.zeros_like(value))
                head = 2 * pair + which
                probs = jnp.exp(scores - lse[pl.ds(head, 1), :])
                dprobs = dot_flipped(value_own, grad)
                delta = column_sum(probs * dprobs)
                dscores = (probs * (dprobs - delta)).astype(low)
                parts.append(
                    (dot_leading(dscores, key), dot_plain(dscores, query), dot_plain(probs.astype(low), grad))
                )
            low_lanes = head_lanes((size, 128), 0)
            dquery, dkey, dvalue = (jnp.where(low_lanes, one, two) for one, two in zip(*parts))
            dquery = (dquery * HEAD_DIM ** (-0.5)).astype(low)
            dvalue = dvalue.astype(low)
            dqkv[:, cols[0]] = dquery
            dqkv[:, cols[1]] = dkey.astype(low)
            dqkv[:, cols[2]] = dvalue
            vec[0:1, cols[0]] = column_sum(dquery.astype(full))
            vec[1:2, cols[0]] = column_sum(dvalue.astype(full))

        in_pairs(width // 128, heads)
        out.send(dqkv, outs_h[0])
        out.send(vec, outs_h[2])
        wait_all(loads[7:])
        value = first[...] + dot_flipped(dqkv[...], wqkv[...])
        din[...] = jnp.where(scal[2] > 0, inc[...], value.astype(low))
        out.send(din, outs_h[3])
        out.finish()


def run_chain(active, scal, vecs, top, kept, held, earlier, after):
    u, qkv, att, lse, n1, r1, dg = kept[:7]
    inc, dffn = top[:2]
    size, width = u.shape
    hidden = dg.shape[1]
    outs = [
        ("h", (size, 3 * width), low),
        ("h", (size, width), low),
        ("h", (16, width), full),
        ("h", (size, width), low),
    ]
    members = (inc, dffn, dg, n1, r1, qkv, lse, *held, kept[11])
    operands = [("s", scal), ("c", vecs)] + [("h", member) for member in members]
    at_alias = len(operands)
    operands += [(out[0], member) for out, member in zip(outs, earlier)]
    operands += list(after)
    return kernel_call(
        partial(chain_kernel, active, len(earlier), len(after)),
        operands,
        outs,
        scratch_like(outs)
        + [pltpu.VMEM(member.shape, member.dtype) for member in members]
        + [
            pltpu.VMEM((size, hidden), low),
            pltpu.VMEM((size, width), low),
            pltpu.VMEM((size, width), full),
            pltpu.SemaphoreType.DMA((2 * (hidden // width) + 10,)),
            pltpu.SemaphoreType.DMA((4,)),
        ],
        48,
        {at_alias + i: i for i in range(len(earlier))},
    )


def split_high(value):
    high = value.astype(low)
    return high, (value - high.astype(full)).astype(low)


def wide_pair(value, rows):
    pair = jnp.concatenate(split_high(value), axis=1)
    return jnp.concatenate([pair, jnp.zeros((rows - pair.shape[0], pair.shape[1]), low)], axis=0)


def joined(high, rest):
    return high.astype(full) + rest.astype(full)


def attn_grad_kernel(n_after, scal, top_vec, chain_vec, *refs):
    ins_h, refs = refs[:4], refs[4 + n_after :]
    send_a, keep_a, send_b, keep_b, vec = refs[:5]
    (u, att, dqkv, dbranch), out, pair, in_sems, sems = refs[5:9], *refs[9:]
    width = u.shape[1]
    dp = scal[3]
    bit_y, bit_x = dp // 2, dp % 2
    left, right = pl.ds(0, 2 * width), pl.ds(2 * width, 2 * width)
    each = width // 4
    loads = copy_list([(ins_h[at], (u, att, dqkv, dbranch)[at]) for at in (0, 2, 1, 3)], in_sems)
    sent = Outgoing(sems)
    value = jnp.concatenate([top_vec[...], chain_vec[...]], axis=0)
    vec[...] = value
    pair[...] = wide_pair(value, VEC_ROWS)
    sent.send(pair, send_a.at[pl.ds(2 * each, VEC_ROWS)])
    wait_all(loads[:2])
    flipped = u[...].T
    out[:, : 2 * width] = dot_plain(flipped, dqkv[:, : 2 * width]).astype(low)
    for at in range(2):
        sent.send(out.at[rows_of(2 * at + 1 - bit_x, each), left], send_a.at[pl.ds(at * each, each)])
        sent.send(out.at[rows_of(2 * at + bit_x, each), left], keep_a.at[at])
    out[:, 2 * width : 3 * width] = dot_plain(flipped, dqkv[:, 2 * width :]).astype(low)
    wait_all(loads[2:])
    out[:, 3 * width :] = dot_leading(att[...], dbranch[...]).astype(low)
    for at in range(2):
        sent.send(out.at[rows_of(2 * (1 - bit_y) + at, each), right], send_b.at[at])
        sent.send(out.at[rows_of(2 * bit_y + at, each), right], keep_b.at[at])
    sent.finish()


VEC_ROWS = 32


def run_attn_grad(scal, top_vec, chain_vec, u, att, dqkv, dbranch, after):
    width = u.shape[1]
    each = width // 4
    members = (u, att, dqkv, dbranch)
    half_shape = ("h", (2, each, 2 * width), low)
    return kernel_call(
        partial(attn_grad_kernel, len(after)),
        [("s", scal), ("c", top_vec), ("c", chain_vec)] + [("h", member) for member in members] + list(after),
        [("h", (2 * each + VEC_ROWS, 2 * width), low)] + [half_shape] * 3 + [("c", (24, width), full)],
        [pltpu.VMEM(member.shape, low) for member in members]
        + [
            pltpu.VMEM((width, 4 * width), low),
            pltpu.VMEM((VEC_ROWS, 2 * width), low),
            pltpu.SemaphoreType.DMA((4,)),
            pltpu.SemaphoreType.DMA((9,)),
        ],
        24,
    )


def ffn_grad_kernel(n_after, scal, inner_bias_ref, win_h, wout_h, first_h, dffn_h, *refs):
    from_one, firsts, dffns = refs[:3], refs[3:6], refs[6:9]
    send, keep, first, dffn, active, dinner, win, wout, out, sems = refs[9 + n_after :]
    size, width = dffn_h.shape
    own = rows_of(2 * (scal[3] % 2) + scal[1] % 2, width)
    loads = copy_list(
        [
            (first_h, first.at[:size]),
            (win_h.at[:, own], win),
            (dffn_h, dffn.at[:size]),
            (wout_h.at[own, :], wout),
        ],
        sems,
    )
    is_zero = scal[0] == 0
    for at in range(4):
        rows = slice(at * size, (at + 1) * size)
        if at == 0:
            wait_all(loads)
            value, grad = first[rows], dffn[rows]
        else:
            value = jnp.where(is_zero, firsts[at - 1][...], from_one[at - 1][0])
            grad = jnp.where(is_zero, dffns[at - 1][...], from_one[at - 1][1])
            first[rows] = value
            dffn[rows] = grad
        inner = dot_plain(value, win[...]) + inner_bias_ref[:, own]
        active_value, slope = gelu_parts(inner)
        active[rows] = active_value.astype(low)
        dinner[rows] = (dot_flipped(grad, wout[...]) * slope).astype(low)
    each = width // 4
    for half, (left, right) in enumerate(((first, dinner), (dffn, active))):
        part = dot_leading(left[...], right[...]).astype(low)
        for block in range(4):
            out[block, each * half : each * (half + 1)] = part[each * block : each * (block + 1)]
    bit = scal[3] // 2
    wait_all(
        copy_list(
            [(out.at[2 * (1 - bit) + at], send.at[at]) for at in range(2)]
            + [(out.at[2 * bit + at], keep.at[at]) for at in range(2)],
            sems,
        )
    )


def run_ffn_grad(scal, inner_bias, win, wout, first_own, dffn_own, from_one, firsts, dffns, after):
    size, width = dffn_own.shape
    return kernel_call(
        partial(ffn_grad_kernel, len(after)),
        [("s", scal), ("c", inner_bias)]
        + [("h", member) for member in (win, wout, first_own, dffn_own)]
        + [("c", member) for member in (*from_one, *firsts, *dffns)]
        + list(after),
        [("h", (2, width // 2, width), low)] * 2,
        [pltpu.VMEM((4 * size, width), low) for _ in range(4)]
        + [pltpu.VMEM((width, width), low), pltpu.VMEM((width, width), low)]
        + [pltpu.VMEM((4, width // 2, width), low), pltpu.SemaphoreType.DMA((4,))],
        32,
    )


def merge_kernel(scal, got_a, keep_a, got_b, keep_b, vec, send_a, left_a, send_b, left_b, vec_out):
    bit_y, bit_x = scal[3] // 2, scal[3] % 2
    each, width = keep_a.shape[1], vec.shape[1]
    send_a[:each] = added(got_a[rows_of(1 - bit_y, each)], keep_a[1 - bit_y])
    left_a[...] = added(got_a[rows_of(bit_y, each)], keep_a[bit_y])
    send_b[...] = added(got_b[1 - bit_x], keep_b[1 - bit_x])
    left_b[...] = added(got_b[bit_x], keep_b[bit_x])
    pair = got_a[2 * each :]
    value = vec[...] + joined(pair[:24, :width], pair[:24, width:])
    vec_out[...] = value
    send_a[each:] = wide_pair(value, VEC_ROWS)


def turn_kernel(scal, got_a, keep_a, got_b, keep_b, vec, send, keep, vec_out, rows, blocks):
    each, cut = keep_a.shape
    rows[:, :cut] = added(got_a[:each], keep_a[...])
    rows[:, cut:] = added(got_b[...], keep_b[...])
    width = cut // 2
    wide, narrow = 3 * width // 4, width // 4
    for at in range(4):
        blocks[at, :, :wide] = rows[:, wide * at : wide * (at + 1)]
        blocks[at, :, wide:] = rows[:, 3 * width + narrow * at : 3 * width + narrow * (at + 1)]
    bit = scal[1] % 2
    for at in range(2):
        send[at * each : (at + 1) * each] = blocks[2 * at + 1 - bit]
        keep[at] = blocks[2 * at + bit]
    pair = got_a[each:]
    value = vec[...] + joined(pair[:24, :width], pair[:24, width:])
    vec_out[...] = value
    send[2 * each :] = jnp.concatenate(split_high(value), axis=0)


def last_kernel(scal, got, keep, vec, send, left, vec_out):
    bit = scal[1] // 2
    each = keep.shape[1]
    send[:each] = added(got[rows_of(1 - bit, each)], keep[1 - bit])
    left[...] = added(got[rows_of(bit, each)], keep[bit])
    pair = got[2 * each :]
    value = vec[...] + joined(pair[:24], pair[24:])
    vec_out[...] = value
    send[each:] = jnp.concatenate(split_high(value), axis=0)


def end_kernel(scal, got, keep, vec, qkv_out, attn_out, vec_out):
    each = keep.shape[0]
    value = got[:each].astype(full) + keep[...].astype(full)
    qkv_out[...] = value[:, : 3 * each]
    attn_out[...] = value[:, 3 * each :]
    pair = got[each:]
    vec_out[...] = vec[...] + joined(pair[:24], pair[24:])


def half_kernel(scal, got, keep, send, left):
    bit = scal[1] // 2
    send[...] = added(got[1 - bit], keep[1 - bit])
    left[...] = added(got[bit], keep[bit])


def swapped(x, axis, by):
    return lax.ppermute(x, axis, [(i, i ^ by) for i in range(lax.axis_size(axis))])


def near(section, x, by):
    pairs = [
        (16 * section + 4 * i + j, 16 * section + 4 * (i ^ (by & 1)) + (j ^ (by >> 1)))
        for i in range(4)
        for j in range(4)
    ]
    return lax.ppermute(x, ("section", "dp", "ctx"), pairs)


def moved(x, target):
    pairs = [(16 * s + 4 * i + j, 16 * s + target(i, j)) for s in range(2) for i in range(4) for j in range(4)]
    return lax.ppermute(x, ("section", "dp", "ctx"), pairs)


def swapped_in(section, x, axis, by):
    length = lax.axis_size(axis)
    pairs = [(section * length + i, section * length + (i ^ by)) for i in range(length)]
    return lax.ppermute(x, ("section", axis), pairs)


def pick(x, at, dim=0):
    return lax.dynamic_index_in_dim(x, at, dim, False)


def added(one, two):
    return (one.astype(full) + two.astype(full)).astype(low)


def spread(row_half, ctx, swap):
    length = lax.axis_size("ctx")
    size, width = row_half.shape
    parts = row_half.reshape(length, size // length, width)
    out = jnp.zeros(parts.shape, parts.dtype)
    out = lax.dynamic_update_index_in_dim(out, pick(parts, ctx), ctx, 0)
    for k in range(1, length):
        out = lax.dynamic_update_index_in_dim(out, swap(pick(parts, ctx ^ k), "ctx", k), ctx ^ k, 0)
    return out


def to_section(x, section):
    return lax.ppermute(x, "section", [(1 - section, section)])


def following(body, n_operands, n_after, *refs):
    body(*refs[:n_operands], *refs[n_operands + n_after :])


def merged(body, scal, operands, outs, scratch=(), after=()):
    return kernel_call(
        partial(following, body, 1 + len(operands), len(after)),
        [("s", scal)] + [("c", member) for member in operands] + [("a", member) for member in after],
        [("c", shape, kind) for shape, kind in outs],
        list(scratch),
        16,
    )


def row_body(
    tokens,
    segment_ids,
    padding,
    dropped,
    qkv_weight,
    query_bias,
    value_bias,
    attn_weight,
    attn_bias,
    attn_gain,
    attn_shift,
    inner_weight,
    inner_bias,
    outer_weight,
    outer_bias,
    ffn_gain,
    ffn_shift,
    cotangent,
):
    width = tokens.shape[2]
    half, each = width // 2, width // 4
    count = tokens.shape[1]
    section, dp, ctx = (lax.axis_index(name) for name in ("section", "dp", "ctx"))
    weights = (qkv_weight[0], attn_weight[0], inner_weight[0], outer_weight[0])
    vecs = jnp.concatenate(
        [attn_bias, attn_gain, attn_shift, outer_bias, ffn_gain, ffn_shift, query_bias, value_bias]
    )
    qkv_bias = jnp.concatenate([query_bias, jnp.zeros_like(query_bias), value_bias], axis=1)
    qkv_scale = jnp.concatenate(
        [jnp.full((1, width), HEAD_DIM ** (-0.5), jnp.float32), jnp.ones((1, 2 * width), jnp.float32)], axis=1
    )
    small = (qkv_bias, qkv_scale, vecs, inner_bias)
    scal = jnp.stack([section, ctx, pick(dropped[0], ctx), dp]).astype(jnp.int32)

    ids = jnp.stack([segment_ids, jnp.where(padding == 1, segment_ids, -1)], axis=1).astype(low)
    ids = jnp.pad(ids, ((0, 0), (0, 14), (0, width - count)))
    sent = jnp.concatenate([tokens, ids], axis=1)
    own_tokens = [pick(sent, ctx)] + [swapped_in(0, pick(sent, ctx ^ k), "ctx", k) for k in range(1, 4)]
    held = weights
    own_cot = [pick(cotangent, ctx)] + [swapped_in(1, pick(cotangent, ctx ^ k), "ctx", k) for k in range(1, 4)]

    kept = run_forward(0, scal, small, own_tokens, [], held, [], [])
    middle = lax.ppermute(kept[10], "section", [(0, 1)])
    firsts = [near(0, kept[9], k) for k in range(1, 4)]
    made = run_forward(1, scal, small, [middle], own_cot, held, kept, firsts)
    kept, top, both = made[:12], made[12:15], made[15]
    from_one = [near(1, both, k) for k in range(1, 4)]
    chain = run_chain(1, scal, vecs, top, kept, held, [], [])
    incoming = to_section(chain[3], 0)
    top = run_top(0, scal, vecs, incoming, kept[7], kept[8], top, [("c", member) for member in from_one])
    dffns = [near(0, top[1], k) for k in range(1, 4)]
    chain = run_chain(0, scal, vecs, top, kept, held, chain, [])
    dqkv, dbranch, chain_vec, d_input = chain
    result = kept[10][: 4 * count]

    send_a, keep_a, send_b, keep_b, vec = run_attn_grad(
        scal, top[2], chain_vec, kept[0], kept[2], dqkv, dbranch, []
    )
    got_a, got_b = swapped(send_a, "dp", 1), swapped(send_b, "dp", 2)
    ffn_send, ffn_keep = run_ffn_grad(
        scal, inner_bias, held[2], held[3], kept[9], top[1], from_one, firsts, dffns, [("h", keep_b)]
    )
    ffn_got = swapped(ffn_send, "dp", 2)
    wide, block, flat = (each, 2 * width), (each, width), ((24, width), full)
    send_a, keep_a, send_b, keep_b, vec = merged(
        merge_kernel,
        scal,
        (got_a, keep_a, got_b, keep_b, vec),
        [((each + VEC_ROWS, 2 * width), low), (wide, low), (wide, low), (wide, low), flat],
        after=[ffn_keep],
    )
    got_a, got_b = swapped(send_a, "dp", 2), swapped(send_b, "dp", 1)
    ffn_send, ffn_keep = merged(
        half_kernel, scal, (ffn_got, ffn_keep), [(ffn_keep.shape[1:], low)] * 2, after=[send_b]
    )
    ffn_got = swapped(ffn_send, "ctx", 2)
    rows = jnp.where(section == 0, d_input, result)
    rows, ffn_keep = lax.optimization_barrier((rows, ffn_keep))
    rows = spread(rows, ctx, swapped)
    send, keep, vec = merged(
        turn_kernel,
        scal,
        (got_a, keep_a, got_b, keep_b, vec),
        [((2 * each + 48, width), low), ((2, each, width), low), flat],
        [pltpu.VMEM((each, 4 * width), low), pltpu.VMEM((4, each, width), low)],
        after=[ffn_keep],
    )
    got = swapped(send, "ctx", 1)
    send, keep, vec = merged(last_kernel, scal, (got, keep, vec), [((each + 48, width), low), (block, low), flat])
    got = swapped(send, "ctx", 2)
    qkv_grad, attn_grad, vec = merged(
        end_kernel, scal, (got, keep, vec), [((each, 3 * each), full), ((each, each), full), flat]
    )
    ffn_rows = added(ffn_got, ffn_keep)
    inner_grad = moved(ffn_rows[:each], lambda i, j: 4 * (2 * (i // 2) + j // 2) + 2 * (i % 2) + j % 2).astype(full)
    outer_grad = moved(ffn_rows[each:], lambda i, j: 4 * (2 * (i % 2) + j % 2) + 2 * (i // 2) + j // 2).astype(full).T
    rows, vec = lax.optimization_barrier((rows, vec))
    other_half = swapped(jnp.where(section == 0, rows[..., half:], rows[..., :half]), "section", 1)
    tokens_grad = jnp.where(section == 0, rows[..., :half], other_half)
    encoded = jnp.where(section == 0, other_half, rows[..., half:])
    return (
        encoded,
        tokens_grad,
        qkv_grad[None],
        vec[8:9],
        vec[9:10],
        attn_grad[None],
        vec[10:11],
        vec[11:12],
        vec[12:13],
        inner_grad[None],
        vec[16 : 16 + inner_bias.shape[1] // width].reshape(1, -1),
        outer_grad[None],
        vec[0:1],
        vec[1:2],
        vec[2:3],
    )


def solution(mesh):
    placed = (
        P("dp", "ctx", None),
        P("dp", "ctx"),
        P("dp", "ctx"),
        P("section", "dp"),
        P("section", None, None),
        P("section", None),
        P("section", None),
        P("section", None, None),
        P("section", None),
        P("section", None),
        P("section", None),
        P("section", None, None),
        P("section", None),
        P("section", None, None),
        P("section", None),
        P("section", None),
        P("section", None),
        P("dp", "ctx", None),
    )

    def dispatch(*members):
        rows = members[0].shape[0]
        same = rows == lax.axis_size("ctx") == lax.axis_size("dp") == 4
        return (row_body if same else body)(*members)

    return jax.shard_map(
        dispatch,
        mesh=mesh,
        in_specs=placed,
        out_specs=(
            P("dp", "ctx", "section"),
            P("dp", "ctx", "section"),
            P("section", "dp", "ctx"),
            P("section", None),
            P("section", None),
            P("section", "dp", "ctx"),
            P("section", None),
            P("section", None),
            P("section", None),
            P("section", "dp", "ctx"),
            P("section", None),
            P("section", "dp", "ctx"),
            P("section", None),
            P("section", None),
            P("section", None),
        ),
        check_vma=False,
    )
```

```python
from functools import partial

import jax
import jax.numpy as jnp
from jax import lax
from jax.experimental import pallas as pl
from jax.experimental.pallas import tpu as pltpu
from jax.sharding import PartitionSpec as P

HEADS = 12
HEAD_DIM = 64


norm_eps = 1e-05
masked_score = -1e30


def shifted(x, axis, by):
    length = lax.axis_size(axis)
    return lax.ppermute(x, axis, [(i, (i + by) % length) for i in range(length)])


def matmul_low(left, right):
    return jnp.dot(left, right, preferred_element_type=jnp.float32)


def left_product(left, right):
    return jnp.einsum("ti,to->io", left, right, preferred_element_type=jnp.float32)


def right_product(left, right):
    return jnp.einsum("to,io->ti", left, right, preferred_element_type=jnp.float32)


def normalize(values):
    mean_value = jnp.mean(values, axis=-1, keepdims=True)
    centered = values - mean_value
    variance = jnp.mean(centered * centered, axis=-1, keepdims=True)
    inverse = lax.rsqrt(variance + norm_eps)
    return (centered * inverse, inverse)


def norm_back(grad_out, normed, inverse, gain):
    scaled = grad_out * gain
    return inverse * (
        scaled
        - jnp.mean(scaled, axis=-1, keepdims=True)
        - normed * jnp.mean(scaled * normed, axis=-1, keepdims=True)
    )


def attend_piece(query_heads, seg_query, running, pieces):
    run_max, run_total, run_acc = running
    key_piece, value_piece, seg_piece, pad_piece = pieces
    count = key_piece.shape[0]
    key_heads = key_piece.reshape(count, HEADS, HEAD_DIM)
    value_heads = value_piece.reshape(count, HEADS, HEAD_DIM)
    scores = jnp.einsum(
        "qhd,khd->hqk", query_heads, key_heads, preferred_element_type=jnp.float32
    ) * HEAD_DIM ** (-0.5)
    allowed = (seg_query[:, None] == seg_piece[None, :]) & (pad_piece[None, :] == 1)
    scores = jnp.where(allowed[None], scores, masked_score)
    new_max = jnp.maximum(run_max, jnp.max(scores, axis=-1))
    weights = jnp.where(allowed[None], jnp.exp(scores - new_max[..., None]), 0.0)
    run_total = jnp.sum(weights, axis=-1)
    run_acc = jnp.einsum(
        "hqk,khd->hqd",
        weights.astype(jnp.bfloat16),
        value_heads,
        preferred_element_type=jnp.float32,
    )
    return (new_max, run_total, run_acc)


def attention_back(
    query_low, key_all, value_all, seg_query, seg_all, pad_all, log_total, row_delta, grad_att
):
    row_count = query_low.shape[0]
    seq_count = key_all.shape[0]
    score_scale = HEAD_DIM ** (-0.5)
    query_heads = query_low.reshape(row_count, HEADS, HEAD_DIM)
    key_heads = key_all.reshape(seq_count, HEADS, HEAD_DIM)
    value_heads = value_all.reshape(seq_count, HEADS, HEAD_DIM)
    grad_heads = grad_att.reshape(row_count, HEADS, HEAD_DIM)
    scores = (
        jnp.einsum("qhd,khd->hqk", query_heads, key_heads, preferred_element_type=jnp.float32)
        * score_scale
    )
    allowed = (seg_query[:, None] == seg_all[None, :]) & (pad_all[None, :] == 1)
    prob_rows = jnp.where(allowed[None], jnp.exp(scores - log_total[..., None]), 0.0)
    grad_probs = jnp.einsum(
        "qhd,khd->hqk", grad_heads, value_heads, preferred_element_type=jnp.float32
    )
    grad_scores = (prob_rows * (grad_probs - row_delta[..., None])).astype(jnp.bfloat16)
    grad_query = (
        jnp.einsum("hqk,khd->qhd", grad_scores, key_heads, preferred_element_type=jnp.float32)
        * score_scale
    )
    grad_key = (
        jnp.einsum("hqk,qhd->khd", grad_scores, query_heads, preferred_element_type=jnp.float32)
        * score_scale
    )
    grad_value = jnp.einsum(
        "hqk,qhd->khd",
        prob_rows.astype(jnp.bfloat16),
        grad_heads,
        preferred_element_type=jnp.float32,
    )
    model_width = HEADS * HEAD_DIM
    return (
        grad_query.reshape(row_count, model_width),
        grad_key.reshape(seq_count, model_width),
        grad_value.reshape(seq_count, model_width),
    )


def layer_forward(layer_input, params, seg_query, pad_query, drop_flag):
    (
        qkv_weight,
        query_bias,
        value_bias,
        attn_weight,
        attn_bias,
        attn_gain,
        attn_shift,
        inner_weight,
        inner_bias,
        outer_weight,
        outer_bias,
        ffn_gain,
        ffn_shift,
    ) = params
    model_width = layer_input.shape[1]
    row_count = layer_input.shape[0]
    projected = matmul_low(layer_input, qkv_weight)
    query_low = (projected[:, :model_width] + query_bias).astype(jnp.bfloat16)
    key_local = projected[:, model_width : 2 * model_width].astype(jnp.bfloat16)
    value_local = (projected[:, 2 * model_width :] + value_bias).astype(jnp.bfloat16)
    query_heads = query_low.reshape(row_count, HEADS, HEAD_DIM)
    start_state = (
        jnp.full((HEADS, row_count), masked_score, jnp.float32),
        jnp.zeros((HEADS, row_count), jnp.float32),
        jnp.zeros((HEADS, row_count, HEAD_DIM), jnp.float32),
    )
    key_all, value_all, seg_all, pad_all = (
        lax.all_gather(key_local, "ctx", axis=0, tiled=True),
        lax.all_gather(value_local, "ctx", axis=0, tiled=True),
        lax.all_gather(seg_query, "ctx", axis=0, tiled=True),
        lax.all_gather(pad_query, "ctx", axis=0, tiled=True),
    )
    run_max, run_total, run_acc = attend_piece(
        query_heads, seg_query, start_state, (key_all, value_all, seg_all, pad_all)
    )
    gathered = (key_all, value_all, seg_all, pad_all)
    attended = (run_acc / run_total[..., None]).transpose(1, 0, 2).reshape(row_count, model_width)
    log_total = run_max + jnp.log(run_total)
    branch = matmul_low(attended.astype(jnp.bfloat16), attn_weight) + attn_bias
    sum_attn = layer_input.astype(jnp.float32) + branch
    normed, inverse = normalize(sum_attn)
    first_norm = normed * attn_gain + attn_shift
    inner_pre = matmul_low(first_norm.astype(jnp.bfloat16), inner_weight) + inner_bias
    active_low = jax.nn.gelu(inner_pre, approximate=False).astype(jnp.bfloat16)
    sum_ffn = first_norm + matmul_low(active_low, outer_weight) + outer_bias
    normed_two, inverse_two = normalize(sum_ffn)
    result = normed_two * ffn_gain + ffn_shift
    result = jnp.where(drop_flag > 0, layer_input.astype(jnp.float32), result)
    kept_items = (
        layer_input,
        query_low,
        key_local,
        value_local,
        attended,
        log_total,
        sum_attn,
        inner_pre,
        sum_ffn,
    ) + gathered
    return (result, kept_items)


def layer_backward(grad_out, kept_items, params, seg_query):
    (
        qkv_weight,
        query_bias,
        value_bias,
        attn_weight,
        attn_bias,
        attn_gain,
        attn_shift,
        inner_weight,
        inner_bias,
        outer_weight,
        outer_bias,
        ffn_gain,
        ffn_shift,
    ) = params
    (
        layer_input,
        query_low,
        key_local,
        value_local,
        attended,
        log_total,
        sum_attn,
        inner_pre,
        sum_ffn,
    ) = kept_items[:9]
    model_width = layer_input.shape[1]
    row_count = layer_input.shape[0]
    normed, inverse = normalize(sum_attn)
    first_norm = normed * attn_gain + attn_shift
    normed_two, inverse_two = normalize(sum_ffn)
    grad_ffn_gain = jnp.sum(grad_out * normed_two, axis=0)
    grad_ffn_shift = jnp.sum(grad_out, axis=0)
    grad_sum_ffn = norm_back(grad_out, normed_two, inverse_two, ffn_gain)
    grad_ffn_low = grad_sum_ffn.astype(jnp.bfloat16)
    active, gelu_pull = jax.vjp(partial(jax.nn.gelu, approximate=False), inner_pre)
    grad_outer_weight = left_product(active.astype(jnp.bfloat16), grad_ffn_low)
    grad_outer_bias = jnp.sum(grad_ffn_low.astype(jnp.float32), axis=0)
    grad_active = right_product(grad_ffn_low, outer_weight)
    grad_inner = gelu_pull(grad_active)[0].astype(jnp.bfloat16)
    grad_inner_weight = left_product(first_norm.astype(jnp.bfloat16), grad_inner)
    grad_inner_bias = jnp.sum(grad_inner.astype(jnp.float32), axis=0)
    grad_first = grad_sum_ffn + right_product(grad_inner, inner_weight)
    grad_attn_gain = jnp.sum(grad_first * normed, axis=0)
    grad_attn_shift = jnp.sum(grad_first, axis=0)
    grad_sum_attn = norm_back(grad_first, normed, inverse, attn_gain)
    grad_branch = grad_sum_attn.astype(jnp.bfloat16)
    grad_attn_weight = left_product(attended.astype(jnp.bfloat16), grad_branch)
    grad_attn_bias = jnp.sum(grad_branch.astype(jnp.float32), axis=0)
    grad_attended = right_product(grad_branch, attn_weight).astype(jnp.bfloat16)
    key_all, value_all, seg_all, pad_all = kept_items[9:]
    row_delta = jnp.sum(
        (grad_attended.astype(jnp.float32) * attended).reshape(row_count, HEADS, HEAD_DIM), axis=-1
    ).T
    grad_query, grad_key_all, grad_value_all = attention_back(
        query_low,
        key_all,
        value_all,
        seg_query,
        seg_all,
        pad_all,
        log_total,
        row_delta,
        grad_attended,
    )
    grad_key, grad_value = (
        lax.psum_scatter(
            grad_key_all.astype(jnp.bfloat16), "ctx", scatter_dimension=0, tiled=True
        ).astype(jnp.float32),
        lax.psum_scatter(
            grad_value_all.astype(jnp.bfloat16), "ctx", scatter_dimension=0, tiled=True
        ).astype(jnp.float32),
    )
    grad_qkv = jnp.concatenate([grad_query, grad_key, grad_value], axis=1).astype(jnp.bfloat16)
    grad_qkv_weight = left_product(layer_input, grad_qkv)
    grad_query_bias = jnp.sum(grad_qkv[:, :model_width].astype(jnp.float32), axis=0)
    grad_value_bias = jnp.sum(grad_qkv[:, 2 * model_width :].astype(jnp.float32), axis=0)
    grad_input = grad_sum_attn + right_product(grad_qkv, qkv_weight)
    layer_grads = (
        grad_qkv_weight,
        grad_query_bias,
        grad_value_bias,
        grad_attn_weight,
        grad_attn_bias,
        grad_attn_gain,
        grad_attn_shift,
        grad_inner_weight,
        grad_inner_bias,
        grad_outer_weight,
        grad_outer_bias,
        grad_ffn_gain,
        grad_ffn_shift,
    )
    return (layer_grads, grad_input)


def body(
    tokens,
    segment_ids,
    padding,
    dropped,
    qkv_weight,
    query_bias,
    value_bias,
    attn_weight,
    attn_bias,
    attn_gain,
    attn_shift,
    inner_weight,
    inner_bias,
    outer_weight,
    outer_bias,
    ffn_gain,
    ffn_shift,
    cotangent,
):
    micro_count = tokens.shape[0]
    section_index = lax.axis_index("section")
    half_width = tokens.shape[2] // lax.axis_size("section")
    params = tuple(
        (
            member[0]
            for member in (
                qkv_weight,
                query_bias,
                value_bias,
                attn_weight,
                attn_bias,
                attn_gain,
                attn_shift,
                inner_weight,
                inner_bias,
                outer_weight,
                outer_bias,
                ffn_gain,
                ffn_shift,
            )
        )
    )
    drop_row = dropped[0]
    incoming = jnp.zeros(tokens.shape[1:], jnp.bfloat16)
    saved_ticks = []
    encoded_rows = []
    for tick_index in range(micro_count + 1):
        micro_index = jnp.clip(tick_index - section_index, 0, micro_count - 1)
        own_input = lax.dynamic_index_in_dim(tokens, micro_index, 0, False)
        layer_input = jnp.where(section_index == 0, own_input, incoming)
        seg_query = lax.dynamic_index_in_dim(segment_ids, micro_index, 0, False)
        pad_query = lax.dynamic_index_in_dim(padding, micro_index, 0, False)
        drop_flag = lax.dynamic_index_in_dim(drop_row, micro_index, 0, False)
        layer_out, kept_items = layer_forward(layer_input, params, seg_query, pad_query, drop_flag)
        layer_low = layer_out.astype(jnp.bfloat16)
        received = shifted(layer_low, "section", 1)
        incoming = received
        if tick_index >= 1:
            encoded_rows.append(jnp.where(section_index == 0, received, layer_low))
        saved_ticks.append(kept_items)
    stacked = jax.tree.map(lambda *members: jnp.stack(members), *saved_ticks)
    grad_totals = tuple((jnp.zeros(member.shape, jnp.float32) for member in params))
    grad_incoming = jnp.zeros(tokens.shape[1:], jnp.bfloat16)
    input_rows = []
    for tick_index in range(micro_count + 1):
        raw_index = tick_index - 1 + section_index
        micro_index = jnp.clip(raw_index, 0, micro_count - 1)
        live_tick = ((raw_index >= 0) & (raw_index < micro_count)).astype(jnp.float32)
        forward_tick = jnp.clip(tick_index - 1 + 2 * section_index, 0, micro_count)
        kept_items = jax.tree.map(
            lambda member: lax.dynamic_index_in_dim(member, forward_tick, 0, False), stacked
        )
        own_cot = lax.dynamic_index_in_dim(cotangent, micro_index, 0, False)
        upstream = jnp.where(section_index == 1, own_cot, grad_incoming).astype(jnp.float32)
        seg_query = lax.dynamic_index_in_dim(segment_ids, micro_index, 0, False)
        pad_query = lax.dynamic_index_in_dim(padding, micro_index, 0, False)
        drop_flag = lax.dynamic_index_in_dim(drop_row, micro_index, 0, False)
        keep_scale = (drop_flag == 0).astype(jnp.float32) * live_tick
        layer_grads, grad_input = layer_backward(
            upstream * keep_scale, kept_items, params, seg_query
        )
        grad_totals = tuple((total + term for total, term in zip(grad_totals, layer_grads)))
        grad_input = grad_input + (drop_flag > 0).astype(jnp.float32) * upstream
        grad_low = grad_input.astype(jnp.bfloat16)
        received = shifted(grad_low, "section", 1)
        grad_incoming = received
        if tick_index >= 1:
            input_rows.append(jnp.where(section_index == 0, grad_low, received))
    reduced_once = (
        lax.psum_scatter(
            grad_totals[0][None].astype(jnp.bfloat16), "dp", scatter_dimension=1, tiled=True
        ).astype(jnp.float32),
        lax.psum_scatter(
            grad_totals[3][None].astype(jnp.bfloat16), "dp", scatter_dimension=1, tiled=True
        ).astype(jnp.float32),
        lax.psum_scatter(
            grad_totals[7][None].astype(jnp.bfloat16), "dp", scatter_dimension=1, tiled=True
        ).astype(jnp.float32),
        lax.psum_scatter(
            grad_totals[9][None].astype(jnp.bfloat16), "dp", scatter_dimension=1, tiled=True
        ).astype(jnp.float32),
    )
    matrix_grads = (
        lax.psum_scatter(
            reduced_once[0].astype(jnp.bfloat16), "ctx", scatter_dimension=2, tiled=True
        ).astype(jnp.float32),
        lax.psum_scatter(
            reduced_once[1].astype(jnp.bfloat16), "ctx", scatter_dimension=2, tiled=True
        ).astype(jnp.float32),
        lax.psum_scatter(
            reduced_once[2].astype(jnp.bfloat16), "ctx", scatter_dimension=2, tiled=True
        ).astype(jnp.float32),
        lax.psum_scatter(
            reduced_once[3].astype(jnp.bfloat16), "ctx", scatter_dimension=2, tiled=True
        ).astype(jnp.float32),
    )
    vector_grads = lax.psum(
        (
            grad_totals[1][None],
            grad_totals[2][None],
            grad_totals[4][None],
            grad_totals[5][None],
            grad_totals[6][None],
            grad_totals[8][None],
            grad_totals[10][None],
            grad_totals[11][None],
            grad_totals[12][None],
        ),
        ("dp", "ctx"),
    )
    encoded = lax.dynamic_slice_in_dim(
        jnp.stack(encoded_rows), section_index * half_width, half_width, 2
    )
    tokens_grad = lax.dynamic_slice_in_dim(
        jnp.stack(input_rows), section_index * half_width, half_width, 2
    )
    return (
        encoded,
        tokens_grad,
        matrix_grads[0],
        vector_grads[0],
        vector_grads[1],
        matrix_grads[1],
        vector_grads[2],
        vector_grads[3],
        vector_grads[4],
        matrix_grads[2],
        vector_grads[5],
        matrix_grads[3],
        vector_grads[6],
        vector_grads[7],
        vector_grads[8],
    )


def dot_plain(left, right):
    return lax.dot_general(left, right, (((1,), (0,)), ((), ())), preferred_element_type=jnp.float32)


def dot_flipped(left, right):
    return lax.dot_general(left, right, (((1,), (1,)), ((), ())), preferred_element_type=jnp.float32)


def dot_leading(left, right):
    return lax.dot_general(left, right, (((0,), (0,)), ((), ())), preferred_element_type=jnp.float32)


def gelu_parts(x):
    below = 0.5 * (1.0 + lax.erf(x * 0.7071067811865476))
    density = jnp.exp(-0.5 * x * x) * 0.3989422804014327
    return (x * below, below + x * density)


def rows_of(index, size):
    return pl.ds(pl.multiple_of(index * size, size), size)


def piece_rows(ctx, at, count, n_pieces):
    return pl.ds(0, count) if n_pieces == 1 else rows_of(ctx ^ at, count)


def head_lanes(shape, which):
    lane = lax.broadcasted_iota(jnp.int32, shape, 1)
    return (lane < HEAD_DIM) if which == 0 else (lane >= HEAD_DIM)


def copy_list(pairs, sems, first=0):
    copies = [pltpu.make_async_copy(src, dst, sems.at[first + at]) for at, (src, dst) in enumerate(pairs)]
    for copy in copies:
        copy.start()
    return copies


def wait_all(copies):
    for copy in copies:
        copy.wait()


low, full = jnp.bfloat16, jnp.float32


def kernel_call(body, operands, outs, scratch, mib, aliases=None):
    spaces = {"a": pl.ANY, "s": pltpu.SMEM, "v": pltpu.VMEM, "h": pltpu.HBM, "c": pltpu.VMEM}
    members = []
    for space, array in operands:
        if space in "vh":
            array = pltpu.with_memory_space_constraint(array, spaces[space])
        members.append(array)
    return pl.pallas_call(
        body,
        out_shape=[spaces[space](shape, kind) for space, shape, kind in outs],
        in_specs=[pl.BlockSpec(memory_space=spaces[space]) for space, _ in operands],
        out_specs=[pl.BlockSpec(memory_space=spaces[space]) for space, _, _ in outs],
        scratch_shapes=scratch,
        input_output_aliases=aliases or {},
        compiler_params=pltpu.CompilerParams(vmem_limit_bytes=mib * 2**20),
    )(*members)


class Outgoing:
    def __init__(self, sems):
        self.sems, self.copies = sems, []

    def send(self, src, dst):
        copy = pltpu.make_async_copy(src, dst, self.sems.at[len(self.copies)])
        copy.start()
        self.copies.append(copy)

    def finish(self):
        wait_all(self.copies)


def scratch_like(shapes):
    return [pltpu.VMEM(shape, kind) for _, shape, kind in shapes]


def in_pairs(count, step):
    def both_steps(at, carry):
        for which in range(UNROLL):
            step(UNROLL * at + which)
        return carry

    lax.fori_loop(0, count // UNROLL, both_steps, 0)


UNROLL = 2


documents = 5


def forward_kernel(active, n_pieces, n_cot, n_alias, scal, qkv_bias_ref, qkv_scale_ref, vec_ref, inner_bias_ref, *refs):
    pieces, refs = refs[:n_pieces], refs[n_pieces:]
    cot_pieces, refs = refs[:n_cot], refs[n_cot:]
    weights_h, refs = refs[:4], refs[4 + n_alias :]
    n_outs = 16 if n_cot else 12
    outs_h, outs, (wqkv, wattn, win, wout, first, code_rows, ids, in_sems, out_sems) = (
        refs[:n_outs],
        refs[n_outs : 2 * n_outs],
        refs[2 * n_outs :],
    )
    u, qkv, att, lse, n1, r1, dg, n2, r2, first_low, res, feats = outs[:12]
    top = outs[12:]
    size, width = u.shape

    @pl.when(scal[0] == active)
    def _():
        loads = [
            pltpu.make_async_copy(src, dst, in_sems.at[at])
            for at, (src, dst) in enumerate(zip(weights_h, (wqkv, wattn, win, wout)))
        ]
        loads[0].start()
        out = Outgoing(out_sems)

        def save(*places):
            for place in places:
                out.send(outs[place], outs_h[place])

        count = size // 4
        if n_pieces == 1:
            u[...] = pieces[0][:size]
            ids[...] = pieces[0][size:, :size].astype(full)[:8]
        else:
            for at, piece in enumerate(pieces):
                place = rows_of(scal[1] ^ at, count)
                u[place, :] = piece[:count]
                ids[:, place] = piece[count:, :count].astype(full)[:8]
        lane = lax.broadcasted_iota(jnp.int32, (size, 128), 1)
        lane = jnp.where(lane < HEAD_DIM, lane, lane - HEAD_DIM).astype(full)
        for which in range(2):
            for at in range(4):
                place = slice(at * count, (at + 1) * count)
                code_rows[place, :] = jnp.broadcast_to(ids[which : which + 1, place], (count, count)).T
            if which == 0:
                differs = (lane < documents) & (code_rows[...] != lane)
                feats[0] = jnp.where(differs | (lane == documents), masked_score, 0.0).astype(low)
            else:
                padded = (lane == documents) & (code_rows[...] < 0)
                feats[1] = jnp.where(padded | (code_rows[...] == lane), 1.0, 0.0).astype(low)
        loads[0].wait()
        loads[1].start()
        loads[2].start()
        save(0, 11)
        value = dot_plain(u[...], wqkv[...]) + qkv_bias_ref[...]
        qkv[...] = (value * qkv_scale_ref[...]).astype(low)
        save(1)
        def heads(pair):
            query, key, value = (qkv[:, rows_of(pair + part * (width // 128), 128)] for part in range(3))
            sides = []
            for which in range(2):
                own = head_lanes(key.shape, which)
                scores = dot_flipped(jnp.where(own, key, feats[1]), jnp.where(own, query, feats[0]))
                top_score = jnp.max(scores, axis=0, keepdims=True)
                weights = jnp.exp(scores - top_score)
                total = jnp.sum(weights, axis=0, keepdims=True)
                head = 2 * pair + which
                lse[pl.ds(head, 1), :] = top_score + jnp.log(total)
                sides.append(dot_leading((weights * (1.0 / total)).astype(low), value))
            att[:, rows_of(pair, 128)] = jnp.where(head_lanes((size, 128), 0), sides[0], sides[1]).astype(low)

        in_pairs(width // 128, heads)
        save(2, 3)
        loads[1].wait()
        value = dot_plain(att[...], wattn[...]) + u[...].astype(full) + vec_ref[0:1, :]
        normed, inverse = normalize(value)
        n1[...] = normed.astype(low)
        r1[...] = jnp.broadcast_to(inverse, r1.shape)
        value = normed * vec_ref[1:2, :] + vec_ref[2:3, :]
        first[...] = value + vec_ref[3:4, :]
        first_low[...] = value.astype(low)
        save(9, 4, 5)
        loads[2].wait()
        loads[3].start()
        inner = dot_plain(first_low[...], win[...]) + inner_bias_ref[...]
        active_value, slope = gelu_parts(inner)
        dg[...] = slope.astype(low)
        save(6)
        loads[3].wait()
        normed, inverse = normalize(first[...] + dot_plain(active_value.astype(low), wout[...]))
        n2[...] = normed.astype(low)
        r2[...] = jnp.broadcast_to(inverse, r2.shape)
        value = normed * vec_ref[4:5, :] + vec_ref[5:6, :]
        res[:size] = jnp.where(scal[2] > 0, u[...], value.astype(low))
        res[size:, :size] = jnp.concatenate([ids[...], jnp.zeros_like(ids)], axis=0).astype(low)
        save(10)
        if n_cot:
            for at, piece in enumerate(cot_pieces):
                top[0][rows_of(scal[1] ^ at, count), :] = piece[...]
            top_of_backward(scal, vec_ref, normed, inverse, *top[:3])
            top[3][0] = first_low[...]
            top[3][1] = top[1][...]
            save(15, 13, 12, 14)
        else:
            save(7, 8)
        out.finish()


def top_of_backward(scal, vec_ref, normed, inverse, inc, dffn, vec):
    grad = inc[...].astype(full) * jnp.where(scal[2] > 0, 0.0, 1.0)
    value = norm_back(grad, normed, inverse, vec_ref[4:5, :])
    rounded = value.astype(low)
    dffn[...] = rounded
    vec[0:1, :] = column_sum(rounded.astype(full))
    vec[1:2, :] = column_sum(grad * normed)
    vec[2:3, :] = column_sum(grad)


def top_shapes(size, width):
    return [
        ("h", (size, width), low),
        ("h", (size, width), low),
        ("h", (8, width), full),
    ]


def run_forward(active, scal, small, pieces, cot_pieces, held, earlier, after):
    width, hidden = held[2].shape
    size = len(pieces) * (pieces[0].shape[0] - 16)
    outs = [
        ("h", (size, width), low),
        ("h", (size, 3 * width), low),
        ("h", (size, width), low),
        ("h", (16, size), full),
        ("h", (size, width), low),
        ("h", (size, 128), full),
        ("h", (size, hidden), low),
        ("h", (size, width), low),
        ("h", (size, 128), full),
        ("h", (size, width), low),
        ("h", (size + 16, width), low),
        ("h", (2, size, 128), low),
    ]
    if cot_pieces:
        outs += top_shapes(size, width) + [("h", (2, size, width), low)]
    operands = [("s", scal)] + [("c", member) for member in small]
    operands += [("c", member) for member in (*pieces, *cot_pieces)] + [("h", member) for member in held]
    at_alias = len(operands)
    operands += [(out[0], member) for out, member in zip(outs, earlier)] + [("c", member) for member in after]
    return kernel_call(
        partial(forward_kernel, active, len(pieces), len(cot_pieces), len(earlier) + len(after)),
        operands,
        outs,
        scratch_like(outs)
        + [pltpu.VMEM(member.shape, low) for member in held]
        + [
            pltpu.VMEM((size, width), full),
            pltpu.VMEM((size, size // 4), full),
            pltpu.VMEM((8, size), full),
            pltpu.SemaphoreType.DMA((4,)),
            pltpu.SemaphoreType.DMA((len(outs),)),
        ],
        48,
        {at_alias + i: i for i in range(len(earlier))},
    )


def column_sum(value):
    return jnp.sum(value, axis=0, keepdims=True)


def top_kernel(active, n_alias, n_after, scal, vec_ref, incoming, n2_h, r2_h, *refs):
    refs = refs[n_alias + n_after :]
    outs_h, outs, (n2, r2, in_sems, out_sems) = refs[:3], refs[3:6], refs[6:]

    @pl.when(scal[0] == active)
    def _():
        loads = copy_list([(n2_h, n2), (r2_h, r2)], in_sems)
        outs[0][...] = incoming[...]
        wait_all(loads)
        top_of_backward(scal, vec_ref, n2[...].astype(full), r2[:, :1], *outs)
        wait_all(copy_list(list(zip(outs, outs_h)), out_sems))


def run_top(active, scal, vecs, incoming, n2, r2, earlier, after):
    size, width = n2.shape
    outs = top_shapes(size, width)
    operands = [("s", scal), ("c", vecs), ("c", incoming)] + [("h", member) for member in (n2, r2)]
    at_alias = len(operands)
    operands += [(out[0], member) for out, member in zip(outs, earlier)] + list(after)
    return kernel_call(
        partial(top_kernel, active, len(earlier), len(after)),
        operands,
        outs,
        scratch_like(outs)
        + [
            pltpu.VMEM(n2.shape, low),
            pltpu.VMEM(r2.shape, full),
            pltpu.SemaphoreType.DMA((2,)),
            pltpu.SemaphoreType.DMA((3,)),
        ],
        16,
        {at_alias + i: i for i in range(len(earlier))},
    )


def chain_kernel(active, n_alias, n_after, scal, vec_ref, *refs):
    held_h, refs = refs[:12], refs[12 + n_alias + n_after :]
    outs_h, outs, held, (dinner, datt, first, in_sems, out_sems) = refs[:4], refs[4:8], refs[8:20], refs[20:]
    inc, dffn, dg, n1, r1, qkv, lse, wqkv, wattn, win, wout, feats = held
    dqkv, dbranch, vec, din = outs
    size, width = inc.shape
    hidden = win.shape[1]

    @pl.when(scal[0] == active)
    def _():
        chunks = hidden // width
        cuts = [slice(at * width, (at + 1) * width) for at in range(chunks)]
        order = [(held_h[1], dffn)]
        for cut in cuts:
            order += [(held_h[10].at[cut, :], wout.at[cut, :]), (held_h[2].at[:, cut], dg.at[:, cut])]
        order += [(held_h[at], held[at]) for at in (9, 3, 4, 8, 5, 6, 11, 7, 0)]
        loads = [pltpu.make_async_copy(src, dst, in_sems.at[at]) for at, (src, dst) in enumerate(order)]

        def begin(first_copy, last_copy):
            for copy in loads[first_copy:last_copy]:
                copy.start()

        begin(0, 5)
        out = Outgoing(out_sems)
        for at, cut in enumerate(cuts):
            wait_all(loads[: 3] if at == 0 else loads[2 * at + 1 : 2 * at + 3])
            begin(2 * at + 5, 2 * at + 7)
            value = (dot_flipped(dffn[...], wout[cut, :]) * dg[:, cut].astype(full)).astype(low)
            dinner[:, cut] = value
            vec[8 + at : 9 + at, :] = column_sum(value.astype(full))
        begin(2 * chunks + 5, len(loads))
        loads = loads[2 * chunks + 1 :]
        wait_all(loads[:3])
        grad = dot_flipped(dinner[...], win[...]) + dffn[...].astype(full)
        normed = n1[...].astype(full)
        value = norm_back(grad, normed, r1[:, :1], vec_ref[1:2, :])
        first[...] = value
        rounded = value.astype(low)
        dbranch[...] = rounded
        vec[2:3, :] = column_sum(rounded.astype(full))
        vec[3:4, :] = column_sum(grad * normed)
        vec[4:5, :] = column_sum(grad)
        out.send(dbranch, outs_h[1])
        loads[3].wait()
        datt[...] = dot_flipped(dbranch[...], wattn[...]).astype(low)
        wait_all(loads[4:7])
        def heads(pair):
            cols = [rows_of(pair + part * (width // 128), 128) for part in range(3)]
            query, key, value = (qkv[:, col] for col in cols)
            grad = datt[:, cols[0]]
            parts = []
            for which in range(2):
                own = head_lanes(key.shape, which)
                scores = dot_flipped(jnp.where(own, key, feats[1]), jnp.where(own, query, feats[0]))
                value_own = jnp.where(own, value, jnp.zeros_like(value))
                head = 2 * pair + which
                probs = jnp.exp(scores - lse[pl.ds(head, 1), :])
                dprobs = dot_flipped(value_own, grad)
                delta = column_sum(probs * dprobs)
                dscores = (probs * (dprobs - delta)).astype(low)
                parts.append(
                    (dot_leading(dscores, key), dot_plain(dscores, query), dot_plain(probs.astype(low), grad))
                )
            low_lanes = head_lanes((size, 128), 0)
            dquery, dkey, dvalue = (jnp.where(low_lanes, one, two) for one, two in zip(*parts))
            dquery = (dquery * HEAD_DIM ** (-0.5)).astype(low)
            dvalue = dvalue.astype(low)
            dqkv[:, cols[0]] = dquery
            dqkv[:, cols[1]] = dkey.astype(low)
            dqkv[:, cols[2]] = dvalue
            vec[0:1, cols[0]] = column_sum(dquery.astype(full))
            vec[1:2, cols[0]] = column_sum(dvalue.astype(full))

        in_pairs(width // 128, heads)
        out.send(dqkv, outs_h[0])
        out.send(vec, outs_h[2])
        wait_all(loads[7:])
        value = first[...] + dot_flipped(dqkv[...], wqkv[...])
        din[...] = jnp.where(scal[2] > 0, inc[...], value.astype(low))
        out.send(din, outs_h[3])
        out.finish()


def run_chain(active, scal, vecs, top, kept, held, earlier, after):
    u, qkv, att, lse, n1, r1, dg = kept[:7]
    inc, dffn = top[:2]
    size, width = u.shape
    hidden = dg.shape[1]
    outs = [
        ("h", (size, 3 * width), low),
        ("h", (size, width), low),
        ("h", (16, width), full),
        ("h", (size, width), low),
    ]
    members = (inc, dffn, dg, n1, r1, qkv, lse, *held, kept[11])
    operands = [("s", scal), ("c", vecs)] + [("h", member) for member in members]
    at_alias = len(operands)
    operands += [(out[0], member) for out, member in zip(outs, earlier)]
    operands += list(after)
    return kernel_call(
        partial(chain_kernel, active, len(earlier), len(after)),
        operands,
        outs,
        scratch_like(outs)
        + [pltpu.VMEM(member.shape, member.dtype) for member in members]
        + [
            pltpu.VMEM((size, hidden), low),
            pltpu.VMEM((size, width), low),
            pltpu.VMEM((size, width), full),
            pltpu.SemaphoreType.DMA((2 * (hidden // width) + 10,)),
            pltpu.SemaphoreType.DMA((4,)),
        ],
        48,
        {at_alias + i: i for i in range(len(earlier))},
    )


def split_high(value):
    high = value.astype(low)
    return high, (value - high.astype(full)).astype(low)


def wide_pair(value, rows):
    pair = jnp.concatenate(split_high(value), axis=1)
    return jnp.concatenate([pair, jnp.zeros((rows - pair.shape[0], pair.shape[1]), low)], axis=0)


def joined(high, rest):
    return high.astype(full) + rest.astype(full)


def attn_grad_kernel(n_after, scal, top_vec, chain_vec, *refs):
    ins_h, refs = refs[:4], refs[4 + n_after :]
    send_a, keep_a, send_b, keep_b, vec = refs[:5]
    (u, att, dqkv, dbranch), out, pair, in_sems, sems = refs[5:9], *refs[9:]
    width = u.shape[1]
    dp = scal[3]
    bit_y, bit_x = dp // 2, dp % 2
    left, right = pl.ds(0, 2 * width), pl.ds(2 * width, 2 * width)
    each = width // 4
    loads = copy_list([(ins_h[at], (u, att, dqkv, dbranch)[at]) for at in (0, 2, 1, 3)], in_sems)
    sent = Outgoing(sems)
    value = jnp.concatenate([top_vec[...], chain_vec[...]], axis=0)
    vec[...] = value
    pair[...] = wide_pair(value, VEC_ROWS)
    sent.send(pair, send_a.at[pl.ds(2 * each, VEC_ROWS)])
    wait_all(loads[:2])
    flipped = u[...].T
    out[:, : 2 * width] = dot_plain(flipped, dqkv[:, : 2 * width]).astype(low)
    for at in range(2):
        sent.send(out.at[rows_of(2 * at + 1 - bit_x, each), left], send_a.at[pl.ds(at * each, each)])
        sent.send(out.at[rows_of(2 * at + bit_x, each), left], keep_a.at[at])
    out[:, 2 * width : 3 * width] = dot_plain(flipped, dqkv[:, 2 * width :]).astype(low)
    wait_all(loads[2:])
    out[:, 3 * width :] = dot_leading(att[...], dbranch[...]).astype(low)
    for at in range(2):
        sent.send(out.at[rows_of(2 * (1 - bit_y) + at, each), right], send_b.at[at])
        sent.send(out.at[rows_of(2 * bit_y + at, each), right], keep_b.at[at])
    sent.finish()


VEC_ROWS = 32


def run_attn_grad(scal, top_vec, chain_vec, u, att, dqkv, dbranch, after):
    width = u.shape[1]
    each = width // 4
    members = (u, att, dqkv, dbranch)
    half_shape = ("h", (2, each, 2 * width), low)
    return kernel_call(
        partial(attn_grad_kernel, len(after)),
        [("s", scal), ("c", top_vec), ("c", chain_vec)] + [("h", member) for member in members] + list(after),
        [("h", (2 * each + VEC_ROWS, 2 * width), low)] + [half_shape] * 3 + [("c", (24, width), full)],
        [pltpu.VMEM(member.shape, low) for member in members]
        + [
            pltpu.VMEM((width, 4 * width), low),
            pltpu.VMEM((VEC_ROWS, 2 * width), low),
            pltpu.SemaphoreType.DMA((4,)),
            pltpu.SemaphoreType.DMA((9,)),
        ],
        24,
    )


def ffn_grad_kernel(n_after, scal, inner_bias_ref, win_h, wout_h, first_h, dffn_h, *refs):
    from_one, firsts, dffns = refs[:3], refs[3:6], refs[6:9]
    send, keep, first, dffn, active, dinner, win, wout, out, sems = refs[9 + n_after :]
    size, width = dffn_h.shape
    own = rows_of(2 * (scal[3] % 2) + scal[1] % 2, width)
    loads = copy_list(
        [
            (first_h, first.at[:size]),
            (win_h.at[:, own], win),
            (dffn_h, dffn.at[:size]),
            (wout_h.at[own, :], wout),
        ],
        sems,
    )
    is_zero = scal[0] == 0
    for at in range(4):
        rows = slice(at * size, (at + 1) * size)
        if at == 0:
            wait_all(loads)
            value, grad = first[rows], dffn[rows]
        else:
            value = jnp.where(is_zero, firsts[at - 1][...], from_one[at - 1][0])
            grad = jnp.where(is_zero, dffns[at - 1][...], from_one[at - 1][1])
            first[rows] = value
            dffn[rows] = grad
        inner = dot_plain(value, win[...]) + inner_bias_ref[:, own]
        active_value, slope = gelu_parts(inner)
        active[rows] = active_value.astype(low)
        dinner[rows] = (dot_flipped(grad, wout[...]) * slope).astype(low)
    each = width // 4
    for half, (left, right) in enumerate(((first, dinner), (dffn, active))):
        part = dot_leading(left[...], right[...]).astype(low)
        for block in range(4):
            source = block if half == 0 else 2 * (block % 2) + block // 2
            out[block, each * half : each * (half + 1)] = part[each * source : each * (source + 1)]
    bit = scal[3] // 2
    wait_all(
        copy_list(
            [(out.at[2 * (1 - bit) + at], send.at[at]) for at in range(2)]
            + [(out.at[2 * bit + at], keep.at[at]) for at in range(2)],
            sems,
        )
    )


def run_ffn_grad(scal, inner_bias, win, wout, first_own, dffn_own, from_one, firsts, dffns, after):
    size, width = dffn_own.shape
    return kernel_call(
        partial(ffn_grad_kernel, len(after)),
        [("s", scal), ("c", inner_bias)]
        + [("h", member) for member in (win, wout, first_own, dffn_own)]
        + [("c", member) for member in (*from_one, *firsts, *dffns)]
        + list(after),
        [("h", (2, width // 2, width), low)] * 2,
        [pltpu.VMEM((4 * size, width), low) for _ in range(4)]
        + [pltpu.VMEM((width, width), low), pltpu.VMEM((width, width), low)]
        + [pltpu.VMEM((4, width // 2, width), low), pltpu.SemaphoreType.DMA((4,))],
        32,
    )


def merge_kernel(scal, got_a, keep_a, got_b, keep_b, vec, send_a, left_a, send_b, left_b, vec_out):
    bit_y, bit_x = scal[3] // 2, scal[3] % 2
    each, width = keep_a.shape[1], vec.shape[1]
    send_a[:each] = added(got_a[rows_of(1 - bit_y, each)], keep_a[1 - bit_y])
    left_a[...] = added(got_a[rows_of(bit_y, each)], keep_a[bit_y])
    send_b[...] = added(got_b[1 - bit_x], keep_b[1 - bit_x])
    left_b[...] = added(got_b[bit_x], keep_b[bit_x])
    pair = got_a[2 * each :]
    value = vec[...] + joined(pair[:24, :width], pair[:24, width:])
    vec_out[...] = value
    send_a[each:] = wide_pair(value, VEC_ROWS)


def turn_kernel(scal, got_a, keep_a, got_b, keep_b, vec, send, keep, vec_out, rows, blocks):
    each, cut = keep_a.shape
    rows[:, :cut] = added(got_a[:each], keep_a[...])
    rows[:, cut:] = added(got_b[...], keep_b[...])
    width = cut // 2
    wide, narrow = 3 * width // 4, width // 4
    for at in range(4):
        blocks[at, :, :wide] = rows[:, wide * at : wide * (at + 1)]
        blocks[at, :, wide:] = rows[:, 3 * width + narrow * at : 3 * width + narrow * (at + 1)]
    bit = scal[1] % 2
    for at in range(2):
        send[at * each : (at + 1) * each] = blocks[2 * at + 1 - bit]
        keep[at] = blocks[2 * at + bit]
    pair = got_a[each:]
    value = vec[...] + joined(pair[:24, :width], pair[:24, width:])
    vec_out[...] = value
    send[2 * each :] = jnp.concatenate(split_high(value), axis=0)


def last_kernel(scal, got, keep, vec, send, left, vec_out):
    bit = scal[1] // 2
    each = keep.shape[1]
    send[:each] = added(got[rows_of(1 - bit, each)], keep[1 - bit])
    left[...] = added(got[rows_of(bit, each)], keep[bit])
    pair = got[2 * each :]
    value = vec[...] + joined(pair[:24], pair[24:])
    vec_out[...] = value
    send[each:] = jnp.concatenate(split_high(value), axis=0)


def end_kernel(scal, got, keep, vec, qkv_out, attn_out, vec_out):
    each = keep.shape[0]
    value = got[:each].astype(full) + keep[...].astype(full)
    qkv_out[...] = value[:, : 3 * each]
    attn_out[...] = value[:, 3 * each :]
    pair = got[each:]
    vec_out[...] = vec[...] + joined(pair[:24], pair[24:])


def half_kernel(scal, got, keep, send, left):
    bit = scal[1] // 2
    send[...] = added(got[1 - bit], keep[1 - bit])
    left[...] = added(got[bit], keep[bit])


def swapped(x, axis, by):
    return lax.ppermute(x, axis, [(i, i ^ by) for i in range(lax.axis_size(axis))])


def near(section, x, by):
    pairs = [
        (16 * section + 4 * i + j, 16 * section + 4 * (i ^ (by & 1)) + (j ^ (by >> 1)))
        for i in range(4)
        for j in range(4)
    ]
    return lax.ppermute(x, ("section", "dp", "ctx"), pairs)


def moved(x, target):
    pairs = [(16 * s + 4 * i + j, 16 * s + target(i, j)) for s in range(2) for i in range(4) for j in range(4)]
    return lax.ppermute(x, ("section", "dp", "ctx"), pairs)


def swapped_in(section, x, axis, by):
    length = lax.axis_size(axis)
    pairs = [(section * length + i, section * length + (i ^ by)) for i in range(length)]
    return lax.ppermute(x, ("section", axis), pairs)


def pick(x, at, dim=0):
    return lax.dynamic_index_in_dim(x, at, dim, False)


def added(one, two):
    return (one.astype(full) + two.astype(full)).astype(low)


def spread(row_half, ctx, swap):
    length = lax.axis_size("ctx")
    size, width = row_half.shape
    parts = row_half.reshape(length, size // length, width)
    out = jnp.zeros(parts.shape, parts.dtype)
    out = lax.dynamic_update_index_in_dim(out, pick(parts, ctx), ctx, 0)
    for k in range(1, length):
        out = lax.dynamic_update_index_in_dim(out, swap(pick(parts, ctx ^ k), "ctx", k), ctx ^ k, 0)
    return out


def to_section(x, section):
    return lax.ppermute(x, "section", [(1 - section, section)])


def following(body, n_operands, n_after, *refs):
    body(*refs[:n_operands], *refs[n_operands + n_after :])


def merged(body, scal, operands, outs, scratch=(), after=()):
    return kernel_call(
        partial(following, body, 1 + len(operands), len(after)),
        [("s", scal)] + [("c", member) for member in operands] + [("a", member) for member in after],
        [("c", shape, kind) for shape, kind in outs],
        list(scratch),
        16,
    )


def row_body(
    tokens,
    segment_ids,
    padding,
    dropped,
    qkv_weight,
    query_bias,
    value_bias,
    attn_weight,
    attn_bias,
    attn_gain,
    attn_shift,
    inner_weight,
    inner_bias,
    outer_weight,
    outer_bias,
    ffn_gain,
    ffn_shift,
    cotangent,
):
    width = tokens.shape[2]
    half, each = width // 2, width // 4
    count = tokens.shape[1]
    section, dp, ctx = (lax.axis_index(name) for name in ("section", "dp", "ctx"))
    weights = (qkv_weight[0], attn_weight[0], inner_weight[0], outer_weight[0])
    vecs = jnp.concatenate(
        [attn_bias, attn_gain, attn_shift, outer_bias, ffn_gain, ffn_shift, query_bias, value_bias]
    )
    qkv_bias = jnp.concatenate([query_bias, jnp.zeros_like(query_bias), value_bias], axis=1)
    qkv_scale = jnp.concatenate(
        [jnp.full((1, width), HEAD_DIM ** (-0.5), jnp.float32), jnp.ones((1, 2 * width), jnp.float32)], axis=1
    )
    small = (qkv_bias, qkv_scale, vecs, inner_bias)
    scal = jnp.stack([section, ctx, pick(dropped[0], ctx), dp]).astype(jnp.int32)

    ids = jnp.stack([segment_ids, jnp.where(padding == 1, segment_ids, -1)], axis=1).astype(low)
    ids = jnp.pad(ids, ((0, 0), (0, 14), (0, width - count)))
    sent = jnp.concatenate([tokens, ids], axis=1)
    far = {k: swapped_in(0, pick(sent, ctx ^ k), "ctx", k) for k in (2, 3, 1)}
    own_tokens = [pick(sent, ctx), far[1], far[2], far[3]]
    held = weights
    own_cot = [pick(cotangent, ctx)] + [swapped_in(1, pick(cotangent, ctx ^ k), "ctx", k) for k in range(1, 4)]

    kept = run_forward(0, scal, small, own_tokens, [], held, [], [])
    middle = lax.ppermute(kept[10], "section", [(0, 1)])
    firsts = [near(0, kept[9], k) for k in range(1, 4)]
    made = run_forward(1, scal, small, [middle], own_cot, held, kept, firsts)
    kept, top, both = made[:12], made[12:15], made[15]
    from_one = [near(1, both, k) for k in range(1, 4)]
    chain = run_chain(1, scal, vecs, top, kept, held, [], [])
    incoming = to_section(chain[3], 0)
    top = run_top(0, scal, vecs, incoming, kept[7], kept[8], top, [("c", member) for member in from_one])
    dffns = [near(0, top[1], k) for k in range(1, 4)]
    chain = run_chain(0, scal, vecs, top, kept, held, chain, [])
    dqkv, dbranch, chain_vec, d_input = chain
    result = kept[10][: 4 * count]

    send_a, keep_a, send_b, keep_b, vec = run_attn_grad(
        scal, top[2], chain_vec, kept[0], kept[2], dqkv, dbranch, []
    )
    got_a, got_b = swapped(send_a, "dp", 1), swapped(send_b, "dp", 2)
    ffn_send, ffn_keep = run_ffn_grad(
        scal, inner_bias, held[2], held[3], kept[9], top[1], from_one, firsts, dffns, [("h", keep_b)]
    )
    ffn_got = swapped(ffn_send, "dp", 2)
    wide, block, flat = (each, 2 * width), (each, width), ((24, width), full)
    send_a, keep_a, send_b, keep_b, vec = merged(
        merge_kernel,
        scal,
        (got_a, keep_a, got_b, keep_b, vec),
        [((each + VEC_ROWS, 2 * width), low), (wide, low), (wide, low), (wide, low), flat],
        after=[ffn_keep],
    )
    got_a, got_b = swapped(send_a, "dp", 2), swapped(send_b, "dp", 1)
    ffn_send, ffn_keep = merged(
        half_kernel, scal, (ffn_got, ffn_keep), [(ffn_keep.shape[1:], low)] * 2, after=[send_b]
    )
    ffn_got = swapped(ffn_send, "ctx", 2)
    rows = jnp.where(section == 0, d_input, result)
    rows, ffn_keep = lax.optimization_barrier((rows, ffn_keep))
    rows = spread(rows, ctx, swapped)
    send, keep, vec = merged(
        turn_kernel,
        scal,
        (got_a, keep_a, got_b, keep_b, vec),
        [((2 * each + 48, width), low), ((2, each, width), low), flat],
        [pltpu.VMEM((each, 4 * width), low), pltpu.VMEM((4, each, width), low)],
        after=[ffn_keep],
    )
    got = swapped(send, "ctx", 1)
    send, keep, vec = merged(last_kernel, scal, (got, keep, vec), [((each + 48, width), low), (block, low), flat])
    got = swapped(send, "ctx", 2)
    qkv_grad, attn_grad, vec = merged(
        end_kernel, scal, (got, keep, vec), [((each, 3 * each), full), ((each, each), full), flat]
    )
    ffn_rows = added(ffn_got, ffn_keep)
    inner_grad = moved(ffn_rows[:each], lambda i, j: 4 * (2 * (i // 2) + j // 2) + 2 * (i % 2) + j % 2).astype(full)
    outer_grad = moved(ffn_rows[each:], lambda i, j: 4 * (2 * (i % 2) + j % 2) + 2 * (j // 2) + i // 2).astype(full).T
    rows, vec = lax.optimization_barrier((rows, vec))
    other_half = swapped(jnp.where(section == 0, rows[..., half:], rows[..., :half]), "section", 1)
    tokens_grad = jnp.where(section == 0, rows[..., :half], other_half)
    encoded = jnp.where(section == 0, other_half, rows[..., half:])
    return (
        encoded,
        tokens_grad,
        qkv_grad[None],
        vec[8:9],
        vec[9:10],
        attn_grad[None],
        vec[10:11],
        vec[11:12],
        vec[12:13],
        inner_grad[None],
        vec[16 : 16 + inner_bias.shape[1] // width].reshape(1, -1),
        outer_grad[None],
        vec[0:1],
        vec[1:2],
        vec[2:3],
    )


def solution(mesh):
    placed = (
        P("dp", "ctx", None),
        P("dp", "ctx"),
        P("dp", "ctx"),
        P("section", "dp"),
        P("section", None, None),
        P("section", None),
        P("section", None),
        P("section", None, None),
        P("section", None),
        P("section", None),
        P("section", None),
        P("section", None, None),
        P("section", None),
        P("section", None, None),
        P("section", None),
        P("section", None),
        P("section", None),
        P("dp", "ctx", None),
    )

    def dispatch(*members):
        rows = members[0].shape[0]
        same = rows == lax.axis_size("ctx") == lax.axis_size("dp") == 4
        return (row_body if same else body)(*members)

    return jax.shard_map(
        dispatch,
        mesh=mesh,
        in_specs=placed,
        out_specs=(
            P("dp", "ctx", "section"),
            P("dp", "ctx", "section"),
            P("section", "dp", "ctx"),
            P("section", None),
            P("section", None),
            P("section", "dp", "ctx"),
            P("section", None),
            P("section", None),
            P("section", None),
            P("section", "dp", "ctx"),
            P("section", None),
            P("section", "dp", "ctx"),
            P("section", None),
            P("section", None),
            P("section", None),
        ),
        check_vma=False,
    )
```

```python
from functools import partial

import jax
import jax.numpy as jnp
from jax import lax
from jax.experimental import pallas as pl
from jax.experimental.pallas import tpu as pltpu
from jax.sharding import PartitionSpec as P

HEADS = 12
HEAD_DIM = 64


norm_eps = 1e-05
masked_score = -1e30


def shifted(x, axis, by):
    length = lax.axis_size(axis)
    return lax.ppermute(x, axis, [(i, (i + by) % length) for i in range(length)])


def matmul_low(left, right):
    return jnp.dot(left, right, preferred_element_type=jnp.float32)


def left_product(left, right):
    return jnp.einsum("ti,to->io", left, right, preferred_element_type=jnp.float32)


def right_product(left, right):
    return jnp.einsum("to,io->ti", left, right, preferred_element_type=jnp.float32)


def normalize(values):
    mean_value = jnp.mean(values, axis=-1, keepdims=True)
    centered = values - mean_value
    variance = jnp.mean(centered * centered, axis=-1, keepdims=True)
    inverse = lax.rsqrt(variance + norm_eps)
    return (centered * inverse, inverse)


def norm_back(grad_out, normed, inverse, gain):
    scaled = grad_out * gain
    return inverse * (
        scaled
        - jnp.mean(scaled, axis=-1, keepdims=True)
        - normed * jnp.mean(scaled * normed, axis=-1, keepdims=True)
    )


def attend_piece(query_heads, seg_query, running, pieces):
    run_max, run_total, run_acc = running
    key_piece, value_piece, seg_piece, pad_piece = pieces
    count = key_piece.shape[0]
    key_heads = key_piece.reshape(count, HEADS, HEAD_DIM)
    value_heads = value_piece.reshape(count, HEADS, HEAD_DIM)
    scores = jnp.einsum(
        "qhd,khd->hqk", query_heads, key_heads, preferred_element_type=jnp.float32
    ) * HEAD_DIM ** (-0.5)
    allowed = (seg_query[:, None] == seg_piece[None, :]) & (pad_piece[None, :] == 1)
    scores = jnp.where(allowed[None], scores, masked_score)
    new_max = jnp.maximum(run_max, jnp.max(scores, axis=-1))
    weights = jnp.where(allowed[None], jnp.exp(scores - new_max[..., None]), 0.0)
    run_total = jnp.sum(weights, axis=-1)
    run_acc = jnp.einsum(
        "hqk,khd->hqd",
        weights.astype(jnp.bfloat16),
        value_heads,
        preferred_element_type=jnp.float32,
    )
    return (new_max, run_total, run_acc)


def attention_back(
    query_low, key_all, value_all, seg_query, seg_all, pad_all, log_total, row_delta, grad_att
):
    row_count = query_low.shape[0]
    seq_count = key_all.shape[0]
    score_scale = HEAD_DIM ** (-0.5)
    query_heads = query_low.reshape(row_count, HEADS, HEAD_DIM)
    key_heads = key_all.reshape(seq_count, HEADS, HEAD_DIM)
    value_heads = value_all.reshape(seq_count, HEADS, HEAD_DIM)
    grad_heads = grad_att.reshape(row_count, HEADS, HEAD_DIM)
    scores = (
        jnp.einsum("qhd,khd->hqk", query_heads, key_heads, preferred_element_type=jnp.float32)
        * score_scale
    )
    allowed = (seg_query[:, None] == seg_all[None, :]) & (pad_all[None, :] == 1)
    prob_rows = jnp.where(allowed[None], jnp.exp(scores - log_total[..., None]), 0.0)
    grad_probs = jnp.einsum(
        "qhd,khd->hqk", grad_heads, value_heads, preferred_element_type=jnp.float32
    )
    grad_scores = (prob_rows * (grad_probs - row_delta[..., None])).astype(jnp.bfloat16)
    grad_query = (
        jnp.einsum("hqk,khd->qhd", grad_scores, key_heads, preferred_element_type=jnp.float32)
        * score_scale
    )
    grad_key = (
        jnp.einsum("hqk,qhd->khd", grad_scores, query_heads, preferred_element_type=jnp.float32)
        * score_scale
    )
    grad_value = jnp.einsum(
        "hqk,qhd->khd",
        prob_rows.astype(jnp.bfloat16),
        grad_heads,
        preferred_element_type=jnp.float32,
    )
    model_width = HEADS * HEAD_DIM
    return (
        grad_query.reshape(row_count, model_width),
        grad_key.reshape(seq_count, model_width),
        grad_value.reshape(seq_count, model_width),
    )


def layer_forward(layer_input, params, seg_query, pad_query, drop_flag):
    (
        qkv_weight,
        query_bias,
        value_bias,
        attn_weight,
        attn_bias,
        attn_gain,
        attn_shift,
        inner_weight,
        inner_bias,
        outer_weight,
        outer_bias,
        ffn_gain,
        ffn_shift,
    ) = params
    model_width = layer_input.shape[1]
    row_count = layer_input.shape[0]
    projected = matmul_low(layer_input, qkv_weight)
    query_low = (projected[:, :model_width] + query_bias).astype(jnp.bfloat16)
    key_local = projected[:, model_width : 2 * model_width].astype(jnp.bfloat16)
    value_local = (projected[:, 2 * model_width :] + value_bias).astype(jnp.bfloat16)
    query_heads = query_low.reshape(row_count, HEADS, HEAD_DIM)
    start_state = (
        jnp.full((HEADS, row_count), masked_score, jnp.float32),
        jnp.zeros((HEADS, row_count), jnp.float32),
        jnp.zeros((HEADS, row_count, HEAD_DIM), jnp.float32),
    )
    key_all, value_all, seg_all, pad_all = (
        lax.all_gather(key_local, "ctx", axis=0, tiled=True),
        lax.all_gather(value_local, "ctx", axis=0, tiled=True),
        lax.all_gather(seg_query, "ctx", axis=0, tiled=True),
        lax.all_gather(pad_query, "ctx", axis=0, tiled=True),
    )
    run_max, run_total, run_acc = attend_piece(
        query_heads, seg_query, start_state, (key_all, value_all, seg_all, pad_all)
    )
    gathered = (key_all, value_all, seg_all, pad_all)
    attended = (run_acc / run_total[..., None]).transpose(1, 0, 2).reshape(row_count, model_width)
    log_total = run_max + jnp.log(run_total)
    branch = matmul_low(attended.astype(jnp.bfloat16), attn_weight) + attn_bias
    sum_attn = layer_input.astype(jnp.float32) + branch
    normed, inverse = normalize(sum_attn)
    first_norm = normed * attn_gain + attn_shift
    inner_pre = matmul_low(first_norm.astype(jnp.bfloat16), inner_weight) + inner_bias
    active_low = jax.nn.gelu(inner_pre, approximate=False).astype(jnp.bfloat16)
    sum_ffn = first_norm + matmul_low(active_low, outer_weight) + outer_bias
    normed_two, inverse_two = normalize(sum_ffn)
    result = normed_two * ffn_gain + ffn_shift
    result = jnp.where(drop_flag > 0, layer_input.astype(jnp.float32), result)
    kept_items = (
        layer_input,
        query_low,
        key_local,
        value_local,
        attended,
        log_total,
        sum_attn,
        inner_pre,
        sum_ffn,
    ) + gathered
    return (result, kept_items)


def layer_backward(grad_out, kept_items, params, seg_query):
    (
        qkv_weight,
        query_bias,
        value_bias,
        attn_weight,
        attn_bias,
        attn_gain,
        attn_shift,
        inner_weight,
        inner_bias,
        outer_weight,
        outer_bias,
        ffn_gain,
        ffn_shift,
    ) = params
    (
        layer_input,
        query_low,
        key_local,
        value_local,
        attended,
        log_total,
        sum_attn,
        inner_pre,
        sum_ffn,
    ) = kept_items[:9]
    model_width = layer_input.shape[1]
    row_count = layer_input.shape[0]
    normed, inverse = normalize(sum_attn)
    first_norm = normed * attn_gain + attn_shift
    normed_two, inverse_two = normalize(sum_ffn)
    grad_ffn_gain = jnp.sum(grad_out * normed_two, axis=0)
    grad_ffn_shift = jnp.sum(grad_out, axis=0)
    grad_sum_ffn = norm_back(grad_out, normed_two, inverse_two, ffn_gain)
    grad_ffn_low = grad_sum_ffn.astype(jnp.bfloat16)
    active, gelu_pull = jax.vjp(partial(jax.nn.gelu, approximate=False), inner_pre)
    grad_outer_weight = left_product(active.astype(jnp.bfloat16), grad_ffn_low)
    grad_outer_bias = jnp.sum(grad_ffn_low.astype(jnp.float32), axis=0)
    grad_active = right_product(grad_ffn_low, outer_weight)
    grad_inner = gelu_pull(grad_active)[0].astype(jnp.bfloat16)
    grad_inner_weight = left_product(first_norm.astype(jnp.bfloat16), grad_inner)
    grad_inner_bias = jnp.sum(grad_inner.astype(jnp.float32), axis=0)
    grad_first = grad_sum_ffn + right_product(grad_inner, inner_weight)
    grad_attn_gain = jnp.sum(grad_first * normed, axis=0)
    grad_attn_shift = jnp.sum(grad_first, axis=0)
    grad_sum_attn = norm_back(grad_first, normed, inverse, attn_gain)
    grad_branch = grad_sum_attn.astype(jnp.bfloat16)
    grad_attn_weight = left_product(attended.astype(jnp.bfloat16), grad_branch)
    grad_attn_bias = jnp.sum(grad_branch.astype(jnp.float32), axis=0)
    grad_attended = right_product(grad_branch, attn_weight).astype(jnp.bfloat16)
    key_all, value_all, seg_all, pad_all = kept_items[9:]
    row_delta = jnp.sum(
        (grad_attended.astype(jnp.float32) * attended).reshape(row_count, HEADS, HEAD_DIM), axis=-1
    ).T
    grad_query, grad_key_all, grad_value_all = attention_back(
        query_low,
        key_all,
        value_all,
        seg_query,
        seg_all,
        pad_all,
        log_total,
        row_delta,
        grad_attended,
    )
    grad_key, grad_value = (
        lax.psum_scatter(
            grad_key_all.astype(jnp.bfloat16), "ctx", scatter_dimension=0, tiled=True
        ).astype(jnp.float32),
        lax.psum_scatter(
            grad_value_all.astype(jnp.bfloat16), "ctx", scatter_dimension=0, tiled=True
        ).astype(jnp.float32),
    )
    grad_qkv = jnp.concatenate([grad_query, grad_key, grad_value], axis=1).astype(jnp.bfloat16)
    grad_qkv_weight = left_product(layer_input, grad_qkv)
    grad_query_bias = jnp.sum(grad_qkv[:, :model_width].astype(jnp.float32), axis=0)
    grad_value_bias = jnp.sum(grad_qkv[:, 2 * model_width :].astype(jnp.float32), axis=0)
    grad_input = grad_sum_attn + right_product(grad_qkv, qkv_weight)
    layer_grads = (
        grad_qkv_weight,
        grad_query_bias,
        grad_value_bias,
        grad_attn_weight,
        grad_attn_bias,
        grad_attn_gain,
        grad_attn_shift,
        grad_inner_weight,
        grad_inner_bias,
        grad_outer_weight,
        grad_outer_bias,
        grad_ffn_gain,
        grad_ffn_shift,
    )
    return (layer_grads, grad_input)


def body(
    tokens,
    segment_ids,
    padding,
    dropped,
    qkv_weight,
    query_bias,
    value_bias,
    attn_weight,
    attn_bias,
    attn_gain,
    attn_shift,
    inner_weight,
    inner_bias,
    outer_weight,
    outer_bias,
    ffn_gain,
    ffn_shift,
    cotangent,
):
    micro_count = tokens.shape[0]
    section_index = lax.axis_index("section")
    half_width = tokens.shape[2] // lax.axis_size("section")
    params = tuple(
        (
            member[0]
            for member in (
                qkv_weight,
                query_bias,
                value_bias,
                attn_weight,
                attn_bias,
                attn_gain,
                attn_shift,
                inner_weight,
                inner_bias,
                outer_weight,
                outer_bias,
                ffn_gain,
                ffn_shift,
            )
        )
    )
    drop_row = dropped[0]
    incoming = jnp.zeros(tokens.shape[1:], jnp.bfloat16)
    saved_ticks = []
    encoded_rows = []
    for tick_index in range(micro_count + 1):
        micro_index = jnp.clip(tick_index - section_index, 0, micro_count - 1)
        own_input = lax.dynamic_index_in_dim(tokens, micro_index, 0, False)
        layer_input = jnp.where(section_index == 0, own_input, incoming)
        seg_query = lax.dynamic_index_in_dim(segment_ids, micro_index, 0, False)
        pad_query = lax.dynamic_index_in_dim(padding, micro_index, 0, False)
        drop_flag = lax.dynamic_index_in_dim(drop_row, micro_index, 0, False)
        layer_out, kept_items = layer_forward(layer_input, params, seg_query, pad_query, drop_flag)
        layer_low = layer_out.astype(jnp.bfloat16)
        received = shifted(layer_low, "section", 1)
        incoming = received
        if tick_index >= 1:
            encoded_rows.append(jnp.where(section_index == 0, received, layer_low))
        saved_ticks.append(kept_items)
    stacked = jax.tree.map(lambda *members: jnp.stack(members), *saved_ticks)
    grad_totals = tuple((jnp.zeros(member.shape, jnp.float32) for member in params))
    grad_incoming = jnp.zeros(tokens.shape[1:], jnp.bfloat16)
    input_rows = []
    for tick_index in range(micro_count + 1):
        raw_index = tick_index - 1 + section_index
        micro_index = jnp.clip(raw_index, 0, micro_count - 1)
        live_tick = ((raw_index >= 0) & (raw_index < micro_count)).astype(jnp.float32)
        forward_tick = jnp.clip(tick_index - 1 + 2 * section_index, 0, micro_count)
        kept_items = jax.tree.map(
            lambda member: lax.dynamic_index_in_dim(member, forward_tick, 0, False), stacked
        )
        own_cot = lax.dynamic_index_in_dim(cotangent, micro_index, 0, False)
        upstream = jnp.where(section_index == 1, own_cot, grad_incoming).astype(jnp.float32)
        seg_query = lax.dynamic_index_in_dim(segment_ids, micro_index, 0, False)
        pad_query = lax.dynamic_index_in_dim(padding, micro_index, 0, False)
        drop_flag = lax.dynamic_index_in_dim(drop_row, micro_index, 0, False)
        keep_scale = (drop_flag == 0).astype(jnp.float32) * live_tick
        layer_grads, grad_input = layer_backward(
            upstream * keep_scale, kept_items, params, seg_query
        )
        grad_totals = tuple((total + term for total, term in zip(grad_totals, layer_grads)))
        grad_input = grad_input + (drop_flag > 0).astype(jnp.float32) * upstream
        grad_low = grad_input.astype(jnp.bfloat16)
        received = shifted(grad_low, "section", 1)
        grad_incoming = received
        if tick_index >= 1:
            input_rows.append(jnp.where(section_index == 0, grad_low, received))
    reduced_once = (
        lax.psum_scatter(
            grad_totals[0][None].astype(jnp.bfloat16), "dp", scatter_dimension=1, tiled=True
        ).astype(jnp.float32),
        lax.psum_scatter(
            grad_totals[3][None].astype(jnp.bfloat16), "dp", scatter_dimension=1, tiled=True
        ).astype(jnp.float32),
        lax.psum_scatter(
            grad_totals[7][None].astype(jnp.bfloat16), "dp", scatter_dimension=1, tiled=True
        ).astype(jnp.float32),
        lax.psum_scatter(
            grad_totals[9][None].astype(jnp.bfloat16), "dp", scatter_dimension=1, tiled=True
        ).astype(jnp.float32),
    )
    matrix_grads = (
        lax.psum_scatter(
            reduced_once[0].astype(jnp.bfloat16), "ctx", scatter_dimension=2, tiled=True
        ).astype(jnp.float32),
        lax.psum_scatter(
            reduced_once[1].astype(jnp.bfloat16), "ctx", scatter_dimension=2, tiled=True
        ).astype(jnp.float32),
        lax.psum_scatter(
            reduced_once[2].astype(jnp.bfloat16), "ctx", scatter_dimension=2, tiled=True
        ).astype(jnp.float32),
        lax.psum_scatter(
            reduced_once[3].astype(jnp.bfloat16), "ctx", scatter_dimension=2, tiled=True
        ).astype(jnp.float32),
    )
    vector_grads = lax.psum(
        (
            grad_totals[1][None],
            grad_totals[2][None],
            grad_totals[4][None],
            grad_totals[5][None],
            grad_totals[6][None],
            grad_totals[8][None],
            grad_totals[10][None],
            grad_totals[11][None],
            grad_totals[12][None],
        ),
        ("dp", "ctx"),
    )
    encoded = lax.dynamic_slice_in_dim(
        jnp.stack(encoded_rows), section_index * half_width, half_width, 2
    )
    tokens_grad = lax.dynamic_slice_in_dim(
        jnp.stack(input_rows), section_index * half_width, half_width, 2
    )
    return (
        encoded,
        tokens_grad,
        matrix_grads[0],
        vector_grads[0],
        vector_grads[1],
        matrix_grads[1],
        vector_grads[2],
        vector_grads[3],
        vector_grads[4],
        matrix_grads[2],
        vector_grads[5],
        matrix_grads[3],
        vector_grads[6],
        vector_grads[7],
        vector_grads[8],
    )


def dot_plain(left, right):
    return lax.dot_general(left, right, (((1,), (0,)), ((), ())), preferred_element_type=jnp.float32)


def dot_flipped(left, right):
    return lax.dot_general(left, right, (((1,), (1,)), ((), ())), preferred_element_type=jnp.float32)


def dot_leading(left, right):
    return lax.dot_general(left, right, (((0,), (0,)), ((), ())), preferred_element_type=jnp.float32)


def gelu_parts(x):
    below = 0.5 * (1.0 + lax.erf(x * 0.7071067811865476))
    density = jnp.exp(-0.5 * x * x) * 0.3989422804014327
    return (x * below, below + x * density)


def rows_of(index, size):
    return pl.ds(pl.multiple_of(index * size, size), size)


def piece_rows(ctx, at, count, n_pieces):
    return pl.ds(0, count) if n_pieces == 1 else rows_of(ctx ^ at, count)


def head_lanes(shape, which):
    lane = lax.broadcasted_iota(jnp.int32, shape, 1)
    return (lane < HEAD_DIM) if which == 0 else (lane >= HEAD_DIM)


def copy_list(pairs, sems, first=0):
    copies = [pltpu.make_async_copy(src, dst, sems.at[first + at]) for at, (src, dst) in enumerate(pairs)]
    for copy in copies:
        copy.start()
    return copies


def wait_all(copies):
    for copy in copies:
        copy.wait()


low, full = jnp.bfloat16, jnp.float32


def kernel_call(body, operands, outs, scratch, mib, aliases=None):
    spaces = {"a": pl.ANY, "s": pltpu.SMEM, "v": pltpu.VMEM, "h": pltpu.HBM, "c": pltpu.VMEM}
    members = []
    for space, array in operands:
        if space in "vh":
            array = pltpu.with_memory_space_constraint(array, spaces[space])
        members.append(array)
    return pl.pallas_call(
        body,
        out_shape=[spaces[space](shape, kind) for space, shape, kind in outs],
        in_specs=[pl.BlockSpec(memory_space=spaces[space]) for space, _ in operands],
        out_specs=[pl.BlockSpec(memory_space=spaces[space]) for space, _, _ in outs],
        scratch_shapes=scratch,
        input_output_aliases=aliases or {},
        compiler_params=pltpu.CompilerParams(vmem_limit_bytes=mib * 2**20),
    )(*members)


class Outgoing:
    def __init__(self, sems):
        self.sems, self.copies = sems, []

    def send(self, src, dst):
        copy = pltpu.make_async_copy(src, dst, self.sems.at[len(self.copies)])
        copy.start()
        self.copies.append(copy)

    def finish(self):
        wait_all(self.copies)


def scratch_like(shapes):
    return [pltpu.VMEM(shape, kind) for _, shape, kind in shapes]


def in_pairs(count, step):
    def both_steps(at, carry):
        for which in range(UNROLL):
            step(UNROLL * at + which)
        return carry

    lax.fori_loop(0, count // UNROLL, both_steps, 0)


UNROLL = 2


documents = 5


def forward_kernel(active, n_pieces, n_cot, n_alias, scal, qkv_bias_ref, qkv_scale_ref, vec_ref, inner_bias_ref, *refs):
    pieces, refs = refs[:n_pieces], refs[n_pieces:]
    cot_pieces, refs = refs[:n_cot], refs[n_cot:]
    weights_h, refs = refs[:4], refs[4 + n_alias :]
    n_outs = 16 if n_cot else 12
    outs_h, outs, (wqkv, wattn, win, wout, first, code_rows, ids, in_sems, out_sems) = (
        refs[:n_outs],
        refs[n_outs : 2 * n_outs],
        refs[2 * n_outs :],
    )
    u, qkv, att, lse, n1, r1, dg, n2, r2, first_low, res, feats = outs[:12]
    top = outs[12:]
    size, width = u.shape

    @pl.when(scal[0] == active)
    def _():
        loads = [
            pltpu.make_async_copy(src, dst, in_sems.at[at])
            for at, (src, dst) in enumerate(zip(weights_h, (wqkv, wattn, win, wout)))
        ]
        loads[0].start()
        out = Outgoing(out_sems)

        def save(*places):
            for place in places:
                out.send(outs[place], outs_h[place])

        count = size // 4
        if n_pieces == 1:
            u[...] = pieces[0][:size]
            ids[...] = pieces[0][size:, :size].astype(full)[:8]
        else:
            for at, piece in enumerate(pieces):
                place = rows_of(scal[1] ^ at, count)
                u[place, :] = piece[:count]
                ids[:, place] = piece[count:, :count].astype(full)[:8]
        lane = lax.broadcasted_iota(jnp.int32, (size, 128), 1)
        lane = jnp.where(lane < HEAD_DIM, lane, lane - HEAD_DIM).astype(full)
        for which in range(2):
            for at in range(4):
                place = slice(at * count, (at + 1) * count)
                code_rows[place, :] = jnp.broadcast_to(ids[which : which + 1, place], (count, count)).T
            if which == 0:
                differs = (lane < documents) & (code_rows[...] != lane)
                feats[0] = jnp.where(differs | (lane == documents), masked_score, 0.0).astype(low)
            else:
                padded = (lane == documents) & (code_rows[...] < 0)
                feats[1] = jnp.where(padded | (code_rows[...] == lane), 1.0, 0.0).astype(low)
        loads[0].wait()
        loads[1].start()
        loads[2].start()
        save(0, 11)
        value = dot_plain(u[...], wqkv[...]) + qkv_bias_ref[...]
        qkv[...] = (value * qkv_scale_ref[...]).astype(low)
        save(1)
        def heads(pair):
            query, key, value = (qkv[:, rows_of(pair + part * (width // 128), 128)] for part in range(3))
            sides = []
            for which in range(2):
                own = head_lanes(key.shape, which)
                scores = dot_flipped(jnp.where(own, key, feats[1]), jnp.where(own, query, feats[0]))
                top_score = jnp.max(scores, axis=0, keepdims=True)
                weights = jnp.exp(scores - top_score)
                total = jnp.sum(weights, axis=0, keepdims=True)
                head = 2 * pair + which
                lse[pl.ds(head, 1), :] = top_score + jnp.log(total)
                sides.append(dot_leading((weights * (1.0 / total)).astype(low), value))
            att[:, rows_of(pair, 128)] = jnp.where(head_lanes((size, 128), 0), sides[0], sides[1]).astype(low)

        in_pairs(width // 128, heads)
        save(2, 3)
        loads[1].wait()
        value = dot_plain(att[...], wattn[...]) + u[...].astype(full) + vec_ref[0:1, :]
        normed, inverse = normalize(value)
        n1[...] = normed.astype(low)
        r1[...] = jnp.broadcast_to(inverse, r1.shape)
        value = normed * vec_ref[1:2, :] + vec_ref[2:3, :]
        first[...] = value + vec_ref[3:4, :]
        first_low[...] = value.astype(low)
        save(9, 4, 5)
        loads[2].wait()
        loads[3].start()
        inner = dot_plain(first_low[...], win[...]) + inner_bias_ref[...]
        active_value, slope = gelu_parts(inner)
        dg[...] = slope.astype(low)
        save(6)
        loads[3].wait()
        normed, inverse = normalize(first[...] + dot_plain(active_value.astype(low), wout[...]))
        n2[...] = normed.astype(low)
        r2[...] = jnp.broadcast_to(inverse, r2.shape)
        value = normed * vec_ref[4:5, :] + vec_ref[5:6, :]
        res[:size] = jnp.where(scal[2] > 0, u[...], value.astype(low))
        res[size:, :size] = jnp.concatenate([ids[...], jnp.zeros_like(ids)], axis=0).astype(low)
        save(10)
        if n_cot:
            for at, piece in enumerate(cot_pieces):
                top[0][rows_of(scal[1] ^ at, count), :] = piece[...]
            top_of_backward(scal, vec_ref, normed, inverse, *top[:3])
            top[3][0] = first_low[...]
            top[3][1] = top[1][...]
            save(15, 13, 12, 14)
        else:
            save(7, 8)
        out.finish()


def top_of_backward(scal, vec_ref, normed, inverse, inc, dffn, vec):
    grad = inc[...].astype(full) * jnp.where(scal[2] > 0, 0.0, 1.0)
    value = norm_back(grad, normed, inverse, vec_ref[4:5, :])
    rounded = value.astype(low)
    dffn[...] = rounded
    vec[0:1, :] = column_sum(rounded.astype(full))
    vec[1:2, :] = column_sum(grad * normed)
    vec[2:3, :] = column_sum(grad)


def top_shapes(size, width):
    return [
        ("h", (size, width), low),
        ("h", (size, width), low),
        ("h", (8, width), full),
    ]


def run_forward(active, scal, small, pieces, cot_pieces, held, earlier, after):
    width, hidden = held[2].shape
    size = len(pieces) * (pieces[0].shape[0] - 16)
    outs = [
        ("h", (size, width), low),
        ("h", (size, 3 * width), low),
        ("h", (size, width), low),
        ("h", (16, size), full),
        ("h", (size, width), low),
        ("h", (size, 128), full),
        ("h", (size, hidden), low),
        ("h", (size, width), low),
        ("h", (size, 128), full),
        ("h", (size, width), low),
        ("h", (size + 16, width), low),
        ("h", (2, size, 128), low),
    ]
    if cot_pieces:
        outs += top_shapes(size, width) + [("h", (2, size, width), low)]
    operands = [("s", scal)] + [("c", member) for member in small]
    operands += [("c", member) for member in (*pieces, *cot_pieces)] + [("h", member) for member in held]
    at_alias = len(operands)
    operands += [(out[0], member) for out, member in zip(outs, earlier)] + [("c", member) for member in after]
    return kernel_call(
        partial(forward_kernel, active, len(pieces), len(cot_pieces), len(earlier) + len(after)),
        operands,
        outs,
        scratch_like(outs)
        + [pltpu.VMEM(member.shape, low) for member in held]
        + [
            pltpu.VMEM((size, width), full),
            pltpu.VMEM((size, size // 4), full),
            pltpu.VMEM((8, size), full),
            pltpu.SemaphoreType.DMA((4,)),
            pltpu.SemaphoreType.DMA((len(outs),)),
        ],
        48,
        {at_alias + i: i for i in range(len(earlier))},
    )


def column_sum(value):
    return jnp.sum(value, axis=0, keepdims=True)


def top_kernel(active, n_alias, n_after, scal, vec_ref, incoming, n2_h, r2_h, *refs):
    refs = refs[n_alias + n_after :]
    outs_h, outs, (n2, r2, in_sems, out_sems) = refs[:3], refs[3:6], refs[6:]

    @pl.when(scal[0] == active)
    def _():
        loads = copy_list([(n2_h, n2), (r2_h, r2)], in_sems)
        outs[0][...] = incoming[...]
        wait_all(loads)
        top_of_backward(scal, vec_ref, n2[...].astype(full), r2[:, :1], *outs)
        wait_all(copy_list(list(zip(outs, outs_h)), out_sems))


def run_top(active, scal, vecs, incoming, n2, r2, earlier, after):
    size, width = n2.shape
    outs = top_shapes(size, width)
    operands = [("s", scal), ("c", vecs), ("c", incoming)] + [("h", member) for member in (n2, r2)]
    at_alias = len(operands)
    operands += [(out[0], member) for out, member in zip(outs, earlier)] + list(after)
    return kernel_call(
        partial(top_kernel, active, len(earlier), len(after)),
        operands,
        outs,
        scratch_like(outs)
        + [
            pltpu.VMEM(n2.shape, low),
            pltpu.VMEM(r2.shape, full),
            pltpu.SemaphoreType.DMA((2,)),
            pltpu.SemaphoreType.DMA((3,)),
        ],
        16,
        {at_alias + i: i for i in range(len(earlier))},
    )


def chain_kernel(active, n_alias, n_after, scal, vec_ref, *refs):
    held_h, refs = refs[:12], refs[12 + n_alias + n_after :]
    outs_h, outs, held, (dinner, datt, first, in_sems, out_sems) = refs[:4], refs[4:8], refs[8:20], refs[20:]
    inc, dffn, dg, n1, r1, qkv, lse, wqkv, wattn, win, wout, feats = held
    dqkv, dbranch, vec, din = outs
    size, width = inc.shape
    hidden = win.shape[1]

    @pl.when(scal[0] == active)
    def _():
        chunks = hidden // width
        cuts = [slice(at * width, (at + 1) * width) for at in range(chunks)]
        order = [(held_h[1], dffn)]
        for cut in cuts:
            order += [(held_h[10].at[cut, :], wout.at[cut, :]), (held_h[2].at[:, cut], dg.at[:, cut])]
        order += [(held_h[at], held[at]) for at in (9, 3, 4, 8, 5, 6, 11, 7, 0)]
        loads = [pltpu.make_async_copy(src, dst, in_sems.at[at]) for at, (src, dst) in enumerate(order)]

        def begin(first_copy, last_copy):
            for copy in loads[first_copy:last_copy]:
                copy.start()

        begin(0, 5)
        out = Outgoing(out_sems)
        for at, cut in enumerate(cuts):
            wait_all(loads[: 3] if at == 0 else loads[2 * at + 1 : 2 * at + 3])
            begin(2 * at + 5, 2 * at + 7)
            value = (dot_flipped(dffn[...], wout[cut, :]) * dg[:, cut].astype(full)).astype(low)
            dinner[:, cut] = value
            vec[8 + at : 9 + at, :] = column_sum(value.astype(full))
        begin(2 * chunks + 5, len(loads))
        loads = loads[2 * chunks + 1 :]
        wait_all(loads[:3])
        grad = dot_flipped(dinner[...], win[...]) + dffn[...].astype(full)
        normed = n1[...].astype(full)
        value = norm_back(grad, normed, r1[:, :1], vec_ref[1:2, :])
        first[...] = value
        rounded = value.astype(low)
        dbranch[...] = rounded
        vec[2:3, :] = column_sum(rounded.astype(full))
        vec[3:4, :] = column_sum(grad * normed)
        vec[4:5, :] = column_sum(grad)
        out.send(dbranch, outs_h[1])
        loads[3].wait()
        datt[...] = dot_flipped(dbranch[...], wattn[...]).astype(low)
        wait_all(loads[4:7])
        def heads(pair):
            cols = [rows_of(pair + part * (width // 128), 128) for part in range(3)]
            query, key, value = (qkv[:, col] for col in cols)
            grad = datt[:, cols[0]]
            parts = []
            for which in range(2):
                own = head_lanes(key.shape, which)
                scores = dot_flipped(jnp.where(own, key, feats[1]), jnp.where(own, query, feats[0]))
                value_own = jnp.where(own, value, jnp.zeros_like(value))
                head = 2 * pair + which
                probs = jnp.exp(scores - lse[pl.ds(head, 1), :])
                dprobs = dot_flipped(value_own, grad)
                delta = column_sum(probs * dprobs)
                dscores = (probs * (dprobs - delta)).astype(low)
                parts.append(
                    (dot_leading(dscores, key), dot_plain(dscores, query), dot_plain(probs.astype(low), grad))
                )
            low_lanes = head_lanes((size, 128), 0)
            dquery, dkey, dvalue = (jnp.where(low_lanes, one, two) for one, two in zip(*parts))
            dquery = (dquery * HEAD_DIM ** (-0.5)).astype(low)
            dvalue = dvalue.astype(low)
            dqkv[:, cols[0]] = dquery
            dqkv[:, cols[1]] = dkey.astype(low)
            dqkv[:, cols[2]] = dvalue
            vec[0:1, cols[0]] = column_sum(dquery.astype(full))
            vec[1:2, cols[0]] = column_sum(dvalue.astype(full))

        in_pairs(width // 128, heads)
        out.send(dqkv, outs_h[0])
        out.send(vec, outs_h[2])
        wait_all(loads[7:])
        value = first[...] + dot_flipped(dqkv[...], wqkv[...])
        din[...] = jnp.where(scal[2] > 0, inc[...], value.astype(low))
        out.send(din, outs_h[3])
        out.finish()


def run_chain(active, scal, vecs, top, kept, held, earlier, after):
    u, qkv, att, lse, n1, r1, dg = kept[:7]
    inc, dffn = top[:2]
    size, width = u.shape
    hidden = dg.shape[1]
    outs = [
        ("h", (size, 3 * width), low),
        ("h", (size, width), low),
        ("h", (16, width), full),
        ("h", (size, width), low),
    ]
    members = (inc, dffn, dg, n1, r1, qkv, lse, *held, kept[11])
    operands = [("s", scal), ("c", vecs)] + [("h", member) for member in members]
    at_alias = len(operands)
    operands += [(out[0], member) for out, member in zip(outs, earlier)]
    operands += list(after)
    return kernel_call(
        partial(chain_kernel, active, len(earlier), len(after)),
        operands,
        outs,
        scratch_like(outs)
        + [pltpu.VMEM(member.shape, member.dtype) for member in members]
        + [
            pltpu.VMEM((size, hidden), low),
            pltpu.VMEM((size, width), low),
            pltpu.VMEM((size, width), full),
            pltpu.SemaphoreType.DMA((2 * (hidden // width) + 10,)),
            pltpu.SemaphoreType.DMA((4,)),
        ],
        48,
        {at_alias + i: i for i in range(len(earlier))},
    )


def split_high(value):
    high = value.astype(low)
    return high, (value - high.astype(full)).astype(low)


def wide_pair(value, rows):
    pair = jnp.concatenate(split_high(value), axis=1)
    return jnp.concatenate([pair, jnp.zeros((rows - pair.shape[0], pair.shape[1]), low)], axis=0)


def joined(high, rest):
    return high.astype(full) + rest.astype(full)


def attn_grad_kernel(n_after, scal, top_vec, chain_vec, *refs):
    ins_h, refs = refs[:4], refs[4 + n_after :]
    send_a, keep_a, send_b, keep_b, vec = refs[:5]
    (u, att, dqkv, dbranch), out, pair, in_sems, sems = refs[5:9], *refs[9:]
    width = u.shape[1]
    dp = scal[3]
    bit_y, bit_x = dp // 2, dp % 2
    left, right = pl.ds(0, 2 * width), pl.ds(2 * width, 2 * width)
    each = width // 4
    loads = copy_list([(ins_h[at], (u, att, dqkv, dbranch)[at]) for at in (0, 2, 1, 3)], in_sems)
    sent = Outgoing(sems)
    value = jnp.concatenate([top_vec[...], chain_vec[...]], axis=0)
    vec[...] = value
    pair[...] = wide_pair(value, VEC_ROWS)
    sent.send(pair, send_a.at[pl.ds(2 * each, VEC_ROWS)])
    wait_all(loads[:2])
    flipped = u[...].T
    out[:, : 2 * width] = dot_plain(flipped, dqkv[:, : 2 * width]).astype(low)
    for at in range(2):
        sent.send(out.at[rows_of(2 * at + 1 - bit_x, each), left], send_a.at[pl.ds(at * each, each)])
        sent.send(out.at[rows_of(2 * at + bit_x, each), left], keep_a.at[at])
    out[:, 2 * width : 3 * width] = dot_plain(flipped, dqkv[:, 2 * width :]).astype(low)
    wait_all(loads[2:])
    out[:, 3 * width :] = dot_leading(att[...], dbranch[...]).astype(low)
    for at in range(2):
        sent.send(out.at[rows_of(2 * (1 - bit_y) + at, each), right], send_b.at[at])
        sent.send(out.at[rows_of(2 * bit_y + at, each), right], keep_b.at[at])
    sent.finish()


VEC_ROWS = 32


def run_attn_grad(scal, top_vec, chain_vec, u, att, dqkv, dbranch, after):
    width = u.shape[1]
    each = width // 4
    members = (u, att, dqkv, dbranch)
    half_shape = ("h", (2, each, 2 * width), low)
    return kernel_call(
        partial(attn_grad_kernel, len(after)),
        [("s", scal), ("c", top_vec), ("c", chain_vec)] + [("h", member) for member in members] + list(after),
        [("h", (2 * each + VEC_ROWS, 2 * width), low)] + [half_shape] * 3 + [("c", (24, width), full)],
        [pltpu.VMEM(member.shape, low) for member in members]
        + [
            pltpu.VMEM((width, 4 * width), low),
            pltpu.VMEM((VEC_ROWS, 2 * width), low),
            pltpu.SemaphoreType.DMA((4,)),
            pltpu.SemaphoreType.DMA((9,)),
        ],
        24,
    )


def ffn_grad_kernel(n_after, scal, inner_bias_ref, win_h, wout_h, first_h, dffn_h, *refs):
    from_one, firsts, dffns = refs[:3], refs[3:6], refs[6:9]
    send, keep, first, dffn, active, dinner, win, wout, out, sems = refs[9 + n_after :]
    size, width = dffn_h.shape
    own = rows_of(2 * (scal[3] % 2) + scal[1] % 2, width)
    loads = copy_list(
        [
            (first_h, first.at[:size]),
            (win_h.at[:, own], win),
            (dffn_h, dffn.at[:size]),
            (wout_h.at[own, :], wout),
        ],
        sems,
    )
    is_zero = scal[0] == 0
    for at in range(4):
        rows = slice(at * size, (at + 1) * size)
        if at == 0:
            wait_all(loads)
            value, grad = first[rows], dffn[rows]
        else:
            value = jnp.where(is_zero, firsts[at - 1][...], from_one[at - 1][0])
            grad = jnp.where(is_zero, dffns[at - 1][...], from_one[at - 1][1])
            first[rows] = value
            dffn[rows] = grad
        inner = dot_plain(value, win[...]) + inner_bias_ref[:, own]
        active_value, slope = gelu_parts(inner)
        active[rows] = active_value.astype(low)
        dinner[rows] = (dot_flipped(grad, wout[...]) * slope).astype(low)
    each = width // 4
    for half, (left, right) in enumerate(((first, dinner), (dffn, active))):
        part = dot_leading(left[...], right[...]).astype(low)
        for block in range(4):
            source = block if half == 0 else 2 * (block % 2) + block // 2
            out[block, each * half : each * (half + 1)] = part[each * source : each * (source + 1)]
    bit = scal[3] // 2
    wait_all(
        copy_list(
            [(out.at[2 * (1 - bit) + at], send.at[at]) for at in range(2)]
            + [(out.at[2 * bit + at], keep.at[at]) for at in range(2)],
            sems,
        )
    )


def run_ffn_grad(scal, inner_bias, win, wout, first_own, dffn_own, from_one, firsts, dffns, after):
    size, width = dffn_own.shape
    return kernel_call(
        partial(ffn_grad_kernel, len(after)),
        [("s", scal), ("c", inner_bias)]
        + [("h", member) for member in (win, wout, first_own, dffn_own)]
        + [("c", member) for member in (*from_one, *firsts, *dffns)]
        + list(after),
        [("h", (2, width // 2, width), low)] * 2,
        [pltpu.VMEM((4 * size, width), low) for _ in range(4)]
        + [pltpu.VMEM((width, width), low), pltpu.VMEM((width, width), low)]
        + [pltpu.VMEM((4, width // 2, width), low), pltpu.SemaphoreType.DMA((4,))],
        32,
    )


def merge_kernel(scal, got_a, keep_a, got_b, keep_b, vec, send_a, left_a, send_b, left_b, vec_out):
    bit_y, bit_x = scal[3] // 2, scal[3] % 2
    each, width = keep_a.shape[1], vec.shape[1]
    send_a[:each] = added(got_a[rows_of(1 - bit_y, each)], keep_a[1 - bit_y])
    left_a[...] = added(got_a[rows_of(bit_y, each)], keep_a[bit_y])
    send_b[...] = added(got_b[1 - bit_x], keep_b[1 - bit_x])
    left_b[...] = added(got_b[bit_x], keep_b[bit_x])
    pair = got_a[2 * each :]
    value = vec[...] + joined(pair[:24, :width], pair[:24, width:])
    vec_out[...] = value
    send_a[each:] = wide_pair(value, VEC_ROWS)


def turn_kernel(scal, got_a, keep_a, got_b, keep_b, vec, send, keep, vec_out, rows, blocks):
    each, cut = keep_a.shape
    rows[:, :cut] = added(got_a[:each], keep_a[...])
    rows[:, cut:] = added(got_b[...], keep_b[...])
    width = cut // 2
    wide, narrow = 3 * width // 4, width // 4
    for at in range(4):
        blocks[at, :, :wide] = rows[:, wide * at : wide * (at + 1)]
        blocks[at, :, wide:] = rows[:, 3 * width + narrow * at : 3 * width + narrow * (at + 1)]
    bit = scal[1] % 2
    for at in range(2):
        send[at * each : (at + 1) * each] = blocks[2 * at + 1 - bit]
        keep[at] = blocks[2 * at + bit]
    pair = got_a[each:]
    value = vec[...] + joined(pair[:24, :width], pair[:24, width:])
    vec_out[...] = value
    send[2 * each :] = jnp.concatenate(split_high(value), axis=0)


def last_kernel(scal, got, keep, vec, send, left, vec_out):
    bit = scal[1] // 2
    each = keep.shape[1]
    send[:each] = added(got[rows_of(1 - bit, each)], keep[1 - bit])
    left[...] = added(got[rows_of(bit, each)], keep[bit])
    pair = got[2 * each :]
    value = vec[...] + joined(pair[:24], pair[24:])
    vec_out[...] = value
    send[each:] = jnp.concatenate(split_high(value), axis=0)


def end_kernel(scal, got, keep, vec, qkv_out, attn_out, vec_out):
    each = keep.shape[0]
    value = got[:each].astype(full) + keep[...].astype(full)
    qkv_out[...] = value[:, : 3 * each]
    attn_out[...] = value[:, 3 * each :]
    pair = got[each:]
    vec_out[...] = vec[...] + joined(pair[:24], pair[24:])


def half_kernel(scal, got, keep, send, left):
    bit = scal[1] // 2
    send[...] = added(got[1 - bit], keep[1 - bit])
    left[...] = added(got[bit], keep[bit])


def swapped(x, axis, by):
    return lax.ppermute(x, axis, [(i, i ^ by) for i in range(lax.axis_size(axis))])


def near(section, x, by):
    pairs = [
        (16 * section + 4 * i + j, 16 * section + 4 * (i ^ (by & 1)) + (j ^ (by >> 1)))
        for i in range(4)
        for j in range(4)
    ]
    return lax.ppermute(x, ("section", "dp", "ctx"), pairs)


def moved(x, target):
    pairs = [(16 * s + 4 * i + j, 16 * s + target(i, j)) for s in range(2) for i in range(4) for j in range(4)]
    return lax.ppermute(x, ("section", "dp", "ctx"), pairs)


def swapped_in(section, x, axis, by):
    length = lax.axis_size(axis)
    pairs = [(section * length + i, section * length + (i ^ by)) for i in range(length)]
    return lax.ppermute(x, ("section", axis), pairs)


def pick(x, at, dim=0):
    return lax.dynamic_index_in_dim(x, at, dim, False)


def added(one, two):
    return (one.astype(full) + two.astype(full)).astype(low)


def spread(row_half, ctx, swap):
    length = lax.axis_size("ctx")
    size, width = row_half.shape
    parts = row_half.reshape(length, size // length, width)
    out = jnp.zeros(parts.shape, parts.dtype)
    out = lax.dynamic_update_index_in_dim(out, pick(parts, ctx), ctx, 0)
    for k in range(1, length):
        out = lax.dynamic_update_index_in_dim(out, swap(pick(parts, ctx ^ k), "ctx", k), ctx ^ k, 0)
    return out


def to_section(x, section):
    return lax.ppermute(x, "section", [(1 - section, section)])


def following(body, n_operands, n_after, *refs):
    body(*refs[:n_operands], *refs[n_operands + n_after :])


def merged(body, scal, operands, outs, scratch=(), after=()):
    return kernel_call(
        partial(following, body, 1 + len(operands), len(after)),
        [("s", scal)] + [("c", member) for member in operands] + [("a", member) for member in after],
        [("c", shape, kind) for shape, kind in outs],
        list(scratch),
        16,
    )


def row_body(
    tokens,
    segment_ids,
    padding,
    dropped,
    qkv_weight,
    query_bias,
    value_bias,
    attn_weight,
    attn_bias,
    attn_gain,
    attn_shift,
    inner_weight,
    inner_bias,
    outer_weight,
    outer_bias,
    ffn_gain,
    ffn_shift,
    cotangent,
):
    width = tokens.shape[2]
    half, each = width // 2, width // 4
    count = tokens.shape[1]
    section, dp, ctx = (lax.axis_index(name) for name in ("section", "dp", "ctx"))
    weights = (qkv_weight[0], attn_weight[0], inner_weight[0], outer_weight[0])
    vecs = jnp.concatenate(
        [attn_bias, attn_gain, attn_shift, outer_bias, ffn_gain, ffn_shift, query_bias, value_bias]
    )
    qkv_bias = jnp.concatenate([query_bias, jnp.zeros_like(query_bias), value_bias], axis=1)
    qkv_scale = jnp.concatenate(
        [jnp.full((1, width), HEAD_DIM ** (-0.5), jnp.float32), jnp.ones((1, 2 * width), jnp.float32)], axis=1
    )
    small = (qkv_bias, qkv_scale, vecs, inner_bias)
    scal = jnp.stack([section, ctx, pick(dropped[0], ctx), dp]).astype(jnp.int32)

    ids = jnp.stack([segment_ids, jnp.where(padding == 1, segment_ids, -1)], axis=1).astype(low)
    ids = jnp.pad(ids, ((0, 0), (0, 14), (0, width - count)))
    sent = jnp.concatenate([tokens, ids], axis=1)
    far = {k: swapped_in(0, pick(sent, ctx ^ k), "ctx", k) for k in (2, 3, 1)}
    own_tokens = [pick(sent, ctx), far[1], far[2], far[3]]
    held = weights
    own_cot = [pick(cotangent, ctx)] + [swapped_in(1, pick(cotangent, ctx ^ k), "ctx", k) for k in range(1, 4)]

    kept = run_forward(0, scal, small, own_tokens, [], held, [], [])
    middle = lax.ppermute(kept[10], "section", [(0, 1)])
    firsts = [near(0, kept[9], k) for k in (3, 2, 1)]
    made = run_forward(1, scal, small, [middle], own_cot, held, kept, firsts)
    kept, top, both = made[:12], made[12:15], made[15]
    from_one = [near(1, both, k) for k in (3, 2, 1)]
    chain = run_chain(1, scal, vecs, top, kept, held, [], [])
    incoming = to_section(chain[3], 0)
    top = run_top(0, scal, vecs, incoming, kept[7], kept[8], top, [("c", member) for member in from_one])
    dffns = [near(0, top[1], k) for k in (3, 2, 1)]
    chain = run_chain(0, scal, vecs, top, kept, held, chain, [])
    dqkv, dbranch, chain_vec, d_input = chain
    result = kept[10][: 4 * count]

    send_a, keep_a, send_b, keep_b, vec = run_attn_grad(
        scal, top[2], chain_vec, kept[0], kept[2], dqkv, dbranch, []
    )
    got_a, got_b = swapped(send_a, "dp", 1), swapped(send_b, "dp", 2)
    ffn_send, ffn_keep = run_ffn_grad(
        scal, inner_bias, held[2], held[3], kept[9], top[1], from_one, firsts, dffns, [("h", keep_b)]
    )
    ffn_got = swapped(ffn_send, "dp", 2)
    wide, block, flat = (each, 2 * width), (each, width), ((24, width), full)
    send_a, keep_a, send_b, keep_b, vec = merged(
        merge_kernel,
        scal,
        (got_a, keep_a, got_b, keep_b, vec),
        [((each + VEC_ROWS, 2 * width), low), (wide, low), (wide, low), (wide, low), flat],
        after=[ffn_keep],
    )
    got_a, got_b = swapped(send_a, "dp", 2), swapped(send_b, "dp", 1)
    ffn_send, ffn_keep = merged(
        half_kernel, scal, (ffn_got, ffn_keep), [(ffn_keep.shape[1:], low)] * 2, after=[send_b]
    )
    ffn_got = swapped(ffn_send, "ctx", 2)
    rows = jnp.where(section == 0, d_input, result)
    rows, ffn_keep = lax.optimization_barrier((rows, ffn_keep))
    rows = spread(rows, ctx, swapped)
    send, keep, vec = merged(
        turn_kernel,
        scal,
        (got_a, keep_a, got_b, keep_b, vec),
        [((2 * each + 48, width), low), ((2, each, width), low), flat],
        [pltpu.VMEM((each, 4 * width), low), pltpu.VMEM((4, each, width), low)],
        after=[ffn_keep],
    )
    got = swapped(send, "ctx", 1)
    send, keep, vec = merged(last_kernel, scal, (got, keep, vec), [((each + 48, width), low), (block, low), flat])
    got = swapped(send, "ctx", 2)
    qkv_grad, attn_grad, vec = merged(
        end_kernel, scal, (got, keep, vec), [((each, 3 * each), full), ((each, each), full), flat]
    )
    ffn_rows = added(ffn_got, ffn_keep)
    inner_grad = moved(ffn_rows[:each], lambda i, j: 4 * (2 * (i // 2) + j // 2) + 2 * (i % 2) + j % 2).astype(full)
    outer_grad = moved(ffn_rows[each:], lambda i, j: 4 * (2 * (i % 2) + j % 2) + 2 * (j // 2) + i // 2).astype(full).T
    rows, vec = lax.optimization_barrier((rows, vec))
    other_half = swapped(jnp.where(section == 0, rows[..., half:], rows[..., :half]), "section", 1)
    tokens_grad = jnp.where(section == 0, rows[..., :half], other_half)
    encoded = jnp.where(section == 0, other_half, rows[..., half:])
    return (
        encoded,
        tokens_grad,
        qkv_grad[None],
        vec[8:9],
        vec[9:10],
        attn_grad[None],
        vec[10:11],
        vec[11:12],
        vec[12:13],
        inner_grad[None],
        vec[16 : 16 + inner_bias.shape[1] // width].reshape(1, -1),
        outer_grad[None],
        vec[0:1],
        vec[1:2],
        vec[2:3],
    )


def solution(mesh):
    placed = (
        P("dp", "ctx", None),
        P("dp", "ctx"),
        P("dp", "ctx"),
        P("section", "dp"),
        P("section", None, None),
        P("section", None),
        P("section", None),
        P("section", None, None),
        P("section", None),
        P("section", None),
        P("section", None),
        P("section", None, None),
        P("section", None),
        P("section", None, None),
        P("section", None),
        P("section", None),
        P("section", None),
        P("dp", "ctx", None),
    )

    def dispatch(*members):
        rows = members[0].shape[0]
        same = rows == lax.axis_size("ctx") == lax.axis_size("dp") == 4
        return (row_body if same else body)(*members)

    return jax.shard_map(
        dispatch,
        mesh=mesh,
        in_specs=placed,
        out_specs=(
            P("dp", "ctx", "section"),
            P("dp", "ctx", "section"),
            P("section", "dp", "ctx"),
            P("section", None),
            P("section", None),
            P("section", "dp", "ctx"),
            P("section", None),
            P("section", None),
            P("section", None),
            P("section", "dp", "ctx"),
            P("section", None),
            P("section", "dp", "ctx"),
            P("section", None),
            P("section", None),
            P("section", None),
        ),
        check_vma=False,
    )
```

```python
from functools import partial

import jax
import jax.numpy as jnp
from jax import lax
from jax.experimental import pallas as pl
from jax.experimental.pallas import tpu as pltpu
from jax.sharding import PartitionSpec as P

HEADS = 12
HEAD_DIM = 64


norm_eps = 1e-05
masked_score = -1e30


def shifted(x, axis, by):
    length = lax.axis_size(axis)
    return lax.ppermute(x, axis, [(i, (i + by) % length) for i in range(length)])


def matmul_low(left, right):
    return jnp.dot(left, right, preferred_element_type=jnp.float32)


def left_product(left, right):
    return jnp.einsum("ti,to->io", left, right, preferred_element_type=jnp.float32)


def right_product(left, right):
    return jnp.einsum("to,io->ti", left, right, preferred_element_type=jnp.float32)


def normalize(values):
    mean_value = jnp.mean(values, axis=-1, keepdims=True)
    centered = values - mean_value
    variance = jnp.mean(centered * centered, axis=-1, keepdims=True)
    inverse = lax.rsqrt(variance + norm_eps)
    return (centered * inverse, inverse)


def norm_back(grad_out, normed, inverse, gain):
    scaled = grad_out * gain
    return inverse * (
        scaled
        - jnp.mean(scaled, axis=-1, keepdims=True)
        - normed * jnp.mean(scaled * normed, axis=-1, keepdims=True)
    )


def attend_piece(query_heads, seg_query, running, pieces):
    run_max, run_total, run_acc = running
    key_piece, value_piece, seg_piece, pad_piece = pieces
    count = key_piece.shape[0]
    key_heads = key_piece.reshape(count, HEADS, HEAD_DIM)
    value_heads = value_piece.reshape(count, HEADS, HEAD_DIM)
    scores = jnp.einsum(
        "qhd,khd->hqk", query_heads, key_heads, preferred_element_type=jnp.float32
    ) * HEAD_DIM ** (-0.5)
    allowed = (seg_query[:, None] == seg_piece[None, :]) & (pad_piece[None, :] == 1)
    scores = jnp.where(allowed[None], scores, masked_score)
    new_max = jnp.maximum(run_max, jnp.max(scores, axis=-1))
    weights = jnp.where(allowed[None], jnp.exp(scores - new_max[..., None]), 0.0)
    run_total = jnp.sum(weights, axis=-1)
    run_acc = jnp.einsum(
        "hqk,khd->hqd",
        weights.astype(jnp.bfloat16),
        value_heads,
        preferred_element_type=jnp.float32,
    )
    return (new_max, run_total, run_acc)


def attention_back(
    query_low, key_all, value_all, seg_query, seg_all, pad_all, log_total, row_delta, grad_att
):
    row_count = query_low.shape[0]
    seq_count = key_all.shape[0]
    score_scale = HEAD_DIM ** (-0.5)
    query_heads = query_low.reshape(row_count, HEADS, HEAD_DIM)
    key_heads = key_all.reshape(seq_count, HEADS, HEAD_DIM)
    value_heads = value_all.reshape(seq_count, HEADS, HEAD_DIM)
    grad_heads = grad_att.reshape(row_count, HEADS, HEAD_DIM)
    scores = (
        jnp.einsum("qhd,khd->hqk", query_heads, key_heads, preferred_element_type=jnp.float32)
        * score_scale
    )
    allowed = (seg_query[:, None] == seg_all[None, :]) & (pad_all[None, :] == 1)
    prob_rows = jnp.where(allowed[None], jnp.exp(scores - log_total[..., None]), 0.0)
    grad_probs = jnp.einsum(
        "qhd,khd->hqk", grad_heads, value_heads, preferred_element_type=jnp.float32
    )
    grad_scores = (prob_rows * (grad_probs - row_delta[..., None])).astype(jnp.bfloat16)
    grad_query = (
        jnp.einsum("hqk,khd->qhd", grad_scores, key_heads, preferred_element_type=jnp.float32)
        * score_scale
    )
    grad_key = (
        jnp.einsum("hqk,qhd->khd", grad_scores, query_heads, preferred_element_type=jnp.float32)
        * score_scale
    )
    grad_value = jnp.einsum(
        "hqk,qhd->khd",
        prob_rows.astype(jnp.bfloat16),
        grad_heads,
        preferred_element_type=jnp.float32,
    )
    model_width = HEADS * HEAD_DIM
    return (
        grad_query.reshape(row_count, model_width),
        grad_key.reshape(seq_count, model_width),
        grad_value.reshape(seq_count, model_width),
    )


def layer_forward(layer_input, params, seg_query, pad_query, drop_flag):
    (
        qkv_weight,
        query_bias,
        value_bias,
        attn_weight,
        attn_bias,
        attn_gain,
        attn_shift,
        inner_weight,
        inner_bias,
        outer_weight,
        outer_bias,
        ffn_gain,
        ffn_shift,
    ) = params
    model_width = layer_input.shape[1]
    row_count = layer_input.shape[0]
    projected = matmul_low(layer_input, qkv_weight)
    query_low = (projected[:, :model_width] + query_bias).astype(jnp.bfloat16)
    key_local = projected[:, model_width : 2 * model_width].astype(jnp.bfloat16)
    value_local = (projected[:, 2 * model_width :] + value_bias).astype(jnp.bfloat16)
    query_heads = query_low.reshape(row_count, HEADS, HEAD_DIM)
    start_state = (
        jnp.full((HEADS, row_count), masked_score, jnp.float32),
        jnp.zeros((HEADS, row_count), jnp.float32),
        jnp.zeros((HEADS, row_count, HEAD_DIM), jnp.float32),
    )
    key_all, value_all, seg_all, pad_all = (
        lax.all_gather(key_local, "ctx", axis=0, tiled=True),
        lax.all_gather(value_local, "ctx", axis=0, tiled=True),
        lax.all_gather(seg_query, "ctx", axis=0, tiled=True),
        lax.all_gather(pad_query, "ctx", axis=0, tiled=True),
    )
    run_max, run_total, run_acc = attend_piece(
        query_heads, seg_query, start_state, (key_all, value_all, seg_all, pad_all)
    )
    gathered = (key_all, value_all, seg_all, pad_all)
    attended = (run_acc / run_total[..., None]).transpose(1, 0, 2).reshape(row_count, model_width)
    log_total = run_max + jnp.log(run_total)
    branch = matmul_low(attended.astype(jnp.bfloat16), attn_weight) + attn_bias
    sum_attn = layer_input.astype(jnp.float32) + branch
    normed, inverse = normalize(sum_attn)
    first_norm = normed * attn_gain + attn_shift
    inner_pre = matmul_low(first_norm.astype(jnp.bfloat16), inner_weight) + inner_bias
    active_low = jax.nn.gelu(inner_pre, approximate=False).astype(jnp.bfloat16)
    sum_ffn = first_norm + matmul_low(active_low, outer_weight) + outer_bias
    normed_two, inverse_two = normalize(sum_ffn)
    result = normed_two * ffn_gain + ffn_shift
    result = jnp.where(drop_flag > 0, layer_input.astype(jnp.float32), result)
    kept_items = (
        layer_input,
        query_low,
        key_local,
        value_local,
        attended,
        log_total,
        sum_attn,
        inner_pre,
        sum_ffn,
    ) + gathered
    return (result, kept_items)


def layer_backward(grad_out, kept_items, params, seg_query):
    (
        qkv_weight,
        query_bias,
        value_bias,
        attn_weight,
        attn_bias,
        attn_gain,
        attn_shift,
        inner_weight,
        inner_bias,
        outer_weight,
        outer_bias,
        ffn_gain,
        ffn_shift,
    ) = params
    (
        layer_input,
        query_low,
        key_local,
        value_local,
        attended,
        log_total,
        sum_attn,
        inner_pre,
        sum_ffn,
    ) = kept_items[:9]
    model_width = layer_input.shape[1]
    row_count = layer_input.shape[0]
    normed, inverse = normalize(sum_attn)
    first_norm = normed * attn_gain + attn_shift
    normed_two, inverse_two = normalize(sum_ffn)
    grad_ffn_gain = jnp.sum(grad_out * normed_two, axis=0)
    grad_ffn_shift = jnp.sum(grad_out, axis=0)
    grad_sum_ffn = norm_back(grad_out, normed_two, inverse_two, ffn_gain)
    grad_ffn_low = grad_sum_ffn.astype(jnp.bfloat16)
    active, gelu_pull = jax.vjp(partial(jax.nn.gelu, approximate=False), inner_pre)
    grad_outer_weight = left_product(active.astype(jnp.bfloat16), grad_ffn_low)
    grad_outer_bias = jnp.sum(grad_ffn_low.astype(jnp.float32), axis=0)
    grad_active = right_product(grad_ffn_low, outer_weight)
    grad_inner = gelu_pull(grad_active)[0].astype(jnp.bfloat16)
    grad_inner_weight = left_product(first_norm.astype(jnp.bfloat16), grad_inner)
    grad_inner_bias = jnp.sum(grad_inner.astype(jnp.float32), axis=0)
    grad_first = grad_sum_ffn + right_product(grad_inner, inner_weight)
    grad_attn_gain = jnp.sum(grad_first * normed, axis=0)
    grad_attn_shift = jnp.sum(grad_first, axis=0)
    grad_sum_attn = norm_back(grad_first, normed, inverse, attn_gain)
    grad_branch = grad_sum_attn.astype(jnp.bfloat16)
    grad_attn_weight = left_product(attended.astype(jnp.bfloat16), grad_branch)
    grad_attn_bias = jnp.sum(grad_branch.astype(jnp.float32), axis=0)
    grad_attended = right_product(grad_branch, attn_weight).astype(jnp.bfloat16)
    key_all, value_all, seg_all, pad_all = kept_items[9:]
    row_delta = jnp.sum(
        (grad_attended.astype(jnp.float32) * attended).reshape(row_count, HEADS, HEAD_DIM), axis=-1
    ).T
    grad_query, grad_key_all, grad_value_all = attention_back(
        query_low,
        key_all,
        value_all,
        seg_query,
        seg_all,
        pad_all,
        log_total,
        row_delta,
        grad_attended,
    )
    grad_key, grad_value = (
        lax.psum_scatter(
            grad_key_all.astype(jnp.bfloat16), "ctx", scatter_dimension=0, tiled=True
        ).astype(jnp.float32),
        lax.psum_scatter(
            grad_value_all.astype(jnp.bfloat16), "ctx", scatter_dimension=0, tiled=True
        ).astype(jnp.float32),
    )
    grad_qkv = jnp.concatenate([grad_query, grad_key, grad_value], axis=1).astype(jnp.bfloat16)
    grad_qkv_weight = left_product(layer_input, grad_qkv)
    grad_query_bias = jnp.sum(grad_qkv[:, :model_width].astype(jnp.float32), axis=0)
    grad_value_bias = jnp.sum(grad_qkv[:, 2 * model_width :].astype(jnp.float32), axis=0)
    grad_input = grad_sum_attn + right_product(grad_qkv, qkv_weight)
    layer_grads = (
        grad_qkv_weight,
        grad_query_bias,
        grad_value_bias,
        grad_attn_weight,
        grad_attn_bias,
        grad_attn_gain,
        grad_attn_shift,
        grad_inner_weight,
        grad_inner_bias,
        grad_outer_weight,
        grad_outer_bias,
        grad_ffn_gain,
        grad_ffn_shift,
    )
    return (layer_grads, grad_input)


def body(
    tokens,
    segment_ids,
    padding,
    dropped,
    qkv_weight,
    query_bias,
    value_bias,
    attn_weight,
    attn_bias,
    attn_gain,
    attn_shift,
    inner_weight,
    inner_bias,
    outer_weight,
    outer_bias,
    ffn_gain,
    ffn_shift,
    cotangent,
):
    micro_count = tokens.shape[0]
    section_index = lax.axis_index("section")
    half_width = tokens.shape[2] // lax.axis_size("section")
    params = tuple(
        (
            member[0]
            for member in (
                qkv_weight,
                query_bias,
                value_bias,
                attn_weight,
                attn_bias,
                attn_gain,
                attn_shift,
                inner_weight,
                inner_bias,
                outer_weight,
                outer_bias,
                ffn_gain,
                ffn_shift,
            )
        )
    )
    drop_row = dropped[0]
    incoming = jnp.zeros(tokens.shape[1:], jnp.bfloat16)
    saved_ticks = []
    encoded_rows = []
    for tick_index in range(micro_count + 1):
        micro_index = jnp.clip(tick_index - section_index, 0, micro_count - 1)
        own_input = lax.dynamic_index_in_dim(tokens, micro_index, 0, False)
        layer_input = jnp.where(section_index == 0, own_input, incoming)
        seg_query = lax.dynamic_index_in_dim(segment_ids, micro_index, 0, False)
        pad_query = lax.dynamic_index_in_dim(padding, micro_index, 0, False)
        drop_flag = lax.dynamic_index_in_dim(drop_row, micro_index, 0, False)
        layer_out, kept_items = layer_forward(layer_input, params, seg_query, pad_query, drop_flag)
        layer_low = layer_out.astype(jnp.bfloat16)
        received = shifted(layer_low, "section", 1)
        incoming = received
        if tick_index >= 1:
            encoded_rows.append(jnp.where(section_index == 0, received, layer_low))
        saved_ticks.append(kept_items)
    stacked = jax.tree.map(lambda *members: jnp.stack(members), *saved_ticks)
    grad_totals = tuple((jnp.zeros(member.shape, jnp.float32) for member in params))
    grad_incoming = jnp.zeros(tokens.shape[1:], jnp.bfloat16)
    input_rows = []
    for tick_index in range(micro_count + 1):
        raw_index = tick_index - 1 + section_index
        micro_index = jnp.clip(raw_index, 0, micro_count - 1)
        live_tick = ((raw_index >= 0) & (raw_index < micro_count)).astype(jnp.float32)
        forward_tick = jnp.clip(tick_index - 1 + 2 * section_index, 0, micro_count)
        kept_items = jax.tree.map(
            lambda member: lax.dynamic_index_in_dim(member, forward_tick, 0, False), stacked
        )
        own_cot = lax.dynamic_index_in_dim(cotangent, micro_index, 0, False)
        upstream = jnp.where(section_index == 1, own_cot, grad_incoming).astype(jnp.float32)
        seg_query = lax.dynamic_index_in_dim(segment_ids, micro_index, 0, False)
        pad_query = lax.dynamic_index_in_dim(padding, micro_index, 0, False)
        drop_flag = lax.dynamic_index_in_dim(drop_row, micro_index, 0, False)
        keep_scale = (drop_flag == 0).astype(jnp.float32) * live_tick
        layer_grads, grad_input = layer_backward(
            upstream * keep_scale, kept_items, params, seg_query
        )
        grad_totals = tuple((total + term for total, term in zip(grad_totals, layer_grads)))
        grad_input = grad_input + (drop_flag > 0).astype(jnp.float32) * upstream
        grad_low = grad_input.astype(jnp.bfloat16)
        received = shifted(grad_low, "section", 1)
        grad_incoming = received
        if tick_index >= 1:
            input_rows.append(jnp.where(section_index == 0, grad_low, received))
    reduced_once = (
        lax.psum_scatter(
            grad_totals[0][None].astype(jnp.bfloat16), "dp", scatter_dimension=1, tiled=True
        ).astype(jnp.float32),
        lax.psum_scatter(
            grad_totals[3][None].astype(jnp.bfloat16), "dp", scatter_dimension=1, tiled=True
        ).astype(jnp.float32),
        lax.psum_scatter(
            grad_totals[7][None].astype(jnp.bfloat16), "dp", scatter_dimension=1, tiled=True
        ).astype(jnp.float32),
        lax.psum_scatter(
            grad_totals[9][None].astype(jnp.bfloat16), "dp", scatter_dimension=1, tiled=True
        ).astype(jnp.float32),
    )
    matrix_grads = (
        lax.psum_scatter(
            reduced_once[0].astype(jnp.bfloat16), "ctx", scatter_dimension=2, tiled=True
        ).astype(jnp.float32),
        lax.psum_scatter(
            reduced_once[1].astype(jnp.bfloat16), "ctx", scatter_dimension=2, tiled=True
        ).astype(jnp.float32),
        lax.psum_scatter(
            reduced_once[2].astype(jnp.bfloat16), "ctx", scatter_dimension=2, tiled=True
        ).astype(jnp.float32),
        lax.psum_scatter(
            reduced_once[3].astype(jnp.bfloat16), "ctx", scatter_dimension=2, tiled=True
        ).astype(jnp.float32),
    )
    vector_grads = lax.psum(
        (
            grad_totals[1][None],
            grad_totals[2][None],
            grad_totals[4][None],
            grad_totals[5][None],
            grad_totals[6][None],
            grad_totals[8][None],
            grad_totals[10][None],
            grad_totals[11][None],
            grad_totals[12][None],
        ),
        ("dp", "ctx"),
    )
    encoded = lax.dynamic_slice_in_dim(
        jnp.stack(encoded_rows), section_index * half_width, half_width, 2
    )
    tokens_grad = lax.dynamic_slice_in_dim(
        jnp.stack(input_rows), section_index * half_width, half_width, 2
    )
    return (
        encoded,
        tokens_grad,
        matrix_grads[0],
        vector_grads[0],
        vector_grads[1],
        matrix_grads[1],
        vector_grads[2],
        vector_grads[3],
        vector_grads[4],
        matrix_grads[2],
        vector_grads[5],
        matrix_grads[3],
        vector_grads[6],
        vector_grads[7],
        vector_grads[8],
    )


def dot_plain(left, right):
    return lax.dot_general(left, right, (((1,), (0,)), ((), ())), preferred_element_type=jnp.float32)


def dot_flipped(left, right):
    return lax.dot_general(left, right, (((1,), (1,)), ((), ())), preferred_element_type=jnp.float32)


def dot_leading(left, right):
    return lax.dot_general(left, right, (((0,), (0,)), ((), ())), preferred_element_type=jnp.float32)


def gelu_parts(x):
    below = 0.5 * (1.0 + lax.erf(x * 0.7071067811865476))
    density = jnp.exp(-0.5 * x * x) * 0.3989422804014327
    return (x * below, below + x * density)


def rows_of(index, size):
    return pl.ds(pl.multiple_of(index * size, size), size)


def piece_rows(ctx, at, count, n_pieces):
    return pl.ds(0, count) if n_pieces == 1 else rows_of(ctx ^ at, count)


def head_lanes(shape, which):
    lane = lax.broadcasted_iota(jnp.int32, shape, 1)
    return (lane < HEAD_DIM) if which == 0 else (lane >= HEAD_DIM)


def copy_list(pairs, sems, first=0):
    copies = [pltpu.make_async_copy(src, dst, sems.at[first + at]) for at, (src, dst) in enumerate(pairs)]
    for copy in copies:
        copy.start()
    return copies


def wait_all(copies):
    for copy in copies:
        copy.wait()


low, full = jnp.bfloat16, jnp.float32


def kernel_call(body, operands, outs, scratch, mib, aliases=None):
    spaces = {"a": pl.ANY, "s": pltpu.SMEM, "v": pltpu.VMEM, "h": pltpu.HBM, "c": pltpu.VMEM}
    members = []
    for space, array in operands:
        if space in "vh":
            array = pltpu.with_memory_space_constraint(array, spaces[space])
        members.append(array)
    return pl.pallas_call(
        body,
        out_shape=[spaces[space](shape, kind) for space, shape, kind in outs],
        in_specs=[pl.BlockSpec(memory_space=spaces[space]) for space, _ in operands],
        out_specs=[pl.BlockSpec(memory_space=spaces[space]) for space, _, _ in outs],
        scratch_shapes=scratch,
        input_output_aliases=aliases or {},
        compiler_params=pltpu.CompilerParams(vmem_limit_bytes=mib * 2**20),
    )(*members)


class Outgoing:
    def __init__(self, sems):
        self.sems, self.copies = sems, []

    def send(self, src, dst):
        copy = pltpu.make_async_copy(src, dst, self.sems.at[len(self.copies)])
        copy.start()
        self.copies.append(copy)

    def finish(self):
        wait_all(self.copies)


def scratch_like(shapes):
    return [pltpu.VMEM(shape, kind) for _, shape, kind in shapes]


def in_pairs(count, step, together=2):
    def both_steps(at, carry):
        for which in range(together):
            step(together * at + which)
        return carry

    lax.fori_loop(0, count // together, both_steps, 0)


documents = 5


def forward_kernel(active, n_pieces, n_cot, n_alias, scal, qkv_bias_ref, qkv_scale_ref, vec_ref, inner_bias_ref, *refs):
    pieces, refs = refs[:n_pieces], refs[n_pieces:]
    cot_pieces, refs = refs[:n_cot], refs[n_cot:]
    weights_h, refs = refs[:4], refs[4 + n_alias :]
    n_outs = 16 if n_cot else 12
    outs_h, outs, (wqkv, wattn, win, wout, first, code_rows, ids, in_sems, out_sems) = (
        refs[:n_outs],
        refs[n_outs : 2 * n_outs],
        refs[2 * n_outs :],
    )
    u, qkv, att, lse, n1, r1, dg, n2, r2, first_low, res, feats = outs[:12]
    top = outs[12:]
    size, width = u.shape

    @pl.when(scal[0] == active)
    def _():
        loads = [
            pltpu.make_async_copy(src, dst, in_sems.at[at])
            for at, (src, dst) in enumerate(zip(weights_h, (wqkv, wattn, win, wout)))
        ]
        loads[0].start()
        out = Outgoing(out_sems)

        def save(*places):
            for place in places:
                out.send(outs[place], outs_h[place])

        count = size // 4
        if n_pieces == 1:
            u[...] = pieces[0][:size]
            ids[...] = pieces[0][size:, :size].astype(full)[:8]
        else:
            for at, piece in enumerate(pieces):
                place = rows_of(scal[1] ^ at, count)
                u[place, :] = piece[:count]
                ids[:, place] = piece[count:, :count].astype(full)[:8]
        lane = lax.broadcasted_iota(jnp.int32, (size, 128), 1)
        lane = jnp.where(lane < HEAD_DIM, lane, lane - HEAD_DIM).astype(full)
        for which in range(2):
            for at in range(4):
                place = slice(at * count, (at + 1) * count)
                code_rows[place, :] = jnp.broadcast_to(ids[which : which + 1, place], (count, count)).T
            if which == 0:
                differs = (lane < documents) & (code_rows[...] != lane)
                feats[0] = jnp.where(differs | (lane == documents), masked_score, 0.0).astype(low)
            else:
                padded = (lane == documents) & (code_rows[...] < 0)
                feats[1] = jnp.where(padded | (code_rows[...] == lane), 1.0, 0.0).astype(low)
        loads[0].wait()
        loads[1].start()
        loads[2].start()
        save(0, 11)
        value = dot_plain(u[...], wqkv[...]) + qkv_bias_ref[...]
        qkv[...] = (value * qkv_scale_ref[...]).astype(low)
        save(1)
        def heads(pair):
            query, key, value = (qkv[:, rows_of(pair + part * (width // 128), 128)] for part in range(3))
            sides = []
            for which in range(2):
                own = head_lanes(key.shape, which)
                scores = dot_flipped(jnp.where(own, key, feats[1]), jnp.where(own, query, feats[0]))
                top_score = jnp.max(scores, axis=0, keepdims=True)
                weights = jnp.exp(scores - top_score)
                total = jnp.sum(weights, axis=0, keepdims=True)
                head = 2 * pair + which
                lse[pl.ds(head, 1), :] = top_score + jnp.log(total)
                sides.append(dot_leading((weights * (1.0 / total)).astype(low), value))
            att[:, rows_of(pair, 128)] = jnp.where(head_lanes((size, 128), 0), sides[0], sides[1]).astype(low)

        in_pairs(width // 128, heads, 3)
        save(2, 3)
        loads[1].wait()
        value = dot_plain(att[...], wattn[...]) + u[...].astype(full) + vec_ref[0:1, :]
        normed, inverse = normalize(value)
        n1[...] = normed.astype(low)
        r1[...] = jnp.broadcast_to(inverse, r1.shape)
        value = normed * vec_ref[1:2, :] + vec_ref[2:3, :]
        first[...] = value + vec_ref[3:4, :]
        first_low[...] = value.astype(low)
        save(9, 4, 5)
        loads[2].wait()
        loads[3].start()
        inner = dot_plain(first_low[...], win[...]) + inner_bias_ref[...]
        active_value, slope = gelu_parts(inner)
        dg[...] = slope.astype(low)
        save(6)
        loads[3].wait()
        normed, inverse = normalize(first[...] + dot_plain(active_value.astype(low), wout[...]))
        n2[...] = normed.astype(low)
        r2[...] = jnp.broadcast_to(inverse, r2.shape)
        value = normed * vec_ref[4:5, :] + vec_ref[5:6, :]
        res[:size] = jnp.where(scal[2] > 0, u[...], value.astype(low))
        res[size:, :size] = jnp.concatenate([ids[...], jnp.zeros_like(ids)], axis=0).astype(low)
        save(10)
        if n_cot:
            for at, piece in enumerate(cot_pieces):
                top[0][rows_of(scal[1] ^ at, count), :] = piece[...]
            top_of_backward(scal, vec_ref, normed, inverse, *top[:3])
            top[3][0] = first_low[...]
            top[3][1] = top[1][...]
            save(15, 13, 12, 14)
        else:
            save(7, 8)
        out.finish()


def top_of_backward(scal, vec_ref, normed, inverse, inc, dffn, vec):
    grad = inc[...].astype(full) * jnp.where(scal[2] > 0, 0.0, 1.0)
    value = norm_back(grad, normed, inverse, vec_ref[4:5, :])
    rounded = value.astype(low)
    dffn[...] = rounded
    vec[0:1, :] = column_sum(rounded.astype(full))
    vec[1:2, :] = column_sum(grad * normed)
    vec[2:3, :] = column_sum(grad)


def top_shapes(size, width):
    return [
        ("h", (size, width), low),
        ("h", (size, width), low),
        ("h", (8, width), full),
    ]


def run_forward(active, scal, small, pieces, cot_pieces, held, earlier, after):
    width, hidden = held[2].shape
    size = len(pieces) * (pieces[0].shape[0] - 16)
    outs = [
        ("h", (size, width), low),
        ("h", (size, 3 * width), low),
        ("h", (size, width), low),
        ("h", (16, size), full),
        ("h", (size, width), low),
        ("h", (size, 128), full),
        ("h", (size, hidden), low),
        ("h", (size, width), low),
        ("h", (size, 128), full),
        ("h", (size, width), low),
        ("h", (size + 16, width), low),
        ("h", (2, size, 128), low),
    ]
    if cot_pieces:
        outs += top_shapes(size, width) + [("h", (2, size, width), low)]
    operands = [("s", scal)] + [("c", member) for member in small]
    operands += [("c", member) for member in (*pieces, *cot_pieces)] + [("h", member) for member in held]
    at_alias = len(operands)
    operands += [(out[0], member) for out, member in zip(outs, earlier)] + [("c", member) for member in after]
    return kernel_call(
        partial(forward_kernel, active, len(pieces), len(cot_pieces), len(earlier) + len(after)),
        operands,
        outs,
        scratch_like(outs)
        + [pltpu.VMEM(member.shape, low) for member in held]
        + [
            pltpu.VMEM((size, width), full),
            pltpu.VMEM((size, size // 4), full),
            pltpu.VMEM((8, size), full),
            pltpu.SemaphoreType.DMA((4,)),
            pltpu.SemaphoreType.DMA((len(outs),)),
        ],
        48,
        {at_alias + i: i for i in range(len(earlier))},
    )


def column_sum(value):
    return jnp.sum(value, axis=0, keepdims=True)


def top_kernel(active, n_alias, n_after, scal, vec_ref, incoming, n2_h, r2_h, *refs):
    refs = refs[n_alias + n_after :]
    outs_h, outs, (n2, r2, in_sems, out_sems) = refs[:3], refs[3:6], refs[6:]

    @pl.when(scal[0] == active)
    def _():
        loads = copy_list([(n2_h, n2), (r2_h, r2)], in_sems)
        outs[0][...] = incoming[...]
        wait_all(loads)
        top_of_backward(scal, vec_ref, n2[...].astype(full), r2[:, :1], *outs)
        wait_all(copy_list(list(zip(outs, outs_h)), out_sems))


def run_top(active, scal, vecs, incoming, n2, r2, earlier, after):
    size, width = n2.shape
    outs = top_shapes(size, width)
    operands = [("s", scal), ("c", vecs), ("c", incoming)] + [("h", member) for member in (n2, r2)]
    at_alias = len(operands)
    operands += [(out[0], member) for out, member in zip(outs, earlier)] + list(after)
    return kernel_call(
        partial(top_kernel, active, len(earlier), len(after)),
        operands,
        outs,
        scratch_like(outs)
        + [
            pltpu.VMEM(n2.shape, low),
            pltpu.VMEM(r2.shape, full),
            pltpu.SemaphoreType.DMA((2,)),
            pltpu.SemaphoreType.DMA((3,)),
        ],
        16,
        {at_alias + i: i for i in range(len(earlier))},
    )


def chain_kernel(active, n_alias, n_after, scal, vec_ref, *refs):
    held_h, refs = refs[:12], refs[12 + n_alias + n_after :]
    outs_h, outs, held, (dinner, datt, first, in_sems, out_sems) = refs[:4], refs[4:8], refs[8:20], refs[20:]
    inc, dffn, dg, n1, r1, qkv, lse, wqkv, wattn, win, wout, feats = held
    dqkv, dbranch, vec, din = outs
    size, width = inc.shape
    hidden = win.shape[1]

    @pl.when(scal[0] == active)
    def _():
        chunks = hidden // width
        cuts = [slice(at * width, (at + 1) * width) for at in range(chunks)]
        order = [(held_h[1], dffn)]
        for cut in cuts:
            order += [(held_h[10].at[cut, :], wout.at[cut, :]), (held_h[2].at[:, cut], dg.at[:, cut])]
        order += [(held_h[at], held[at]) for at in (9, 3, 4, 8, 5, 6, 11, 7, 0)]
        loads = [pltpu.make_async_copy(src, dst, in_sems.at[at]) for at, (src, dst) in enumerate(order)]

        def begin(first_copy, last_copy):
            for copy in loads[first_copy:last_copy]:
                copy.start()

        begin(0, 5)
        out = Outgoing(out_sems)
        for at, cut in enumerate(cuts):
            wait_all(loads[: 3] if at == 0 else loads[2 * at + 1 : 2 * at + 3])
            begin(2 * at + 5, 2 * at + 7)
            value = (dot_flipped(dffn[...], wout[cut, :]) * dg[:, cut].astype(full)).astype(low)
            dinner[:, cut] = value
            vec[8 + at : 9 + at, :] = column_sum(value.astype(full))
        begin(2 * chunks + 5, len(loads))
        loads = loads[2 * chunks + 1 :]
        wait_all(loads[:3])
        grad = dot_flipped(dinner[...], win[...]) + dffn[...].astype(full)
        normed = n1[...].astype(full)
        value = norm_back(grad, normed, r1[:, :1], vec_ref[1:2, :])
        first[...] = value
        rounded = value.astype(low)
        dbranch[...] = rounded
        vec[2:3, :] = column_sum(rounded.astype(full))
        vec[3:4, :] = column_sum(grad * normed)
        vec[4:5, :] = column_sum(grad)
        out.send(dbranch, outs_h[1])
        loads[3].wait()
        datt[...] = dot_flipped(dbranch[...], wattn[...]).astype(low)
        wait_all(loads[4:7])
        def heads(pair):
            cols = [rows_of(pair + part * (width // 128), 128) for part in range(3)]
            query, key, value = (qkv[:, col] for col in cols)
            grad = datt[:, cols[0]]
            parts = []
            for which in range(2):
                own = head_lanes(key.shape, which)
                scores = dot_flipped(jnp.where(own, key, feats[1]), jnp.where(own, query, feats[0]))
                value_own = jnp.where(own, value, jnp.zeros_like(value))
                head = 2 * pair + which
                probs = jnp.exp(scores - lse[pl.ds(head, 1), :])
                dprobs = dot_flipped(value_own, grad)
                delta = column_sum(probs * dprobs)
                dscores = (probs * (dprobs - delta)).astype(low)
                parts.append(
                    (dot_leading(dscores, key), dot_plain(dscores, query), dot_plain(probs.astype(low), grad))
                )
            low_lanes = head_lanes((size, 128), 0)
            dquery, dkey, dvalue = (jnp.where(low_lanes, one, two) for one, two in zip(*parts))
            dquery = (dquery * HEAD_DIM ** (-0.5)).astype(low)
            dvalue = dvalue.astype(low)
            dqkv[:, cols[0]] = dquery
            dqkv[:, cols[1]] = dkey.astype(low)
            dqkv[:, cols[2]] = dvalue
            vec[0:1, cols[0]] = column_sum(dquery.astype(full))
            vec[1:2, cols[0]] = column_sum(dvalue.astype(full))

        in_pairs(width // 128, heads)
        out.send(dqkv, outs_h[0])
        out.send(vec, outs_h[2])
        wait_all(loads[7:])
        value = first[...] + dot_flipped(dqkv[...], wqkv[...])
        din[...] = jnp.where(scal[2] > 0, inc[...], value.astype(low))
        out.send(din, outs_h[3])
        out.finish()


def run_chain(active, scal, vecs, top, kept, held, earlier, after):
    u, qkv, att, lse, n1, r1, dg = kept[:7]
    inc, dffn = top[:2]
    size, width = u.shape
    hidden = dg.shape[1]
    outs = [
        ("h", (size, 3 * width), low),
        ("h", (size, width), low),
        ("h", (16, width), full),
        ("h", (size, width), low),
    ]
    members = (inc, dffn, dg, n1, r1, qkv, lse, *held, kept[11])
    operands = [("s", scal), ("c", vecs)] + [("h", member) for member in members]
    at_alias = len(operands)
    operands += [(out[0], member) for out, member in zip(outs, earlier)]
    operands += list(after)
    return kernel_call(
        partial(chain_kernel, active, len(earlier), len(after)),
        operands,
        outs,
        scratch_like(outs)
        + [pltpu.VMEM(member.shape, member.dtype) for member in members]
        + [
            pltpu.VMEM((size, hidden), low),
            pltpu.VMEM((size, width), low),
            pltpu.VMEM((size, width), full),
            pltpu.SemaphoreType.DMA((2 * (hidden // width) + 10,)),
            pltpu.SemaphoreType.DMA((4,)),
        ],
        48,
        {at_alias + i: i for i in range(len(earlier))},
    )


def split_high(value):
    high = value.astype(low)
    return high, (value - high.astype(full)).astype(low)


def wide_pair(value, rows):
    pair = jnp.concatenate(split_high(value), axis=1)
    return jnp.concatenate([pair, jnp.zeros((rows - pair.shape[0], pair.shape[1]), low)], axis=0)


def joined(high, rest):
    return high.astype(full) + rest.astype(full)


def attn_grad_kernel(n_after, scal, top_vec, chain_vec, *refs):
    ins_h, refs = refs[:4], refs[4 + n_after :]
    send_a, keep_a, send_b, keep_b, vec = refs[:5]
    (u, att, dqkv, dbranch), out, pair, in_sems, sems = refs[5:9], *refs[9:]
    width = u.shape[1]
    dp = scal[3]
    bit_y, bit_x = dp // 2, dp % 2
    left, right = pl.ds(0, 2 * width), pl.ds(2 * width, 2 * width)
    each = width // 4
    loads = copy_list([(ins_h[at], (u, att, dqkv, dbranch)[at]) for at in (0, 2, 1, 3)], in_sems)
    sent = Outgoing(sems)
    value = jnp.concatenate([top_vec[...], chain_vec[...]], axis=0)
    vec[...] = value
    pair[...] = wide_pair(value, VEC_ROWS)
    sent.send(pair, send_a.at[pl.ds(2 * each, VEC_ROWS)])
    wait_all(loads[:2])
    flipped = u[...].T
    out[:, : 2 * width] = dot_plain(flipped, dqkv[:, : 2 * width]).astype(low)
    for at in range(2):
        sent.send(out.at[rows_of(2 * at + 1 - bit_x, each), left], send_a.at[pl.ds(at * each, each)])
        sent.send(out.at[rows_of(2 * at + bit_x, each), left], keep_a.at[at])
    out[:, 2 * width : 3 * width] = dot_plain(flipped, dqkv[:, 2 * width :]).astype(low)
    wait_all(loads[2:])
    out[:, 3 * width :] = dot_leading(att[...], dbranch[...]).astype(low)
    for at in range(2):
        sent.send(out.at[rows_of(2 * (1 - bit_y) + at, each), right], send_b.at[at])
        sent.send(out.at[rows_of(2 * bit_y + at, each), right], keep_b.at[at])
    sent.finish()


VEC_ROWS = 32


def run_attn_grad(scal, top_vec, chain_vec, u, att, dqkv, dbranch, after):
    width = u.shape[1]
    each = width // 4
    members = (u, att, dqkv, dbranch)
    half_shape = ("h", (2, each, 2 * width), low)
    return kernel_call(
        partial(attn_grad_kernel, len(after)),
        [("s", scal), ("c", top_vec), ("c", chain_vec)] + [("h", member) for member in members] + list(after),
        [("h", (2 * each + VEC_ROWS, 2 * width), low)] + [half_shape] * 3 + [("c", (24, width), full)],
        [pltpu.VMEM(member.shape, low) for member in members]
        + [
            pltpu.VMEM((width, 4 * width), low),
            pltpu.VMEM((VEC_ROWS, 2 * width), low),
            pltpu.SemaphoreType.DMA((4,)),
            pltpu.SemaphoreType.DMA((9,)),
        ],
        24,
    )


def ffn_grad_kernel(n_after, scal, inner_bias_ref, win_h, wout_h, first_h, dffn_h, *refs):
    from_one, firsts, dffns = refs[:3], refs[3:6], refs[6:9]
    send, keep, first, dffn, active, dinner, win, wout, out, sems = refs[9 + n_after :]
    size, width = dffn_h.shape
    own = rows_of(2 * (scal[3] % 2) + scal[1] % 2, width)
    loads = copy_list(
        [
            (first_h, first.at[:size]),
            (win_h.at[:, own], win),
            (dffn_h, dffn.at[:size]),
            (wout_h.at[own, :], wout),
        ],
        sems,
    )
    is_zero = scal[0] == 0
    for at in range(4):
        rows = slice(at * size, (at + 1) * size)
        if at == 0:
            wait_all(loads)
            value, grad = first[rows], dffn[rows]
        else:
            value = jnp.where(is_zero, firsts[at - 1][...], from_one[at - 1][0])
            grad = jnp.where(is_zero, dffns[at - 1][...], from_one[at - 1][1])
            first[rows] = value
            dffn[rows] = grad
        inner = dot_plain(value, win[...]) + inner_bias_ref[:, own]
        active_value, slope = gelu_parts(inner)
        active[rows] = active_value.astype(low)
        dinner[rows] = (dot_flipped(grad, wout[...]) * slope).astype(low)
    each = width // 4
    for half, (left, right) in enumerate(((first, dinner), (dffn, active))):
        part = dot_leading(left[...], right[...]).astype(low)
        for block in range(4):
            source = block if half == 0 else 2 * (block % 2) + block // 2
            out[block, each * half : each * (half + 1)] = part[each * source : each * (source + 1)]
    bit = scal[3] // 2
    wait_all(
        copy_list(
            [(out.at[2 * (1 - bit) + at], send.at[at]) for at in range(2)]
            + [(out.at[2 * bit + at], keep.at[at]) for at in range(2)],
            sems,
        )
    )


def run_ffn_grad(scal, inner_bias, win, wout, first_own, dffn_own, from_one, firsts, dffns, after):
    size, width = dffn_own.shape
    return kernel_call(
        partial(ffn_grad_kernel, len(after)),
        [("s", scal), ("c", inner_bias)]
        + [("h", member) for member in (win, wout, first_own, dffn_own)]
        + [("c", member) for member in (*from_one, *firsts, *dffns)]
        + list(after),
        [("h", (2, width // 2, width), low)] * 2,
        [pltpu.VMEM((4 * size, width), low) for _ in range(4)]
        + [pltpu.VMEM((width, width), low), pltpu.VMEM((width, width), low)]
        + [pltpu.VMEM((4, width // 2, width), low), pltpu.SemaphoreType.DMA((4,))],
        32,
    )


def merge_kernel(scal, got_a, keep_a, got_b, keep_b, vec, send_a, left_a, send_b, left_b, vec_out):
    bit_y, bit_x = scal[3] // 2, scal[3] % 2
    each, width = keep_a.shape[1], vec.shape[1]
    send_a[:each] = added(got_a[rows_of(1 - bit_y, each)], keep_a[1 - bit_y])
    left_a[...] = added(got_a[rows_of(bit_y, each)], keep_a[bit_y])
    send_b[...] = added(got_b[1 - bit_x], keep_b[1 - bit_x])
    left_b[...] = added(got_b[bit_x], keep_b[bit_x])
    pair = got_a[2 * each :]
    value = vec[...] + joined(pair[:24, :width], pair[:24, width:])
    vec_out[...] = value
    send_a[each:] = wide_pair(value, VEC_ROWS)


def turn_kernel(scal, got_a, keep_a, got_b, keep_b, vec, send, keep, vec_out, rows, blocks):
    each, cut = keep_a.shape
    rows[:, :cut] = added(got_a[:each], keep_a[...])
    rows[:, cut:] = added(got_b[...], keep_b[...])
    width = cut // 2
    wide, narrow = 3 * width // 4, width // 4
    for at in range(4):
        blocks[at, :, :wide] = rows[:, wide * at : wide * (at + 1)]
        blocks[at, :, wide:] = rows[:, 3 * width + narrow * at : 3 * width + narrow * (at + 1)]
    bit = scal[1] % 2
    for at in range(2):
        send[at * each : (at + 1) * each] = blocks[2 * at + 1 - bit]
        keep[at] = blocks[2 * at + bit]
    pair = got_a[each:]
    value = vec[...] + joined(pair[:24, :width], pair[:24, width:])
    vec_out[...] = value
    send[2 * each :] = jnp.concatenate(split_high(value), axis=0)


def last_kernel(scal, got, keep, vec, send, left, vec_out):
    bit = scal[1] // 2
    each = keep.shape[1]
    send[:each] = added(got[rows_of(1 - bit, each)], keep[1 - bit])
    left[...] = added(got[rows_of(bit, each)], keep[bit])
    pair = got[2 * each :]
    value = vec[...] + joined(pair[:24], pair[24:])
    vec_out[...] = value
    send[each:] = jnp.concatenate(split_high(value), axis=0)


def end_kernel(scal, got, keep, vec, qkv_out, attn_out, vec_out):
    each = keep.shape[0]
    value = got[:each].astype(full) + keep[...].astype(full)
    qkv_out[...] = value[:, : 3 * each]
    attn_out[...] = value[:, 3 * each :]
    pair = got[each:]
    vec_out[...] = vec[...] + joined(pair[:24], pair[24:])


def half_kernel(scal, got, keep, send, left):
    bit = scal[1] // 2
    send[...] = added(got[1 - bit], keep[1 - bit])
    left[...] = added(got[bit], keep[bit])


def swapped(x, axis, by):
    return lax.ppermute(x, axis, [(i, i ^ by) for i in range(lax.axis_size(axis))])


def near(section, x, by):
    pairs = [
        (16 * section + 4 * i + j, 16 * section + 4 * (i ^ (by & 1)) + (j ^ (by >> 1)))
        for i in range(4)
        for j in range(4)
    ]
    return lax.ppermute(x, ("section", "dp", "ctx"), pairs)


def moved(x, target):
    pairs = [(16 * s + 4 * i + j, 16 * s + target(i, j)) for s in range(2) for i in range(4) for j in range(4)]
    return lax.ppermute(x, ("section", "dp", "ctx"), pairs)


def swapped_in(section, x, axis, by):
    length = lax.axis_size(axis)
    pairs = [(section * length + i, section * length + (i ^ by)) for i in range(length)]
    return lax.ppermute(x, ("section", axis), pairs)


def pick(x, at, dim=0):
    return lax.dynamic_index_in_dim(x, at, dim, False)


def added(one, two):
    return (one.astype(full) + two.astype(full)).astype(low)


def spread(row_half, ctx, swap):
    length = lax.axis_size("ctx")
    size, width = row_half.shape
    parts = row_half.reshape(length, size // length, width)
    out = jnp.zeros(parts.shape, parts.dtype)
    out = lax.dynamic_update_index_in_dim(out, pick(parts, ctx), ctx, 0)
    for k in range(1, length):
        out = lax.dynamic_update_index_in_dim(out, swap(pick(parts, ctx ^ k), "ctx", k), ctx ^ k, 0)
    return out


def to_section(x, section):
    return lax.ppermute(x, "section", [(1 - section, section)])


def following(body, n_operands, n_after, *refs):
    body(*refs[:n_operands], *refs[n_operands + n_after :])


def merged(body, scal, operands, outs, scratch=(), after=()):
    return kernel_call(
        partial(following, body, 1 + len(operands), len(after)),
        [("s", scal)] + [("c", member) for member in operands] + [("a", member) for member in after],
        [("c", shape, kind) for shape, kind in outs],
        list(scratch),
        16,
    )


def row_body(
    tokens,
    segment_ids,
    padding,
    dropped,
    qkv_weight,
    query_bias,
    value_bias,
    attn_weight,
    attn_bias,
    attn_gain,
    attn_shift,
    inner_weight,
    inner_bias,
    outer_weight,
    outer_bias,
    ffn_gain,
    ffn_shift,
    cotangent,
):
    width = tokens.shape[2]
    half, each = width // 2, width // 4
    count = tokens.shape[1]
    section, dp, ctx = (lax.axis_index(name) for name in ("section", "dp", "ctx"))
    weights = (qkv_weight[0], attn_weight[0], inner_weight[0], outer_weight[0])
    vecs = jnp.concatenate(
        [attn_bias, attn_gain, attn_shift, outer_bias, ffn_gain, ffn_shift, query_bias, value_bias]
    )
    qkv_bias = jnp.concatenate([query_bias, jnp.zeros_like(query_bias), value_bias], axis=1)
    qkv_scale = jnp.concatenate(
        [jnp.full((1, width), HEAD_DIM ** (-0.5), jnp.float32), jnp.ones((1, 2 * width), jnp.float32)], axis=1
    )
    small = (qkv_bias, qkv_scale, vecs, inner_bias)
    scal = jnp.stack([section, ctx, pick(dropped[0], ctx), dp]).astype(jnp.int32)

    ids = jnp.stack([segment_ids, jnp.where(padding == 1, segment_ids, -1)], axis=1).astype(low)
    ids = jnp.pad(ids, ((0, 0), (0, 14), (0, width - count)))
    sent = jnp.concatenate([tokens, ids], axis=1)
    far = {k: swapped_in(0, pick(sent, ctx ^ k), "ctx", k) for k in (2, 3, 1)}
    own_tokens = [pick(sent, ctx), far[1], far[2], far[3]]
    held = weights
    own_cot = [pick(cotangent, ctx)] + [swapped_in(1, pick(cotangent, ctx ^ k), "ctx", k) for k in range(1, 4)]

    kept = run_forward(0, scal, small, own_tokens, [], held, [], [])
    middle = lax.ppermute(kept[10], "section", [(0, 1)])
    firsts = [near(0, kept[9], k) for k in (3, 2, 1)]
    made = run_forward(1, scal, small, [middle], own_cot, held, kept, firsts)
    kept, top, both = made[:12], made[12:15], made[15]
    from_one = [near(1, both, k) for k in (3, 2, 1)]
    chain = run_chain(1, scal, vecs, top, kept, held, [], [])
    incoming = to_section(chain[3], 0)
    top = run_top(0, scal, vecs, incoming, kept[7], kept[8], top, [("c", member) for member in from_one])
    dffns = [near(0, top[1], k) for k in (3, 2, 1)]
    chain = run_chain(0, scal, vecs, top, kept, held, chain, [])
    dqkv, dbranch, chain_vec, d_input = chain
    result = kept[10][: 4 * count]

    send_a, keep_a, send_b, keep_b, vec = run_attn_grad(
        scal, top[2], chain_vec, kept[0], kept[2], dqkv, dbranch, []
    )
    got_a, got_b = swapped(send_a, "dp", 1), swapped(send_b, "dp", 2)
    ffn_send, ffn_keep = run_ffn_grad(
        scal, inner_bias, held[2], held[3], kept[9], top[1], from_one, firsts, dffns, [("h", keep_b)]
    )
    ffn_got = swapped(ffn_send, "dp", 2)
    wide, block, flat = (each, 2 * width), (each, width), ((24, width), full)
    send_a, keep_a, send_b, keep_b, vec = merged(
        merge_kernel,
        scal,
        (got_a, keep_a, got_b, keep_b, vec),
        [((each + VEC_ROWS, 2 * width), low), (wide, low), (wide, low), (wide, low), flat],
        after=[ffn_keep],
    )
    got_a, got_b = swapped(send_a, "dp", 2), swapped(send_b, "dp", 1)
    ffn_send, ffn_keep = merged(
        half_kernel, scal, (ffn_got, ffn_keep), [(ffn_keep.shape[1:], low)] * 2, after=[send_b]
    )
    ffn_got = swapped(ffn_send, "ctx", 2)
    rows = jnp.where(section == 0, d_input, result)
    rows, ffn_keep = lax.optimization_barrier((rows, ffn_keep))
    rows = spread(rows, ctx, swapped)
    send, keep, vec = merged(
        turn_kernel,
        scal,
        (got_a, keep_a, got_b, keep_b, vec),
        [((2 * each + 48, width), low), ((2, each, width), low), flat],
        [pltpu.VMEM((each, 4 * width), low), pltpu.VMEM((4, each, width), low)],
        after=[ffn_keep],
    )
    got = swapped(send, "ctx", 1)
    send, keep, vec = merged(last_kernel, scal, (got, keep, vec), [((each + 48, width), low), (block, low), flat])
    got = swapped(send, "ctx", 2)
    qkv_grad, attn_grad, vec = merged(
        end_kernel, scal, (got, keep, vec), [((each, 3 * each), full), ((each, each), full), flat]
    )
    ffn_rows = added(ffn_got, ffn_keep)
    inner_grad = moved(ffn_rows[:each], lambda i, j: 4 * (2 * (i // 2) + j // 2) + 2 * (i % 2) + j % 2).astype(full)
    outer_grad = moved(ffn_rows[each:], lambda i, j: 4 * (2 * (i % 2) + j % 2) + 2 * (j // 2) + i // 2).astype(full).T
    rows, vec = lax.optimization_barrier((rows, vec))
    other_half = swapped(jnp.where(section == 0, rows[..., half:], rows[..., :half]), "section", 1)
    tokens_grad = jnp.where(section == 0, rows[..., :half], other_half)
    encoded = jnp.where(section == 0, other_half, rows[..., half:])
    return (
        encoded,
        tokens_grad,
        qkv_grad[None],
        vec[8:9],
        vec[9:10],
        attn_grad[None],
        vec[10:11],
        vec[11:12],
        vec[12:13],
        inner_grad[None],
        vec[16 : 16 + inner_bias.shape[1] // width].reshape(1, -1),
        outer_grad[None],
        vec[0:1],
        vec[1:2],
        vec[2:3],
    )


def solution(mesh):
    placed = (
        P("dp", "ctx", None),
        P("dp", "ctx"),
        P("dp", "ctx"),
        P("section", "dp"),
        P("section", None, None),
        P("section", None),
        P("section", None),
        P("section", None, None),
        P("section", None),
        P("section", None),
        P("section", None),
        P("section", None, None),
        P("section", None),
        P("section", None, None),
        P("section", None),
        P("section", None),
        P("section", None),
        P("dp", "ctx", None),
    )

    def dispatch(*members):
        rows = members[0].shape[0]
        same = rows == lax.axis_size("ctx") == lax.axis_size("dp") == 4
        return (row_body if same else body)(*members)

    return jax.shard_map(
        dispatch,
        mesh=mesh,
        in_specs=placed,
        out_specs=(
            P("dp", "ctx", "section"),
            P("dp", "ctx", "section"),
            P("section", "dp", "ctx"),
            P("section", None),
            P("section", None),
            P("section", "dp", "ctx"),
            P("section", None),
            P("section", None),
            P("section", None),
            P("section", "dp", "ctx"),
            P("section", None),
            P("section", "dp", "ctx"),
            P("section", None),
            P("section", None),
            P("section", None),
        ),
        check_vma=False,
    )
```
